32 devices in a mesh: dp: 2 (over x), fsdp: 16 (over z, y, core).
Axes of the slice: x: 2, y: 2, z: 4, core: 2. Of those that a mesh axis runs over, the one named last changes fastest.
Arguments:
- tokens: bfloat16 [64, 256, 768], P(('dp', 'fsdp')), may hold values from -6 to 6
- lengths: int32 [64, 3], P(('dp', 'fsdp')), may hold values from 18 to 82, as said below
- keep_mask: int32 [64, 3, 2], P(('dp', 'fsdp')), may hold values 0 or 1
- cotangent: bfloat16 [64, 256, 768], P(('dp', 'fsdp')), may hold values from -6 to 6
- ln1_gain: bfloat16 [768], P('fsdp'), may hold values from 0.5 to 1.5
- ln1_bias: bfloat16 [768], P('fsdp'), may hold values from -3 to 3
- qkv_weight: bfloat16 [768, 2304], P('fsdp'), may hold values from -0.21875 to 0.21875
- q_bias: bfloat16 [768], P('fsdp'), may hold values from -4 to 4
- v_bias: bfloat16 [768], P('fsdp'), may hold values from -0.75 to 0.75
- proj_weight: bfloat16 [768, 768], P('fsdp'), may hold values from -1.25 to 1.25
- proj_bias: bfloat16 [768], P('fsdp'), may hold values from -3 to 3
- ln2_gain: bfloat16 [768], P('fsdp'), may hold values from 0.5 to 1.5
- ln2_bias: bfloat16 [768], P('fsdp'), may hold values from -3 to 3
- fc1_weight: bfloat16 [768, 3072], P('fsdp'), may hold values from -0.21875 to 0.21875
- fc1_bias: bfloat16 [3072], P('fsdp'), may hold values from -4 to 4
- fc2_weight: bfloat16 [3072, 768], P('fsdp'), may hold values from -0.109375 to 0.109375
- fc2_bias: bfloat16 [768], P('fsdp'), may hold values from -3 to 3
Outputs:
- output: bfloat16 [64, 256, 768], P(('dp', 'fsdp'))
- tokens_grad: float32 [64, 256, 768], P(('dp', 'fsdp'))
- ln1_gain_grad: float32 [768], P('fsdp')
- ln1_bias_grad: float32 [768], P('fsdp')
- qkv_weight_grad: float32 [768, 2304], P('fsdp')
- q_bias_grad: float32 [768], P('fsdp')
- v_bias_grad: float32 [768], P('fsdp')
- proj_weight_grad: float32 [768, 768], P('fsdp')
- proj_bias_grad: float32 [768], P('fsdp')
- ln2_gain_grad: float32 [768], P('fsdp')
- ln2_bias_grad: float32 [768], P('fsdp')
- fc1_weight_grad: float32 [768, 3072], P('fsdp')
- fc1_bias_grad: float32 [3072], P('fsdp')
- fc2_weight_grad: float32 [3072, 768], P('fsdp')
- fc2_bias_grad: float32 [768], P('fsdp')
The draws below stay inside these ranges and needn't reach their ends.
Inputs may be any that keep to these rules, and one draw needn't show every extreme that they name: `lengths`: the 3 images of a row fill its first tokens in order; the remaining tokens of the row are padding.
All inputs are finite; a program needn't handle non-finite values. No bound on the sum of `keep_mask` on one device may be relied on, other than what follows from the above.
Results may differ from the reference program's by a relative error of at most 0.014.
Values may be sent and summed in bfloat16 or wider, within the bound.
No kernel may reach another device: no remote copies, remote signals or barrier semaphores. Data moves between devices by JAX's collectives and lax.ppermute only.
A program may use at most 192 MiB of HBM per device.

```python
import math
import jax
import jax.numpy as jnp
from jax import lax

D = 768
FF = 3072
HEADS = 12
HEAD_DIM = 64
SEQ = 256
IMGS = 3
MIN_IMG = 18
MAX_IMG = 82
ROWS = 64


def draw_lengths(key, part):
    key = jax.random.fold_in(key, 11)
    key_values, key_slot, key_other = jax.random.split(key, 3)
    values = jax.random.randint(key_values, (ROWS, IMGS), MIN_IMG, MAX_IMG + 1, dtype=jnp.int32)
    slot_index = jax.random.randint(key_slot, (), 0, IMGS, dtype=jnp.int32)
    values = values.at[0, slot_index].set(MAX_IMG)
    other_row = jax.random.randint(key_other, (), 1, ROWS, dtype=jnp.int32)
    values = values.at[other_row, slot_index].set(MIN_IMG)
    return values


def place_ends(array, stream_key, low, high):
    index_at = [jax.random.randint(jax.random.fold_in(stream_key, axis), (), 0, length) for axis, length in enumerate(array.shape)]
    main_axis = array.shape.index(max(array.shape))
    neighbour = index_at[:main_axis] + [(index_at[main_axis] + 1) % array.shape[main_axis]] + index_at[main_axis + 1:]
    return array.at[tuple(index_at)].set(low).at[tuple(neighbour)].set(high)


def block_scale(rng, extent, cuts, smallest, top_value):
    loudness, own = 1.0, jax.random.fold_in(rng, 6)
    for axis_at, blocks in cuts:
        steps = jnp.exp(jax.random.uniform(jax.random.fold_in(own, axis_at), (blocks,), jnp.float32, smallest / len(cuts), top_value / len(cuts)))
        loudness = loudness * jnp.repeat(steps, extent[axis_at] // blocks).reshape([-1 if axis == axis_at else 1 for axis in range(len(extent))])
    return loudness


def bell_draw(key, shape, scale, most, cuts=(), kind=jnp.bfloat16):
    entries = jax.random.normal(key, shape, jnp.float32) * scale
    if len(cuts) > 0:
        entries = block_scale(key, shape, cuts, -0.22, 0.18) * entries
    return jnp.clip(entries, min=-most, max=most).astype(kind)


def setup_inputs(seed: int = 0) -> dict:
    arg_keys = jax.random.split(jax.random.key(seed), 18)
    tokens = bell_draw(arg_keys[0], (ROWS, SEQ, D), 1.0, 6.0, ((0, 32),))
    lengths = draw_lengths(jax.random.fold_in(arg_keys[17], 71), 0)
    keep_mask = place_ends((jax.random.randint(arg_keys[2], (ROWS, IMGS, 2), 0, 10) < 9).astype(jnp.int32), jax.random.fold_in(arg_keys[2], 1), 0, 1)
    cotangent = bell_draw(arg_keys[3], (ROWS, SEQ, D), 1.0, 6.0, ((0, 32),))
    ln1_gain = jnp.clip(1.0 + 0.1 * jax.random.normal(arg_keys[4], (D,), jnp.float32), 0.5, 1.5).astype(jnp.bfloat16)
    ln1_bias = bell_draw(arg_keys[5], (D,), 0.2, 3.0, ((0, 16),))
    qkv_weight = bell_draw(arg_keys[6], (D, 3 * D), D ** -0.5, 0.21875, ((0, 16),))
    q_bias = bell_draw(arg_keys[7], (D,), 0.3, 4.0, ((0, 16),))
    v_bias = bell_draw(arg_keys[8], (D,), 0.05, 0.75, ((0, 16),))
    proj_weight = bell_draw(arg_keys[9], (D, D), (D // 32) ** -0.5, 1.25, ((0, 16),))
    proj_bias = bell_draw(arg_keys[10], (D,), 0.2, 3.0, ((0, 16),))
    ln2_gain = jnp.clip(1.0 + 0.1 * jax.random.normal(arg_keys[11], (D,), jnp.float32), 0.5, 1.5).astype(jnp.bfloat16)
    ln2_bias = bell_draw(arg_keys[12], (D,), 0.2, 3.0, ((0, 16),))
    fc1_weight = bell_draw(arg_keys[13], (D, FF), D ** -0.5, 0.21875, ((0, 16),))
    fc1_bias = bell_draw(arg_keys[14], (FF,), 0.3, 4.0, ((0, 16),))
    fc2_weight = bell_draw(arg_keys[15], (FF, D), FF ** -0.5, 0.109375, ((0, 16),))
    fc2_bias = bell_draw(arg_keys[16], (D,), 0.2, 3.0, ((0, 16),))
    return dict(tokens=tokens, lengths=lengths, keep_mask=keep_mask, cotangent=cotangent, ln1_gain=ln1_gain, ln1_bias=ln1_bias, qkv_weight=qkv_weight, q_bias=q_bias, v_bias=v_bias, proj_weight=proj_weight, proj_bias=proj_bias, ln2_gain=ln2_gain, ln2_bias=ln2_bias, fc1_weight=fc1_weight, fc1_bias=fc1_bias, fc2_weight=fc2_weight, fc2_bias=fc2_bias)


EPSILON = 1e-06
KEEP_RATE = 0.9
NEGATIVE = -1e+30
HIGHEST = lax.Precision.HIGHEST

@jax.custom_vjp
def low(v):
    return lax.optimization_barrier(v.astype(jnp.bfloat16)).astype(jnp.float32)

@jax.custom_vjp
def low_back(v):
    return v

def low_keep(v):
    return (low(v), None)

def low_pass(kept, grad):
    return (grad,)

def back_keep(v):
    return (v, None)

def back_low(kept, grad):
    return (low(grad),)
low.defvjp(low_keep, low_pass)
low_back.defvjp(back_keep, back_low)

def product(left, right):
    return jnp.dot(left, right, precision=HIGHEST)

def normalize(values, gain, shift):
    center = values - lax.optimization_barrier(jnp.mean(values, axis=-1, keepdims=True))
    spread = lax.optimization_barrier(jnp.mean(center * center, axis=-1, keepdims=True))
    return center * lax.rsqrt(spread + EPSILON) * gain + shift

def layout(lengths, keep_mask):
    image_ends = jnp.cumsum(lengths, axis=-1, dtype=jnp.int32)
    position = jnp.arange(SEQ, dtype=jnp.int32)
    segment = lax.optimization_barrier(jnp.sum((position[None, :, None] >= image_ends[:, None, :]).astype(jnp.int32), axis=-1, dtype=jnp.int32))
    images = jnp.arange(IMGS, dtype=jnp.int32)
    member = (segment[:, :, None] == images[None, None, :]).astype(jnp.float32)
    keeping = keep_mask.astype(jnp.float32)
    scales = lax.optimization_barrier(jnp.sum(member[:, :, :, None] * keeping[:, None, :, :], axis=2)) / KEEP_RATE
    inside = lax.optimization_barrier(jnp.sum(member, axis=-1))
    return (segment, scales, inside)

def forward(block_input, segment, scales, inside, weights):
    ln1_gain, ln1_bias, qkv_weight, q_bias, v_bias, proj_weight, proj_bias, ln2_gain, ln2_bias, fc1_weight, fc1_bias, fc2_weight, fc2_bias = weights
    rowset, length, features = block_input.shape
    flattened = block_input.reshape(rowset * length, features)
    normed_one = low(normalize(flattened, ln1_gain, ln1_bias))
    bias_all = jnp.concatenate([q_bias, jnp.zeros_like(q_bias), v_bias])
    packed = low(low_back(product(normed_one, qkv_weight) + bias_all))
    packed = packed.reshape(rowset, length, 3, HEADS, HEAD_DIM)
    queries = packed[:, :, 0]
    keys_all = packed[:, :, 1]
    values_all = packed[:, :, 2]
    key_scale = HEAD_DIM ** (-0.5)
    scores = low_back(jnp.einsum('rqhd,rkhd->rhqk', queries, keys_all, precision=HIGHEST) * key_scale)
    matching = segment[:, :, None] == segment[:, None, :]
    scores = jnp.where(matching[:, None], scores, NEGATIVE)
    raised = jnp.exp(scores - lax.optimization_barrier(jnp.max(scores, axis=-1, keepdims=True)))
    weighting = low(raised / lax.optimization_barrier(jnp.sum(raised, axis=-1, keepdims=True)))
    attended = jnp.einsum('rhqk,rkhd->rqhd', weighting, values_all, precision=HIGHEST)
    attended = low(low_back(attended.reshape(rowset * length, features)))
    branch_one = low_back(product(attended, proj_weight) + proj_bias)
    middle = flattened + scales[:, :, 0].reshape(-1, 1) * branch_one
    normed_two = low(normalize(middle, ln2_gain, ln2_bias))
    hidden = low_back(product(normed_two, fc1_weight) + fc1_bias)
    active = low(jax.nn.gelu(hidden, approximate=False))
    branch_two = low_back(product(active, fc2_weight) + fc2_bias)
    result = (middle + scales[:, :, 1].reshape(-1, 1) * branch_two) * inside.reshape(-1, 1)
    return result.reshape(rowset, length, features)

def reference(tokens, lengths, keep_mask, cotangent, ln1_gain, ln1_bias, qkv_weight, q_bias, v_bias, proj_weight, proj_bias, ln2_gain, ln2_bias, fc1_weight, fc1_bias, fc2_weight, fc2_bias):
    weights = tuple((element.astype(jnp.float32) for element in (ln1_gain, ln1_bias, qkv_weight, q_bias, v_bias, proj_weight, proj_bias, ln2_gain, ln2_bias, fc1_weight, fc1_bias, fc2_weight, fc2_bias)))
    segment, scales, inside = layout(lengths, keep_mask)
    group_rows = math.gcd(ROWS, 16)
    group_count = ROWS // group_rows

    def grouped(source_array):
        return source_array.reshape((group_count, group_rows) + source_array.shape[1:])

    def one_group(totals, group_items):
        group_input, group_cot, group_segment, group_scales, group_inside = group_items

        def apply_block(block_input, params):
            return forward(block_input, group_segment, group_scales, group_inside, params)
        result, pullback = jax.vjp(jax.checkpoint(apply_block), group_input.astype(jnp.float32), weights)
        input_grad, weight_grads = pullback(group_cot.astype(jnp.float32))
        totals = jax.tree.map(jnp.add, totals, weight_grads)
        return (totals, (result.astype(jnp.bfloat16), input_grad))
    zero_grads = tuple((jnp.zeros_like(element) for element in weights))
    totals, (outputs, input_grads) = lax.scan(one_group, zero_grads, (grouped(tokens), grouped(cotangent), grouped(segment), grouped(scales), grouped(inside)))
    return (outputs.reshape(ROWS, SEQ, D), input_grads.reshape(ROWS, SEQ, D), totals[0], totals[1], totals[2], totals[3], totals[4], totals[5], totals[6], totals[7], totals[8], totals[9], totals[10], totals[11], totals[12])
```

```python
import jax
import jax.numpy as jnp
from jax import lax
from jax.experimental import pallas as pl
from jax.experimental.pallas import tpu as pltpu
from jax.sharding import PartitionSpec as P

HEADS = 12


EPSILON = 1e-06
KEEP_RATE = 0.9
NEGATIVE = -1e30


def normalize(values, gain, shift):
    center = values - jnp.mean(values, axis=-1, keepdims=True)
    spread = jnp.mean(center * center, axis=-1, keepdims=True)
    return center * lax.rsqrt(spread + EPSILON) * gain + shift


def standardize(values):
    center = values - jnp.mean(values, axis=-1, keepdims=True)
    spread = jnp.mean(center * center, axis=-1, keepdims=True)
    return center * lax.rsqrt(spread + EPSILON)


def affine_low(unit_values, gain, shift):
    return (unit_values * gain.astype(jnp.float32) + shift.astype(jnp.float32)).astype(jnp.bfloat16)


def exact_gelu(values):
    return jax.nn.gelu(values, approximate=False)


def norm_back(values, gain, shift, incoming):
    _, pullback = jax.vjp(normalize, values, gain, shift)
    return pullback(incoming)


def inner_rows(left, right):
    return lax.dot_general(
        left, right, (((0,), (0,)), ((), ())), preferred_element_type=jnp.float32
    )


def times_transpose(left, right):
    return lax.dot_general(
        left, right, (((1,), (1,)), ((), ())), preferred_element_type=jnp.float32
    )


def layout(lengths, keep_mask, length):
    image_ends = jnp.cumsum(lengths, axis=-1, dtype=jnp.int32)
    position = jnp.arange(length, dtype=jnp.int32)
    segment = jnp.sum(
        (position[None, :, None] >= image_ends[:, None, :]).astype(jnp.int32),
        axis=-1,
        dtype=jnp.int32,
    )
    images = jnp.arange(lengths.shape[1], dtype=jnp.int32)
    member = (segment[:, :, None] == images[None, None, :]).astype(jnp.float32)
    keeping = keep_mask.astype(jnp.float32)
    scales = jnp.sum(member[:, :, :, None] * keeping[:, None, :, :], axis=2) / KEEP_RATE
    inside = jnp.sum(member, axis=-1)
    return (segment, scales, inside)


def attention_forward(packed, segment, rowset, length, head_size):
    split_view = packed.reshape(rowset, length, 3, HEADS, head_size)
    queries = split_view[:, :, 0]
    keys_all = split_view[:, :, 1]
    values_all = split_view[:, :, 2]
    scores = jnp.einsum(
        "rqhd,rkhd->rhqk", queries, keys_all, preferred_element_type=jnp.float32
    ) * head_size ** (-0.5)
    matching = segment[:, :, None] == segment[:, None, :]
    scores = jnp.where(matching[:, None], scores, NEGATIVE)
    raised = jnp.exp(scores - jnp.max(scores, axis=-1, keepdims=True))
    weighting = raised / jnp.sum(raised, axis=-1, keepdims=True)
    weighting_low = weighting.astype(jnp.bfloat16)
    attended = jnp.einsum(
        "rhqk,rkhd->rqhd", weighting_low, values_all, preferred_element_type=jnp.float32
    )
    attended = attended.reshape(rowset * length, HEADS * head_size).astype(jnp.bfloat16)
    return (queries, keys_all, values_all, weighting, weighting_low, attended)


def per_device(
    tokens,
    lengths,
    keep_mask,
    cotangent,
    ln1_gain,
    ln1_bias,
    qkv_weight,
    q_bias,
    v_bias,
    proj_weight,
    proj_bias,
    ln2_gain,
    ln2_bias,
    fc1_weight,
    fc1_bias,
    fc2_weight,
    fc2_bias,
):
    rowset, length, features = tokens.shape
    head_size = features // HEADS
    token_count = rowset * length
    segment, scales, inside = layout(lengths, keep_mask, length)
    scale_one = scales[:, :, 0].reshape(token_count, 1)
    scale_two = scales[:, :, 1].reshape(token_count, 1)
    inside_column = inside.reshape(token_count, 1)
    flattened = tokens.reshape(token_count, features).astype(jnp.float32)
    unit_one = standardize(flattened)
    qkv_full, proj_full, gain_one, shift_one, query_bias, value_bias, out_bias = (
        lax.all_gather(qkv_weight, "fsdp", axis=0, tiled=True),
        lax.all_gather(proj_weight, "fsdp", axis=0, tiled=True),
        lax.all_gather(ln1_gain, "fsdp", axis=0, tiled=True),
        lax.all_gather(ln1_bias, "fsdp", axis=0, tiled=True),
        lax.all_gather(q_bias, "fsdp", axis=0, tiled=True),
        lax.all_gather(v_bias, "fsdp", axis=0, tiled=True),
        lax.all_gather(proj_bias, "fsdp", axis=0, tiled=True),
    )
    normed_one = affine_low(unit_one, gain_one, shift_one)
    bias_all = jnp.concatenate(
        [
            query_bias.astype(jnp.float32),
            jnp.zeros((features,), jnp.float32),
            value_bias.astype(jnp.float32),
        ]
    )
    packed = (jnp.dot(normed_one, qkv_full, preferred_element_type=jnp.float32) + bias_all).astype(
        jnp.bfloat16
    )
    _, _, _, _, _, attended = attention_forward(packed, segment, rowset, length, head_size)
    branch_one = jnp.dot(attended, proj_full, preferred_element_type=jnp.float32) + out_bias.astype(
        jnp.float32
    )
    middle = flattened + scale_one * branch_one
    unit_two = standardize(middle)
    up_full, down_full, gain_two, shift_two, up_bias, down_bias = (
        lax.all_gather(fc1_weight, "fsdp", axis=0, tiled=True),
        lax.all_gather(fc2_weight, "fsdp", axis=0, tiled=True),
        lax.all_gather(ln2_gain, "fsdp", axis=0, tiled=True),
        lax.all_gather(ln2_bias, "fsdp", axis=0, tiled=True),
        lax.all_gather(fc1_bias, "fsdp", axis=0, tiled=True),
        lax.all_gather(fc2_bias, "fsdp", axis=0, tiled=True),
    )
    normed_two = affine_low(unit_two, gain_two, shift_two)
    hidden = jnp.dot(normed_two, up_full, preferred_element_type=jnp.float32) + up_bias.astype(
        jnp.float32
    )
    active = exact_gelu(hidden).astype(jnp.bfloat16)
    branch_two = jnp.dot(active, down_full, preferred_element_type=jnp.float32) + down_bias.astype(
        jnp.float32
    )
    output = (
        ((middle + scale_two * branch_two) * inside_column)
        .astype(jnp.bfloat16)
        .reshape(rowset, length, features)
    )
    up_full, down_full = (
        lax.all_gather(fc1_weight, "fsdp", axis=0, tiled=True),
        lax.all_gather(fc2_weight, "fsdp", axis=0, tiled=True),
    )
    gain_two_f = gain_two.astype(jnp.float32)
    shift_two_f = shift_two.astype(jnp.float32)
    grad_out = cotangent.reshape(token_count, features).astype(jnp.float32) * inside_column
    grad_two_low = (grad_out * scale_two).astype(jnp.bfloat16)
    fc2_grad = inner_rows(active, grad_two_low)
    fc2_bias_part = jnp.sum(grad_two_low.astype(jnp.float32), axis=0)
    grad_active = times_transpose(grad_two_low, down_full)
    _, gelu_pull = jax.vjp(exact_gelu, hidden)
    grad_hidden_low = gelu_pull(grad_active)[0].astype(jnp.bfloat16)
    fc1_grad = inner_rows(normed_two, grad_hidden_low)
    fc1_bias_part = jnp.sum(grad_hidden_low.astype(jnp.float32), axis=0)
    grad_normed_two = times_transpose(grad_hidden_low, up_full)
    grad_middle_norm, gain_two_part, shift_two_part = norm_back(
        middle, gain_two_f, shift_two_f, grad_normed_two
    )
    grad_middle = grad_out + grad_middle_norm
    qkv_full, proj_full = (
        lax.all_gather(qkv_weight, "fsdp", axis=0, tiled=True),
        lax.all_gather(proj_weight, "fsdp", axis=0, tiled=True),
    )
    gain_one_f = gain_one.astype(jnp.float32)
    shift_one_f = shift_one.astype(jnp.float32)
    queries, keys_all, values_all, weighting, weighting_low, attended = attention_forward(
        packed, segment, rowset, length, head_size
    )
    grad_one_low = (grad_middle * scale_one).astype(jnp.bfloat16)
    proj_grad = inner_rows(attended, grad_one_low)
    proj_bias_part = jnp.sum(grad_one_low.astype(jnp.float32), axis=0)
    grad_attended_low = times_transpose(grad_one_low, proj_full).astype(jnp.bfloat16)
    grad_attended_low = grad_attended_low.reshape(rowset, length, HEADS, head_size)
    grad_weighting = jnp.einsum(
        "rqhd,rkhd->rhqk", grad_attended_low, values_all, preferred_element_type=jnp.float32
    )
    value_grad = jnp.einsum(
        "rhqk,rqhd->rkhd", weighting_low, grad_attended_low, preferred_element_type=jnp.float32
    )
    row_inner = jnp.sum(grad_weighting * weighting, axis=-1, keepdims=True)
    grad_scores_low = (weighting * (grad_weighting - row_inner)).astype(jnp.bfloat16)
    key_scale = head_size ** (-0.5)
    query_grad = (
        jnp.einsum("rhqk,rkhd->rqhd", grad_scores_low, keys_all, preferred_element_type=jnp.float32)
        * key_scale
    )
    key_grad = (
        jnp.einsum("rhqk,rqhd->rkhd", grad_scores_low, queries, preferred_element_type=jnp.float32)
        * key_scale
    )
    grad_packed_low = (
        jnp.stack([query_grad, key_grad, value_grad], axis=2)
        .reshape(token_count, 3 * features)
        .astype(jnp.bfloat16)
    )
    qkv_grad = inner_rows(normed_one, grad_packed_low)
    column_sums = jnp.sum(grad_packed_low.astype(jnp.float32), axis=0)
    query_bias_part = column_sums[:features]
    value_bias_part = column_sums[2 * features :]
    grad_normed_one = times_transpose(grad_packed_low, qkv_full)
    grad_input_norm, gain_one_part, shift_one_part = norm_back(
        flattened, gain_one_f, shift_one_f, grad_normed_one
    )
    tokens_grad = (grad_middle + grad_input_norm).reshape(rowset, length, features)
    (
        gain_two_grad,
        shift_two_grad,
        fc1_weight_part,
        fc1_bias_shard,
        fc2_weight_part,
        fc2_bias_shard,
    ) = (
        lax.psum_scatter(gain_two_part, "fsdp", scatter_dimension=0, tiled=True),
        lax.psum_scatter(shift_two_part, "fsdp", scatter_dimension=0, tiled=True),
        lax.psum_scatter(fc1_grad, "fsdp", scatter_dimension=0, tiled=True),
        lax.psum_scatter(fc1_bias_part, "fsdp", scatter_dimension=0, tiled=True),
        lax.psum_scatter(fc2_grad, "fsdp", scatter_dimension=0, tiled=True),
        lax.psum_scatter(fc2_bias_part, "fsdp", scatter_dimension=0, tiled=True),
    )
    (
        gain_one_grad,
        shift_one_grad,
        qkv_weight_part,
        query_bias_shard,
        value_bias_shard,
        proj_weight_part,
        proj_bias_shard,
    ) = (
        lax.psum_scatter(gain_one_part, "fsdp", scatter_dimension=0, tiled=True),
        lax.psum_scatter(shift_one_part, "fsdp", scatter_dimension=0, tiled=True),
        lax.psum_scatter(qkv_grad, "fsdp", scatter_dimension=0, tiled=True),
        lax.psum_scatter(query_bias_part, "fsdp", scatter_dimension=0, tiled=True),
        lax.psum_scatter(value_bias_part, "fsdp", scatter_dimension=0, tiled=True),
        lax.psum_scatter(proj_grad, "fsdp", scatter_dimension=0, tiled=True),
        lax.psum_scatter(proj_bias_part, "fsdp", scatter_dimension=0, tiled=True),
    )
    summed = (
        lax.psum(gain_one_grad.astype(jnp.bfloat16), "dp").astype(jnp.float32),
        lax.psum(shift_one_grad.astype(jnp.bfloat16), "dp").astype(jnp.float32),
        lax.psum(qkv_weight_part.astype(jnp.bfloat16), "dp").astype(jnp.float32),
        lax.psum(query_bias_shard.astype(jnp.bfloat16), "dp").astype(jnp.float32),
        lax.psum(value_bias_shard.astype(jnp.bfloat16), "dp").astype(jnp.float32),
        lax.psum(proj_weight_part.astype(jnp.bfloat16), "dp").astype(jnp.float32),
        lax.psum(proj_bias_shard.astype(jnp.bfloat16), "dp").astype(jnp.float32),
        lax.psum(gain_two_grad.astype(jnp.bfloat16), "dp").astype(jnp.float32),
        lax.psum(shift_two_grad.astype(jnp.bfloat16), "dp").astype(jnp.float32),
        lax.psum(fc1_weight_part.astype(jnp.bfloat16), "dp").astype(jnp.float32),
        lax.psum(fc1_bias_shard.astype(jnp.bfloat16), "dp").astype(jnp.float32),
        lax.psum(fc2_weight_part.astype(jnp.bfloat16), "dp").astype(jnp.float32),
        lax.psum(fc2_bias_shard.astype(jnp.bfloat16), "dp").astype(jnp.float32),
    )
    return (
        output,
        tokens_grad,
        summed[0],
        summed[1],
        summed[2],
        summed[3],
        summed[4],
        summed[5],
        summed[6],
        summed[7],
        summed[8],
        summed[9],
        summed[10],
        summed[11],
        summed[12],
    )


BIT_Z1, BIT_Z0, BIT_Y, BIT_C = 8, 4, 2, 1
PIECE = 48
WIDE = 768
SCALE_ON = 1.0 / 0.9
VMEM_BYTES = 56 * 1024 * 1024
f32 = jnp.float32
bf16 = jnp.bfloat16


def hop(array, bit):
    return lax.ppermute(array, "fsdp", [(i, i ^ bit) for i in range(16)])


def swap(array):
    return lax.ppermute(array, "dp", [(0, 1), (1, 0)])


def join(*arrays):
    return jnp.concatenate(arrays, axis=0)


def gather_group(halves, x):
    mine = jnp.where(x == 0, halves[0], halves[1])
    pair = jnp.stack([mine, hop(mine, BIT_Z1)], axis=1)
    far = hop(pair, BIT_Z0)
    line0 = join(pair[0], far[0])
    line1 = join(pair[1], far[1])
    wide0 = join(line0, hop(line0, BIT_Y))
    wide1 = join(line1, swap(line1))
    own = (wide0, swap(wide0), wide1, hop(wide1, BIT_Y))
    other = tuple(hop(part, BIT_C) for part in own)
    return own + other


def plus(left, right):
    return (left.astype(f32) + right.astype(f32)).astype(bf16)


def scatter_group(own, away):
    came = hop(away, BIT_C)
    keep0, send0, keep1, send1 = [plus(own[a], came[a]) for a in range(4)]
    got0 = swap(send0)
    got1 = hop(send1, BIT_Y)
    keep0, send0 = plus(keep0[:4], got0[:4]), plus(keep0[4:], got0[4:])
    keep1, send1 = plus(keep1[:4], got1[:4]), plus(keep1[4:], got1[4:])
    got0 = hop(send0, BIT_Y)
    got1 = swap(send1)
    keep = jnp.stack([plus(keep0[:2], got0[:2]), plus(keep1[:2], got1[:2])])
    send = jnp.stack([plus(keep0[2:], got0[2:]), plus(keep1[2:], got1[2:])])
    got = hop(send, BIT_Z0)
    keep, send = plus(keep[:, 0], got[:, 0]), plus(keep[:, 1], got[:, 1])
    mine = plus(keep, hop(send, BIT_Z1))
    return mine, swap(mine)


def place(mine, other, x, half, line):
    return jnp.where(x == half, mine[line], other[line]).astype(f32)


def product(left, right, dims):
    return lax.dot_general(left, right, (dims, ((), ())), preferred_element_type=f32)


NN = ((1,), (0,))
NT = ((1,), (1,))
TN = ((0,), (0,))


def slot(line, xr, yr):
    return (xr, yr) if line == 0 else (2 + yr, xr)


def load_chunk(store, refs, i, line, xr):
    for m in range(16):
        c, yr, z0r, z1r = m & 1, (m >> 1) & 1, (m >> 2) & 1, (m >> 3) & 1
        array, part = slot(line, xr, yr) if isinstance(xr, int) else (2 + yr, xr)
        row = pl.multiple_of((i ^ m) * PIECE, 16)
        store[pl.ds(row, PIECE), :] = refs[4 * c + array][part * 4 + z0r * 2 + z1r]


def save_chunk(value, outs, i, line, xr):
    for m in range(16):
        c, yr, z0r, z1r = m & 1, (m >> 1) & 1, (m >> 2) & 1, (m >> 3) & 1
        array, part = slot(line, xr, yr) if isinstance(xr, int) else (2 + yr, xr)
        row = pl.multiple_of((i ^ m) * PIECE, 16)
        outs[c][array, part * 4 + z0r * 2 + z1r] = value[pl.ds(row, PIECE), :]


def row_facts(info, r):
    first = info[2 + 3 * r]
    second = first + info[3 + 3 * r]
    third = second + info[4 + 3 * r]

    def segment(shape, axis):
        t = lax.broadcasted_iota(jnp.int32, shape, axis)
        return (t >= first).astype(jnp.int32) + (t >= second).astype(jnp.int32) + (t >= third).astype(jnp.int32)

    column = segment((256, 1), 0)

    def scale(branch):
        keeps = [info[8 + 6 * r + 2 * j + branch].astype(f32) * SCALE_ON for j in range(3)]
        return jnp.where(
            column == 0, keeps[0], jnp.where(column == 1, keeps[1], jnp.where(column == 2, keeps[2], 0.0))
        )

    inside = jnp.where(column < 3, 1.0, 0.0).astype(f32)
    return column, segment((1, 256), 1), scale, inside


def unit_of(values):
    center = values - jnp.mean(values, axis=-1, keepdims=True)
    spread = jnp.mean(center * center, axis=-1, keepdims=True)
    root = lax.rsqrt(spread + EPSILON)
    return center * root, root


def unit_back(unit, root, gain, incoming):
    eg = incoming * gain
    return root * (
        eg - jnp.mean(eg, axis=-1, keepdims=True) - unit * jnp.mean(eg * unit, axis=-1, keepdims=True)
    )


def sums(values):
    return jnp.sum(values, axis=0, keepdims=True)


def qkv_kernel(info, tok, small, *rest):
    refs, (packed, normed, weight) = rest[:8], rest[8:]
    i, x = info[0], info[1]
    for line in range(2):
        for xr in range(2):
            load_chunk(weight.at[line, x ^ xr], refs, i, line, xr)
    for r in range(2):
        rows = slice(256 * r, 256 * r + 256)
        unit, _ = unit_of(tok[rows, :].astype(f32))
        normed[rows, :] = (unit * small[0:1, :] + small[1:2, :]).astype(bf16)
    for r in range(2):
        rows = slice(256 * r, 256 * r + 256)
        low = normed[rows, :]
        packed[rows, 0:768] = (product(low, weight[1, 0], NN) + small[2:3, :]).astype(bf16)
        packed[rows, 768:1536] = product(low, weight[0, 0], NN).astype(bf16)
        packed[rows, 1536:2304] = (product(low, weight[0, 1], NN) + small[3:4, :]).astype(bf16)


def attend_kernel(info, packed, tok, cot, small, *rest):
    refs, (attended, middle, normed, grad_two, lse, weight) = rest[:8], rest[8:]
    i, x, r = info[0], info[1], pl.program_id(0)

    @pl.when(r == 0)
    def _():
        load_chunk(weight, refs, i, 1, x ^ 1)

    column, across, scale, inside = row_facts(info, r)
    same = column == across
    lane = lax.broadcasted_iota(jnp.int32, (256, 128), 1)
    kept = jnp.zeros((256, 128), f32)
    for h in range(0, HEADS, 2):
        pair = []
        for g in (h, h + 1):
            query = packed[:, 64 * g : 64 * g + 64] * 0.125
            scores = product(query, packed[:, 768 + 64 * g : 832 + 64 * g], NT)
            scores = jnp.where(same, scores, NEGATIVE)
            top = jnp.max(scores, axis=-1, keepdims=True)
            raised = jnp.exp(scores - top)
            total = jnp.sum(raised, axis=-1, keepdims=True)
            low = (raised / total).astype(bf16)
            pair.append(product(low, packed[:, 1536 + 64 * g : 1600 + 64 * g], NN).astype(bf16))
            kept = jnp.where(lane == g, top + jnp.log(total), kept)
        attended[:, 64 * h : 64 * h + 128] = jnp.concatenate(pair, axis=1)
    lse[...] = kept
    branch = product(attended[...], weight[...], NN) + small[4:5, :]
    after = tok[...].astype(f32) + scale(0) * branch
    middle[...] = after
    unit, _ = unit_of(after)
    normed[...] = (unit * small[5:6, :] + small[6:7, :]).astype(bf16)
    grad_two[...] = (cot[...].astype(f32) * inside * scale(1)).astype(bf16)


def up_kernel(info, normed, grad_two, small, *rest):
    refs, (hidden, active, own, away, weight, grad) = rest[:8], rest[8:]
    i, x, t = info[0], info[1], pl.program_id(0)
    block = ((t & 1) ^ x) * 2 + (t >> 1)
    for step in range(4):

        @pl.when(t == step)
        def _():
            load_chunk(weight, refs, i, step >> 1, step & 1)

    value = product(normed[...], weight[...], NN) + small[pl.ds(8 + block, 1), :]
    hidden[0] = value
    low = (0.5 * value * (1.0 + lax.erf(value * (0.5**0.5)))).astype(bf16)
    active[0] = low
    grad[...] = product(low, grad_two[...], TN).astype(bf16)
    far = block ^ (i >> 2)
    spot = (far & 1) * 2 + (far >> 1)
    for line in range(2):
        for xr in range(2):
            for near in range(4):
                c, yr = near & 1, near >> 1
                array, part = slot(line, xr, yr)
                row = ((i & 3) ^ near) * 192 + ((xr ^ x) * 2 + line) * PIECE
                (own, away)[c][array, part * 4 + spot] = grad[pl.ds(pl.multiple_of(row, 16), PIECE), :]


def down_kernel(info, normed, grad_two, hidden, active, middle, cot, small, *rest):
    refs1, refs2, outs = rest[:8], rest[8:16], rest[16:]
    result, grad_middle, grad_one, bias, own, away, weight1, weight2, branch, grad_normed, grad = outs
    i, x, t = info[0], info[1], pl.program_id(0)
    block = ((t & 1) ^ x) * 2 + (t >> 1)
    for step in range(4):

        @pl.when(t == step)
        def _():
            load_chunk(weight1, refs1, i, step >> 1, step & 1)

    far = block ^ (i >> 2)
    spot = (far & 1) * 2 + (far >> 1)
    for line in range(2):
        for xr in range(2):
            for near in range(4):
                c, yr = near & 1, near >> 1
                array, part = slot(line, xr, yr)
                row = ((i & 3) ^ near) * 192 + ((xr ^ x) * 2 + line) * PIECE
                weight2[pl.ds(pl.multiple_of(row, 16), PIECE), :] = refs2[4 * c + array][part * 4 + spot]

    @pl.when(t == 0)
    def _():
        branch[...] = jnp.zeros_like(branch)
        grad_normed[...] = jnp.zeros_like(grad_normed)
        bias[...] = jnp.zeros_like(bias)
        bias[7:8, :] = sums(grad_two[...].astype(f32))

    branch[...] += product(active[0], weight2[...], NN)
    value = hidden[0]
    slope = 0.5 * (1.0 + lax.erf(value * (0.5**0.5))) + value * (
        jnp.exp(-0.5 * value * value) * 0.3989422804014327
    )
    low = (product(grad_two[...], weight2[...], NT) * slope).astype(bf16)
    bias[pl.ds(8 + block, 1), :] = sums(low.astype(f32))
    grad_normed[...] += product(low, weight1[...], NT)
    grad[...] = product(normed[...], low, TN).astype(bf16)
    for step in range(4):

        @pl.when(t == step)
        def _():
            save_chunk(grad, (own, away), i, step >> 1, step & 1)

    @pl.when(t == 3)
    def _():
        for r in range(2):
            rows = slice(256 * r, 256 * r + 256)
            _, _, scale, inside = row_facts(info, r)
            after = middle[rows, :]
            result[rows, :] = (
                (after + scale(1) * (branch[rows, :] + small[7:8, :])) * inside
            ).astype(bf16)
            unit, root = unit_of(after)
            incoming = grad_normed[rows, :]
            bias[5:6, :] += sums(incoming * unit)
            bias[6:7, :] += sums(incoming)
            total = cot[rows, :].astype(f32) * inside + unit_back(unit, root, small[5:6, :], incoming)
            grad_middle[rows, :] = total
            low_one = (total * scale(0)).astype(bf16)
            grad_one[rows, :] = low_one
            bias[4:5, :] += sums(low_one.astype(f32))


def attend_back_kernel(info, packed, lse, attended, grad_one, *rest):
    refs, (grad_packed, proj_grad, weight, total) = rest[:8], rest[8:]
    i, x, r = info[0], info[1], pl.program_id(0)

    @pl.when(r == 0)
    def _():
        load_chunk(weight, refs, i, 1, x ^ 1)
        total[...] = jnp.zeros_like(total)

    column, across, _, _ = row_facts(info, r)
    same = column == across
    total[...] += product(attended[...], grad_one[...], TN)

    @pl.when(r == 1)
    def _():
        proj_grad[...] = total[...].astype(bf16)

    grad_attended = product(grad_one[...], weight[...], NT).astype(bf16)
    for h in range(0, HEADS, 2):
        pairs = ([], [], [])
        for g in (h, h + 1):
            query = packed[:, 64 * g : 64 * g + 64] * 0.125
            key = packed[:, 768 + 64 * g : 832 + 64 * g]
            value = packed[:, 1536 + 64 * g : 1600 + 64 * g]
            back = grad_attended[:, 64 * g : 64 * g + 64]
            scores = product(query, key, NT)
            weighting = jnp.where(same, jnp.exp(scores - lse[:, g : g + 1]), 0.0)
            grad_weighting = product(back, value, NT)
            pairs[2].append(product(weighting.astype(bf16), back, TN))
            inner = jnp.sum(grad_weighting * weighting, axis=-1, keepdims=True)
            low = (weighting * (grad_weighting - inner)).astype(bf16)
            pairs[0].append(product(low, key, NN) * 0.125)
            pairs[1].append(product(low, query, TN))
        for k in range(3):
            grad_packed[:, 768 * k + 64 * h : 768 * k + 64 * h + 128] = jnp.concatenate(
                pairs[k], axis=1
            ).astype(bf16)


def qkv_back_kernel(info, tok, normed, grad_packed, grad_middle, proj_grad, bias_in, small, *rest):
    refs, (tokens_grad, bias, own, away, weight, grad) = rest[:8], rest[8:]
    i, x = info[0], info[1]
    for line in range(2):
        for xr in range(2):
            load_chunk(weight.at[line, x ^ xr], refs, i, line, xr)
    bias[...] = bias_in[...]
    bias[2:3, :] = sums(grad_packed[:, 0:768].astype(f32))
    bias[3:4, :] = sums(grad_packed[:, 1536:2304].astype(f32))
    grad[1, 0] = product(normed[...], grad_packed[:, 0:768], TN).astype(bf16)
    grad[0, 0] = product(normed[...], grad_packed[:, 768:1536], TN).astype(bf16)
    grad[0, 1] = product(normed[...], grad_packed[:, 1536:2304], TN).astype(bf16)
    grad[1, 1] = proj_grad[...]
    for line in range(2):
        for xr in range(2):
            save_chunk(grad.at[line, x ^ xr], (own, away), i, line, xr)
    bias[0:2, :] = jnp.zeros((2, WIDE), f32)
    for r in range(2):
        rows = slice(256 * r, 256 * r + 256)
        incoming = (
            product(grad_packed[rows, 0:768], weight[1, 0], NT)
            + product(grad_packed[rows, 768:1536], weight[0, 0], NT)
            + product(grad_packed[rows, 1536:2304], weight[0, 1], NT)
        )
        unit, root = unit_of(tok[rows, :].astype(f32))
        bias[0:1, :] += sums(incoming * unit)
        bias[1:2, :] += sums(incoming)
        tokens_grad[rows, :] = grad_middle[rows, :] + unit_back(unit, root, small[0:1, :], incoming)


def whole(shape):
    return pl.BlockSpec(shape, lambda *_: (0,) * len(shape))


def rowwise(width):
    return pl.BlockSpec((256, width), lambda r, info: (r, 0))


def steps(shape):
    return pl.BlockSpec((1,) + shape, lambda t, info: (t, 0, 0))


def run_kernel(kernel, grid, operands, outs, scratch, flops, moved):
    info = operands[0]
    specs = [spec or whole(array.shape) for spec, array in operands[1]]
    return pl.pallas_call(
        kernel,
        grid_spec=pltpu.PrefetchScalarGridSpec(
            num_scalar_prefetch=1,
            grid=(grid,),
            in_specs=specs,
            out_specs=[spec or whole(shape) for spec, shape, _ in outs],
            scratch_shapes=[pltpu.VMEM(shape, dtype) for shape, dtype in scratch],
        ),
        out_shape=[jax.ShapeDtypeStruct(shape, dtype) for _, shape, dtype in outs],
        compiler_params=pltpu.CompilerParams(
            dimension_semantics=("arbitrary",), vmem_limit_bytes=VMEM_BYTES
        ),
        cost_estimate=pl.CostEstimate(flops=flops, bytes_accessed=moved, transcendentals=0),
    )(info, *[array for _, array in operands[1]])


def fast_device(
    tokens,
    lengths,
    keep_mask,
    cotangent,
    ln1_gain,
    ln1_bias,
    qkv_weight,
    q_bias,
    v_bias,
    proj_weight,
    proj_bias,
    ln2_gain,
    ln2_bias,
    fc1_weight,
    fc1_bias,
    fc2_weight,
    fc2_bias,
):
    count = tokens.shape[0] * tokens.shape[1]
    i = lax.axis_index("fsdp")
    x = lax.axis_index("dp")
    info = jnp.concatenate(
        [jnp.stack([i, x]).astype(jnp.int32), lengths.reshape(-1), keep_mask.reshape(-1)]
    )
    tok = tokens.reshape(count, WIDE)
    cot = cotangent.reshape(count, WIDE)

    line = jnp.concatenate(
        [ln1_gain, ln1_bias, q_bias, v_bias, proj_bias, ln2_gain, ln2_bias, fc2_bias, fc1_bias]
    ).reshape(1, 576)
    line = jnp.pad(line, ((0, 0), (0, WIDE - 576)))
    for bit in (BIT_Z1, BIT_Z0, BIT_Y, BIT_C):
        line = join(line, hop(line, bit))
    order = jnp.array([(m & 1) * 8 + (m >> 1 & 1) * 4 + (m >> 2 & 1) * 2 + (m >> 3) for m in range(16)])
    turned = jnp.arange(16)[:, None] == (order ^ i)[None, :]
    line = jnp.dot(turned.astype(bf16), line, preferred_element_type=f32)
    small = jnp.concatenate(
        [
            line[:, :384].reshape(16, 8, 48).transpose(1, 0, 2).reshape(8, WIDE),
            line[:, 384:576].reshape(4, WIDE),
            jnp.zeros((4, WIDE), f32),
        ]
    )

    query, key, value = (qkv_weight[:, WIDE * k : WIDE * k + WIDE] for k in range(3))
    first = gather_group(jnp.stack([jnp.stack([key, query]), jnp.stack([value, proj_weight])]), x)
    up = gather_group(fc1_weight.reshape(PIECE, 2, 2, WIDE).transpose(1, 2, 0, 3), x)
    down = gather_group(fc2_weight.reshape(2, 2, PIECE, WIDE), x)

    def full(arrays):
        return [(None, array) for array in arrays]

    parts = (4, 8, PIECE, WIDE)
    packed, normed_one = run_kernel(
        qkv_kernel,
        1,
        (info, full((tok, small) + first)),
        [(None, (count, 3 * WIDE), bf16), (None, (count, WIDE), bf16)],
        [((2, 2, WIDE, WIDE), bf16)],
        2 * count * WIDE * 3 * WIDE,
        10 << 20,
    )
    attended, middle, normed_two, grad_two, lse = run_kernel(
        attend_kernel,
        2,
        (
            info,
            [(rowwise(3 * WIDE), packed), (rowwise(WIDE), tok), (rowwise(WIDE), cot), (None, small)]
            + full(first),
        ),
        [
            (rowwise(WIDE), (count, WIDE), bf16),
            (rowwise(WIDE), (count, WIDE), f32),
            (rowwise(WIDE), (count, WIDE), bf16),
            (rowwise(WIDE), (count, WIDE), bf16),
            (rowwise(128), (count, 128), f32),
        ],
        [((WIDE, WIDE), bf16)],
        8 * count * WIDE * WIDE,
        16 << 20,
    )
    hidden, active, fc2_own, fc2_away = run_kernel(
        up_kernel,
        4,
        (info, full((normed_two, grad_two, small) + up)),
        [
            (steps((count, WIDE)), (4, count, WIDE), f32),
            (steps((count, WIDE)), (4, count, WIDE), bf16),
            (None, parts, bf16),
            (None, parts, bf16),
        ],
        [((WIDE, WIDE), bf16), ((WIDE, WIDE), bf16)],
        16 * count * WIDE * WIDE,
        20 << 20,
    )
    output, grad_middle, grad_one, bias, fc1_own, fc1_away = run_kernel(
        down_kernel,
        4,
        (
            info,
            full((normed_two, grad_two))
            + [(steps((count, WIDE)), hidden), (steps((count, WIDE)), active)]
            + full((middle, cot, small) + up + down),
        ),
        [
            (None, (count, WIDE), bf16),
            (None, (count, WIDE), f32),
            (None, (count, WIDE), bf16),
            (None, (16, WIDE), f32),
            (None, parts, bf16),
            (None, parts, bf16),
        ],
        [
            ((WIDE, WIDE), bf16),
            ((WIDE, WIDE), bf16),
            ((count, WIDE), f32),
            ((count, WIDE), f32),
            ((WIDE, WIDE), bf16),
        ],
        32 * count * WIDE * WIDE,
        30 << 20,
    )
    grad_packed, proj_grad = run_kernel(
        attend_back_kernel,
        2,
        (
            info,
            [
                (rowwise(3 * WIDE), packed),
                (rowwise(128), lse),
                (rowwise(WIDE), attended),
                (rowwise(WIDE), grad_one),
            ]
            + full(first),
        ),
        [(rowwise(3 * WIDE), (count, 3 * WIDE), bf16), (None, (WIDE, WIDE), bf16)],
        [((WIDE, WIDE), bf16), ((WIDE, WIDE), f32)],
        16 * count * WIDE * WIDE,
        16 << 20,
    )
    tokens_grad, bias, qkv_own, qkv_away = run_kernel(
        qkv_back_kernel,
        1,
        (info, full((tok, normed_one, grad_packed, grad_middle, proj_grad, bias, small) + first)),
        [
            (None, (count, WIDE), f32),
            (None, (16, WIDE), f32),
            (None, parts, bf16),
            (None, parts, bf16),
        ],
        [((2, 2, WIDE, WIDE), bf16), ((2, 2, WIDE, WIDE), bf16)],
        12 * count * WIDE * WIDE,
        20 << 20,
    )

    down_mine, down_other = scatter_group(fc2_own, fc2_away)
    up_mine, up_other = scatter_group(fc1_own, fc1_away)
    qkv_mine, qkv_other = scatter_group(qkv_own, qkv_away)
    for bit in (BIT_C, BIT_Y, BIT_Z0, BIT_Z1):
        bias = bias + hop(bias, bit)
    bias = bias + swap(bias)
    narrow = lax.dynamic_slice(bias[:8].reshape(8, 16, 48), (0, i, 0), (8, 1, 48)).reshape(8, 48)
    broad = lax.dynamic_slice(bias[8:12].reshape(3072), (i * 192,), (192,))

    fc1_grad = jnp.concatenate([place(up_mine, up_other, x, k >> 1, k & 1) for k in range(4)], axis=1)
    fc2_grad = jnp.concatenate([place(down_mine, down_other, x, k >> 1, k & 1) for k in range(4)], axis=0)
    qkv_grad = jnp.concatenate(
        [place(qkv_mine, qkv_other, x, half, row) for half, row in ((0, 1), (0, 0), (1, 0))], axis=1
    )
    return (
        output.reshape(tokens.shape),
        tokens_grad.reshape(tokens.shape),
        narrow[0],
        narrow[1],
        qkv_grad,
        narrow[2],
        narrow[3],
        place(qkv_mine, qkv_other, x, 1, 1),
        narrow[4],
        narrow[5],
        narrow[6],
        fc1_grad,
        broad,
        fc2_grad,
        narrow[7],
    )


def solution(mesh):
    in_specs = (
        P(("dp", "fsdp"), None, None),
        P(("dp", "fsdp"), None),
        P(("dp", "fsdp"), None, None),
        P(("dp", "fsdp"), None, None),
        P("fsdp"),
        P("fsdp"),
        P("fsdp", None),
        P("fsdp"),
        P("fsdp"),
        P("fsdp", None),
        P("fsdp"),
        P("fsdp"),
        P("fsdp"),
        P("fsdp", None),
        P("fsdp"),
        P("fsdp", None),
        P("fsdp"),
    )
    out_specs = (
        P(("dp", "fsdp"), None, None),
        P(("dp", "fsdp"), None, None),
        P("fsdp"),
        P("fsdp"),
        P("fsdp", None),
        P("fsdp"),
        P("fsdp"),
        P("fsdp", None),
        P("fsdp"),
        P("fsdp"),
        P("fsdp"),
        P("fsdp", None),
        P("fsdp"),
        P("fsdp", None),
        P("fsdp"),
    )
    fits = mesh.shape["dp"] == 2 and mesh.shape["fsdp"] == 16
    return jax.shard_map(
        fast_device if fits else per_device, mesh=mesh, in_specs=in_specs, out_specs=out_specs, check_vma=False
    )
```

```python
import functools

import jax
import jax.numpy as jnp
from jax import lax
from jax.experimental import pallas as pl
from jax.experimental.pallas import tpu as pltpu
from jax.sharding import PartitionSpec as P

HEADS = 12


EPSILON = 1e-06
KEEP_RATE = 0.9
NEGATIVE = -1e30


def normalize(values, gain, shift):
    center = values - jnp.mean(values, axis=-1, keepdims=True)
    spread = jnp.mean(center * center, axis=-1, keepdims=True)
    return center * lax.rsqrt(spread + EPSILON) * gain + shift


def standardize(values):
    center = values - jnp.mean(values, axis=-1, keepdims=True)
    spread = jnp.mean(center * center, axis=-1, keepdims=True)
    return center * lax.rsqrt(spread + EPSILON)


def affine_low(unit_values, gain, shift):
    return (unit_values * gain.astype(jnp.float32) + shift.astype(jnp.float32)).astype(jnp.bfloat16)


def exact_gelu(values):
    return jax.nn.gelu(values, approximate=False)


def norm_back(values, gain, shift, incoming):
    _, pullback = jax.vjp(normalize, values, gain, shift)
    return pullback(incoming)


def inner_rows(left, right):
    return lax.dot_general(
        left, right, (((0,), (0,)), ((), ())), preferred_element_type=jnp.float32
    )


def times_transpose(left, right):
    return lax.dot_general(
        left, right, (((1,), (1,)), ((), ())), preferred_element_type=jnp.float32
    )


def layout(lengths, keep_mask, length):
    image_ends = jnp.cumsum(lengths, axis=-1, dtype=jnp.int32)
    position = jnp.arange(length, dtype=jnp.int32)
    segment = jnp.sum(
        (position[None, :, None] >= image_ends[:, None, :]).astype(jnp.int32),
        axis=-1,
        dtype=jnp.int32,
    )
    images = jnp.arange(lengths.shape[1], dtype=jnp.int32)
    member = (segment[:, :, None] == images[None, None, :]).astype(jnp.float32)
    keeping = keep_mask.astype(jnp.float32)
    scales = jnp.sum(member[:, :, :, None] * keeping[:, None, :, :], axis=2) / KEEP_RATE
    inside = jnp.sum(member, axis=-1)
    return (segment, scales, inside)


def attention_forward(packed, segment, rowset, length, head_size):
    split_view = packed.reshape(rowset, length, 3, HEADS, head_size)
    queries = split_view[:, :, 0]
    keys_all = split_view[:, :, 1]
    values_all = split_view[:, :, 2]
    scores = jnp.einsum(
        "rqhd,rkhd->rhqk", queries, keys_all, preferred_element_type=jnp.float32
    ) * head_size ** (-0.5)
    matching = segment[:, :, None] == segment[:, None, :]
    scores = jnp.where(matching[:, None], scores, NEGATIVE)
    raised = jnp.exp(scores - jnp.max(scores, axis=-1, keepdims=True))
    weighting = raised / jnp.sum(raised, axis=-1, keepdims=True)
    weighting_low = weighting.astype(jnp.bfloat16)
    attended = jnp.einsum(
        "rhqk,rkhd->rqhd", weighting_low, values_all, preferred_element_type=jnp.float32
    )
    attended = attended.reshape(rowset * length, HEADS * head_size).astype(jnp.bfloat16)
    return (queries, keys_all, values_all, weighting, weighting_low, attended)


def per_device(
    tokens,
    lengths,
    keep_mask,
    cotangent,
    ln1_gain,
    ln1_bias,
    qkv_weight,
    q_bias,
    v_bias,
    proj_weight,
    proj_bias,
    ln2_gain,
    ln2_bias,
    fc1_weight,
    fc1_bias,
    fc2_weight,
    fc2_bias,
):
    rowset, length, features = tokens.shape
    head_size = features // HEADS
    token_count = rowset * length
    segment, scales, inside = layout(lengths, keep_mask, length)
    scale_one = scales[:, :, 0].reshape(token_count, 1)
    scale_two = scales[:, :, 1].reshape(token_count, 1)
    inside_column = inside.reshape(token_count, 1)
    flattened = tokens.reshape(token_count, features).astype(jnp.float32)
    unit_one = standardize(flattened)
    qkv_full, proj_full, gain_one, shift_one, query_bias, value_bias, out_bias = (
        lax.all_gather(qkv_weight, "fsdp", axis=0, tiled=True),
        lax.all_gather(proj_weight, "fsdp", axis=0, tiled=True),
        lax.all_gather(ln1_gain, "fsdp", axis=0, tiled=True),
        lax.all_gather(ln1_bias, "fsdp", axis=0, tiled=True),
        lax.all_gather(q_bias, "fsdp", axis=0, tiled=True),
        lax.all_gather(v_bias, "fsdp", axis=0, tiled=True),
        lax.all_gather(proj_bias, "fsdp", axis=0, tiled=True),
    )
    normed_one = affine_low(unit_one, gain_one, shift_one)
    bias_all = jnp.concatenate(
        [
            query_bias.astype(jnp.float32),
            jnp.zeros((features,), jnp.float32),
            value_bias.astype(jnp.float32),
        ]
    )
    packed = (jnp.dot(normed_one, qkv_full, preferred_element_type=jnp.float32) + bias_all).astype(
        jnp.bfloat16
    )
    _, _, _, _, _, attended = attention_forward(packed, segment, rowset, length, head_size)
    branch_one = jnp.dot(attended, proj_full, preferred_element_type=jnp.float32) + out_bias.astype(
        jnp.float32
    )
    middle = flattened + scale_one * branch_one
    unit_two = standardize(middle)
    up_full, down_full, gain_two, shift_two, up_bias, down_bias = (
        lax.all_gather(fc1_weight, "fsdp", axis=0, tiled=True),
        lax.all_gather(fc2_weight, "fsdp", axis=0, tiled=True),
        lax.all_gather(ln2_gain, "fsdp", axis=0, tiled=True),
        lax.all_gather(ln2_bias, "fsdp", axis=0, tiled=True),
        lax.all_gather(fc1_bias, "fsdp", axis=0, tiled=True),
        lax.all_gather(fc2_bias, "fsdp", axis=0, tiled=True),
    )
    normed_two = affine_low(unit_two, gain_two, shift_two)
    hidden = jnp.dot(normed_two, up_full, preferred_element_type=jnp.float32) + up_bias.astype(
        jnp.float32
    )
    active = exact_gelu(hidden).astype(jnp.bfloat16)
    branch_two = jnp.dot(active, down_full, preferred_element_type=jnp.float32) + down_bias.astype(
        jnp.float32
    )
    output = (
        ((middle + scale_two * branch_two) * inside_column)
        .astype(jnp.bfloat16)
        .reshape(rowset, length, features)
    )
    up_full, down_full = (
        lax.all_gather(fc1_weight, "fsdp", axis=0, tiled=True),
        lax.all_gather(fc2_weight, "fsdp", axis=0, tiled=True),
    )
    gain_two_f = gain_two.astype(jnp.float32)
    shift_two_f = shift_two.astype(jnp.float32)
    grad_out = cotangent.reshape(token_count, features).astype(jnp.float32) * inside_column
    grad_two_low = (grad_out * scale_two).astype(jnp.bfloat16)
    fc2_grad = inner_rows(active, grad_two_low)
    fc2_bias_part = jnp.sum(grad_two_low.astype(jnp.float32), axis=0)
    grad_active = times_transpose(grad_two_low, down_full)
    _, gelu_pull = jax.vjp(exact_gelu, hidden)
    grad_hidden_low = gelu_pull(grad_active)[0].astype(jnp.bfloat16)
    fc1_grad = inner_rows(normed_two, grad_hidden_low)
    fc1_bias_part = jnp.sum(grad_hidden_low.astype(jnp.float32), axis=0)
    grad_normed_two = times_transpose(grad_hidden_low, up_full)
    grad_middle_norm, gain_two_part, shift_two_part = norm_back(
        middle, gain_two_f, shift_two_f, grad_normed_two
    )
    grad_middle = grad_out + grad_middle_norm
    qkv_full, proj_full = (
        lax.all_gather(qkv_weight, "fsdp", axis=0, tiled=True),
        lax.all_gather(proj_weight, "fsdp", axis=0, tiled=True),
    )
    gain_one_f = gain_one.astype(jnp.float32)
    shift_one_f = shift_one.astype(jnp.float32)
    queries, keys_all, values_all, weighting, weighting_low, attended = attention_forward(
        packed, segment, rowset, length, head_size
    )
    grad_one_low = (grad_middle * scale_one).astype(jnp.bfloat16)
    proj_grad = inner_rows(attended, grad_one_low)
    proj_bias_part = jnp.sum(grad_one_low.astype(jnp.float32), axis=0)
    grad_attended_low = times_transpose(grad_one_low, proj_full).astype(jnp.bfloat16)
    grad_attended_low = grad_attended_low.reshape(rowset, length, HEADS, head_size)
    grad_weighting = jnp.einsum(
        "rqhd,rkhd->rhqk", grad_attended_low, values_all, preferred_element_type=jnp.float32
    )
    value_grad = jnp.einsum(
        "rhqk,rqhd->rkhd", weighting_low, grad_attended_low, preferred_element_type=jnp.float32
    )
    row_inner = jnp.sum(grad_weighting * weighting, axis=-1, keepdims=True)
    grad_scores_low = (weighting * (grad_weighting - row_inner)).astype(jnp.bfloat16)
    key_scale = head_size ** (-0.5)
    query_grad = (
        jnp.einsum("rhqk,rkhd->rqhd", grad_scores_low, keys_all, preferred_element_type=jnp.float32)
        * key_scale
    )
    key_grad = (
        jnp.einsum("rhqk,rqhd->rkhd", grad_scores_low, queries, preferred_element_type=jnp.float32)
        * key_scale
    )
    grad_packed_low = (
        jnp.stack([query_grad, key_grad, value_grad], axis=2)
        .reshape(token_count, 3 * features)
        .astype(jnp.bfloat16)
    )
    qkv_grad = inner_rows(normed_one, grad_packed_low)
    column_sums = jnp.sum(grad_packed_low.astype(jnp.float32), axis=0)
    query_bias_part = column_sums[:features]
    value_bias_part = column_sums[2 * features :]
    grad_normed_one = times_transpose(grad_packed_low, qkv_full)
    grad_input_norm, gain_one_part, shift_one_part = norm_back(
        flattened, gain_one_f, shift_one_f, grad_normed_one
    )
    tokens_grad = (grad_middle + grad_input_norm).reshape(rowset, length, features)
    (
        gain_two_grad,
        shift_two_grad,
        fc1_weight_part,
        fc1_bias_shard,
        fc2_weight_part,
        fc2_bias_shard,
    ) = (
        lax.psum_scatter(gain_two_part, "fsdp", scatter_dimension=0, tiled=True),
        lax.psum_scatter(shift_two_part, "fsdp", scatter_dimension=0, tiled=True),
        lax.psum_scatter(fc1_grad, "fsdp", scatter_dimension=0, tiled=True),
        lax.psum_scatter(fc1_bias_part, "fsdp", scatter_dimension=0, tiled=True),
        lax.psum_scatter(fc2_grad, "fsdp", scatter_dimension=0, tiled=True),
        lax.psum_scatter(fc2_bias_part, "fsdp", scatter_dimension=0, tiled=True),
    )
    (
        gain_one_grad,
        shift_one_grad,
        qkv_weight_part,
        query_bias_shard,
        value_bias_shard,
        proj_weight_part,
        proj_bias_shard,
    ) = (
        lax.psum_scatter(gain_one_part, "fsdp", scatter_dimension=0, tiled=True),
        lax.psum_scatter(shift_one_part, "fsdp", scatter_dimension=0, tiled=True),
        lax.psum_scatter(qkv_grad, "fsdp", scatter_dimension=0, tiled=True),
        lax.psum_scatter(query_bias_part, "fsdp", scatter_dimension=0, tiled=True),
        lax.psum_scatter(value_bias_part, "fsdp", scatter_dimension=0, tiled=True),
        lax.psum_scatter(proj_grad, "fsdp", scatter_dimension=0, tiled=True),
        lax.psum_scatter(proj_bias_part, "fsdp", scatter_dimension=0, tiled=True),
    )
    summed = (
        lax.psum(gain_one_grad.astype(jnp.bfloat16), "dp").astype(jnp.float32),
        lax.psum(shift_one_grad.astype(jnp.bfloat16), "dp").astype(jnp.float32),
        lax.psum(qkv_weight_part.astype(jnp.bfloat16), "dp").astype(jnp.float32),
        lax.psum(query_bias_shard.astype(jnp.bfloat16), "dp").astype(jnp.float32),
        lax.psum(value_bias_shard.astype(jnp.bfloat16), "dp").astype(jnp.float32),
        lax.psum(proj_weight_part.astype(jnp.bfloat16), "dp").astype(jnp.float32),
        lax.psum(proj_bias_shard.astype(jnp.bfloat16), "dp").astype(jnp.float32),
        lax.psum(gain_two_grad.astype(jnp.bfloat16), "dp").astype(jnp.float32),
        lax.psum(shift_two_grad.astype(jnp.bfloat16), "dp").astype(jnp.float32),
        lax.psum(fc1_weight_part.astype(jnp.bfloat16), "dp").astype(jnp.float32),
        lax.psum(fc1_bias_shard.astype(jnp.bfloat16), "dp").astype(jnp.float32),
        lax.psum(fc2_weight_part.astype(jnp.bfloat16), "dp").astype(jnp.float32),
        lax.psum(fc2_bias_shard.astype(jnp.bfloat16), "dp").astype(jnp.float32),
    )
    return (
        output,
        tokens_grad,
        summed[0],
        summed[1],
        summed[2],
        summed[3],
        summed[4],
        summed[5],
        summed[6],
        summed[7],
        summed[8],
        summed[9],
        summed[10],
        summed[11],
        summed[12],
    )


BIT_Z1, BIT_Z0, BIT_Y, BIT_C = 8, 4, 2, 1
PIECE = 48
WIDE = 768
SCALE_ON = 1.0 / 0.9
VMEM_BYTES = 56 * 1024 * 1024
f32 = jnp.float32
bf16 = jnp.bfloat16


def hop(array, bit):
    return lax.ppermute(array, "fsdp", [(i, i ^ bit) for i in range(16)])


def swap(array):
    return lax.ppermute(array, "dp", [(0, 1), (1, 0)])


def join(*arrays):
    return jnp.concatenate(arrays, axis=0)


def tie(array, *before):
    return lax.optimization_barrier((array,) + before)[0]


def to_other_core(own):
    return own + tuple(hop(part, BIT_C) for part in own)


def plus(left, right):
    return (left.astype(f32) + right.astype(f32)).astype(bf16)


def core_sums(own, came):
    return tuple(plus(own[a], came[a]) for a in range(4))


def first_hops(parts):
    return swap(parts[1]), hop(parts[3], BIT_Y)


def first_sums(parts, got):
    return (
        plus(parts[0][:4], got[0][:4]),
        plus(parts[0][4:], got[0][4:]),
        plus(parts[2][:4], got[1][:4]),
        plus(parts[2][4:], got[1][4:]),
    )


def second_hops(parts):
    return hop(parts[1], BIT_Y), swap(parts[3])


def second_sums(parts, got):
    return tuple(
        jnp.stack([plus(parts[0][half], got[0][half]), plus(parts[2][half], got[1][half])])
        for half in (slice(0, 2), slice(2, 4))
    )


def third_hops(parts):
    return (hop(parts[1], BIT_Z0),)


def third_sums(parts, got):
    return plus(parts[0][:, 0], got[0][:, 0]), plus(parts[0][:, 1], got[0][:, 1])


def fourth_hops(parts):
    return (hop(parts[1], BIT_Z1),)


def fourth_sums(parts, got):
    return plus(parts[0], got[0])


def place(mine, other, x, half, line):
    return jnp.where(x == half, mine[line], other[line]).astype(f32)


def product(left, right, dims):
    return lax.dot_general(left, right, (dims, ((), ())), preferred_element_type=f32)


NN = ((1,), (0,))
NT = ((1,), (1,))
TN = ((0,), (0,))


def slot(line, xr, yr):
    return (xr, yr) if line == 0 else (2 + yr, xr)


def load_chunk(store, refs, i, line, xr):
    for m in range(16):
        c, yr, z0r, z1r = m & 1, (m >> 1) & 1, (m >> 2) & 1, (m >> 3) & 1
        array, part = slot(line, xr, yr) if isinstance(xr, int) else (2 + yr, xr)
        row = pl.multiple_of((i ^ m) * PIECE, 16)
        store[pl.ds(row, PIECE), :] = refs[4 * c + array][part * 4 + z0r * 2 + z1r]


def save_chunk(value, outs, i, line, xr):
    for m in range(16):
        c, yr, z0r, z1r = m & 1, (m >> 1) & 1, (m >> 2) & 1, (m >> 3) & 1
        array, part = slot(line, xr, yr) if isinstance(xr, int) else (2 + yr, xr)
        row = pl.multiple_of((i ^ m) * PIECE, 16)
        outs[c][array, part * 4 + z0r * 2 + z1r] = value[pl.ds(row, PIECE), :]


def row_facts(info, r):
    first = info[2 + 3 * r]
    second = first + info[3 + 3 * r]
    third = second + info[4 + 3 * r]

    def segment(shape, axis):
        t = lax.broadcasted_iota(jnp.int32, shape, axis)
        return (t >= first).astype(jnp.int32) + (t >= second).astype(jnp.int32) + (t >= third).astype(jnp.int32)

    column = segment((256, 1), 0)

    def scale(branch):
        keeps = [info[8 + 6 * r + 2 * j + branch].astype(f32) * SCALE_ON for j in range(3)]
        return jnp.where(
            column == 0, keeps[0], jnp.where(column == 1, keeps[1], jnp.where(column == 2, keeps[2], 0.0))
        )

    inside = jnp.where(column < 3, 1.0, 0.0).astype(f32)
    return column, segment((1, 256), 1), scale, inside


def unit_of(values):
    center = values - jnp.mean(values, axis=-1, keepdims=True)
    spread = jnp.mean(center * center, axis=-1, keepdims=True)
    root = lax.rsqrt(spread + EPSILON)
    return center * root, root


def unit_back(unit, root, gain, incoming):
    eg = incoming * gain
    return root * (
        eg - jnp.mean(eg, axis=-1, keepdims=True) - unit * jnp.mean(eg * unit, axis=-1, keepdims=True)
    )


def sums(values):
    return jnp.sum(values, axis=0, keepdims=True)


def load_direct(store, own, other, i, spots):
    for m in range(16):
        spot = spots[0] * (m >> 3) + spots[1] * (m >> 2 & 1) + spots[2] * (m >> 1 & 1)
        row = pl.multiple_of((i ^ m) * PIECE, 16)
        store[pl.ds(row, PIECE), :] = (other if m & 1 else own)[spot, 0:PIECE, :]


def prepare_kernel(info, qkv, fc1, fc2, *rest):
    vectors, (pair, ahead, up, down) = rest[:9], rest[9:]
    x = info[1]
    ahead[0, 0:PIECE, :] = qkv[:, 0:WIDE]
    rows = [jnp.pad(v[...].astype(f32).reshape(1, -1), ((0, 0), (0, 256 - v.shape[0]))) for v in vectors]
    ahead[0, PIECE : PIECE + 16, 0:256] = jnp.concatenate(rows + [jnp.zeros((7, 256), f32)]).astype(bf16)
    ahead[0, PIECE : PIECE + 16, 256:WIDE] = jnp.zeros((16, WIDE - 256), bf16)
    for line in range(2):
        at = pl.multiple_of(WIDE + WIDE * x + 384 * line, 128)
        pair[line] = qkv[:, pl.ds(at, 384)]
        up[line] = fc1[:, pl.ds(pl.multiple_of((2 * x + line) * WIDE, 128), WIDE)]
        down[line] = fc2[pl.ds(pl.multiple_of((2 * x + line) * PIECE, 16), PIECE), :]


def load_qkv(weight, refs, query_own, query_other, i, x):
    load_direct(weight.at[0], query_own, query_other, i, (2, 4, 1))
    for line in range(2):
        for xr in range(2):
            load_chunk(weight.at[1 + (x ^ xr), :, 384 * line : 384 * line + 384], refs, i, line, xr)


def qkv_kernel(info, tok, small, *rest):
    refs, (query_own, query_other, packed, normed, weight) = rest[:8], rest[8:]
    i, x = info[0], info[1]
    load_qkv(weight, refs, query_own, query_other, i, x)
    for r in range(2):
        rows = slice(256 * r, 256 * r + 256)
        unit, _ = unit_of(tok[rows, :].astype(f32))
        normed[rows, :] = (unit * small[0:1, :] + small[1:2, :]).astype(bf16)
    for r in range(2):
        rows = slice(256 * r, 256 * r + 256)
        low = normed[rows, :]
        packed[rows, 0:768] = (product(low, weight[0], NN) + small[2:3, :]).astype(bf16)
        packed[rows, 768:1536] = product(low, weight[1], NN).astype(bf16)
        packed[rows, 1536:2304] = (product(low, weight[2], NN) + small[3:4, :]).astype(bf16)


def attend_kernel(info, packed, cot, attended, grad_two, lse):
    r = pl.program_id(0)
    column, across, scale, inside = row_facts(info, r)
    same = column == across
    lane = lax.broadcasted_iota(jnp.int32, (256, 128), 1)
    kept = jnp.zeros((256, 128), f32)
    for h in range(0, HEADS, 2):
        pair = []
        for g in (h, h + 1):
            query = packed[:, 64 * g : 64 * g + 64] * 0.125
            scores = product(query, packed[:, 768 + 64 * g : 832 + 64 * g], NT)
            scores = jnp.where(same, scores, NEGATIVE)
            top = jnp.max(scores, axis=-1, keepdims=True)
            raised = jnp.exp(scores - top)
            total = jnp.sum(raised, axis=-1, keepdims=True)
            low = (raised / total).astype(bf16)
            pair.append(product(low, packed[:, 1536 + 64 * g : 1600 + 64 * g], NN).astype(bf16))
            kept = jnp.where(lane == g, top + jnp.log(total), kept)
        attended[:, 64 * h : 64 * h + 128] = jnp.concatenate(pair, axis=1)
    lse[...] = kept
    grad_two[...] = (cot[...].astype(f32) * inside * scale(1)).astype(bf16)


def up_kernel(info, attended, tok, grad_two, small, proj_own, proj_other, *rest):
    refs, (middle, normed, hidden, active, own, away, proj, weight, grad) = rest[:8], rest[8:]
    i, x, t = info[0], info[1], pl.program_id(0)
    block = ((t & 1) ^ x) * 2 + (t >> 1)

    @pl.when(t == 0)
    def _():
        load_direct(proj, proj_own, proj_other, i, (1, 2, 4))
        for r in range(2):
            rows = slice(256 * r, 256 * r + 256)
            _, _, scale, _ = row_facts(info, r)
            branch = product(attended[rows, :], proj[...], NN) + small[4:5, :]
            after = tok[rows, :].astype(f32) + scale(0) * branch
            middle[rows, :] = after
            unit, _ = unit_of(after)
            normed[rows, :] = (unit * small[5:6, :] + small[6:7, :]).astype(bf16)

    for step in range(4):

        @pl.when(t == step)
        def _():
            load_chunk(weight, refs, i, step >> 1, step & 1)

    value = product(normed[...], weight[...], NN) + small[pl.ds(8 + block, 1), :]
    hidden[0] = value
    low = (0.5 * value * (1.0 + lax.erf(value * (0.5**0.5)))).astype(bf16)
    active[0] = low
    grad[...] = product(low, grad_two[...], TN).astype(bf16)
    far = block ^ (i >> 2)
    spot = (far & 1) * 2 + (far >> 1)
    for line in range(2):
        for xr in range(2):
            for near in range(4):
                c, yr = near & 1, near >> 1
                array, part = slot(line, xr, yr)
                row = ((i & 3) ^ near) * 192 + ((xr ^ x) * 2 + line) * PIECE
                (own, away)[c][array, part * 4 + spot] = grad[pl.ds(pl.multiple_of(row, 16), PIECE), :]


def down_kernel(line, info, normed, grad_two, hidden, active, small, *rest):
    refs1 = [None] * 8
    refs1[2 * line], refs1[2 * line + 1], refs1[4 + 2 * line], refs1[5 + 2 * line] = rest[:4]
    refs2, rest = rest[4:12], rest[12:]
    if line == 0:
        branch, grad_normed, bias, own, away, weight1, weight2, grad = rest
    else:
        branch_in, grad_normed_in, bias_in, middle, cot, result, grad_middle, grad_one, bias = rest[:9]
        own, away, weight1, weight2, grad, branch, grad_normed = rest[9:]
    i, x, t = info[0], info[1], pl.program_id(0)
    block = (t ^ x) * 2 + line

    @pl.when(t == 0)
    def _():
        if line == 0:
            branch[...] = jnp.zeros_like(branch)
            grad_normed[...] = jnp.zeros_like(grad_normed)
            bias[...] = jnp.zeros_like(bias)
            bias[7:8, :] = sums(grad_two[...].astype(f32))
        else:
            branch[...] = branch_in[...]
            grad_normed[...] = grad_normed_in[...]
            bias[...] = bias_in[...]

    for step in range(2):

        @pl.when(t == step)
        def _():
            load_chunk(weight1, refs1, i, line, step)

    far = block ^ (i >> 2)
    spot = (far & 1) * 2 + (far >> 1)
    for row_line in range(2):
        for xr in range(2):
            for near in range(4):
                c, yr = near & 1, near >> 1
                array, part = slot(row_line, xr, yr)
                row = ((i & 3) ^ near) * 192 + ((xr ^ x) * 2 + row_line) * PIECE
                weight2[pl.ds(pl.multiple_of(row, 16), PIECE), :] = refs2[4 * c + array][part * 4 + spot]

    branch[...] += product(active[0], weight2[...], NN)
    value = hidden[0]
    slope = 0.5 * (1.0 + lax.erf(value * (0.5**0.5))) + value * (
        jnp.exp(-0.5 * value * value) * 0.3989422804014327
    )
    low = (product(grad_two[...], weight2[...], NT) * slope).astype(bf16)
    bias[pl.ds(8 + block, 1), :] = sums(low.astype(f32))
    grad_normed[...] += product(low, weight1[...], NT)
    grad[...] = product(normed[...], low, TN).astype(bf16)
    for m in range(16):
        c, yr, z0r, z1r = m & 1, (m >> 1) & 1, (m >> 2) & 1, (m >> 3) & 1
        array, part = (t, yr) if line == 0 else (yr, t)
        row = pl.multiple_of((i ^ m) * PIECE, 16)
        (own, away)[c][array, part * 4 + z0r * 2 + z1r] = grad[pl.ds(row, PIECE), :]

    if line == 1:

        @pl.when(t == 1)
        def _():
            for r in range(2):
                rows = slice(256 * r, 256 * r + 256)
                _, _, scale, inside = row_facts(info, r)
                after = middle[rows, :]
                result[rows, :] = (
                    (after + scale(1) * (branch[rows, :] + small[7:8, :])) * inside
                ).astype(bf16)
                unit, root = unit_of(after)
                incoming = grad_normed[rows, :]
                bias[5:6, :] += sums(incoming * unit)
                bias[6:7, :] += sums(incoming)
                total = cot[rows, :].astype(f32) * inside + unit_back(unit, root, small[5:6, :], incoming)
                grad_middle[rows, :] = total
                low_one = (total * scale(0)).astype(bf16)
                grad_one[rows, :] = low_one
                bias[4:5, :] += sums(low_one.astype(f32))


def attend_back_kernel(group, info, queries, keys, values, lse, attended, grad_one, normed, *rest):
    if group == 0:
        proj_own, proj_other, grad_packed, own, away, weight, proj_rest, grad, total = rest
    else:
        weight, proj_rest, grad_packed, own, away, grad = rest
    i, x, r = info[0], info[1], pl.program_id(0)
    if group == 0:

        @pl.when(r == 0)
        def _():
            load_direct(weight, proj_own, proj_other, i, (1, 2, 4))
            total[...] = jnp.zeros_like(total)

        total[...] += product(attended[...], grad_one[...], TN)

    column, across, _, _ = row_facts(info, r)
    same = column == across
    grad_attended = product(grad_one[...], weight[384 * group : 384 * group + 384, :], NT).astype(bf16)
    rows = pl.ds(pl.multiple_of(r * 256, 256), 256)
    for h in range(0, 6, 2):
        pairs = ([], [], [])
        for g in (h, h + 1):
            here = slice(64 * g, 64 * g + 64)
            query = queries[:, here] * 0.125
            key = keys[:, here]
            value = values[:, here]
            back = grad_attended[:, here]
            scores = product(query, key, NT)
            head = 6 * group + g
            weighting = jnp.where(same, jnp.exp(scores - lse[:, head : head + 1]), 0.0)
            grad_weighting = product(back, value, NT)
            pairs[2].append(product(weighting.astype(bf16), back, TN))
            inner = jnp.sum(grad_weighting * weighting, axis=-1, keepdims=True)
            low = (weighting * (grad_weighting - inner)).astype(bf16)
            pairs[0].append(product(low, key, NN) * 0.125)
            pairs[1].append(product(low, query, TN))
        for k in range(3):
            grad_packed[rows, 384 * k + 64 * h : 384 * k + 64 * h + 128] = jnp.concatenate(
                pairs[k], axis=1
            ).astype(bf16)

    @pl.when(r == 1)
    def _():
        low = normed[...]
        grad[1, 0] = product(low, grad_packed[:, 0:384], TN).astype(bf16)
        grad[0, 0] = product(low, grad_packed[:, 384:768], TN).astype(bf16)
        grad[0, 1] = product(low, grad_packed[:, 768:1152], TN).astype(bf16)
        if group == 0:
            grad[1, 1] = total[:, 0:384].astype(bf16)
            proj_rest[...] = total[:, 384:768].astype(bf16)
        else:
            grad[1, 1] = proj_rest[...]
        for line in range(2):
            for xr in range(2):
                save_chunk(grad.at[line, x ^ xr], (own, away), i, line, xr)


def tokens_back_kernel(r, info, tok, back0, back1, grad_middle, bias_in, small, *rest):
    refs, (query_own, query_other), (tokens_grad, bias, weight) = rest[:8], rest[8:10], rest[-3:]
    i, x = info[0], info[1]
    load_qkv(weight, refs, query_own, query_other, i, x)
    bias[...] = bias_in[...]
    for part, back in ((0, back0), (1, back1)):
        columns = slice(384 * part, 384 * part + 384)
        bias[2:3, columns] += sums(back[:, 0:384].astype(f32))
        bias[3:4, columns] += sums(back[:, 768:1152].astype(f32))
    incoming = jnp.zeros((256, WIDE), f32)
    for k in range(3):
        here = slice(384 * k, 384 * k + 384)
        joined = jnp.concatenate([back0[:, here], back1[:, here]], axis=1)
        incoming += product(joined, weight[k], NT)
    unit, root = unit_of(tok[...].astype(f32))
    bias[0:1, :] += sums(incoming * unit)
    bias[1:2, :] += sums(incoming)
    tokens_grad[...] = grad_middle[...] + unit_back(unit, root, small[0:1, :], incoming)


def results_kernel(info, mine0, other0, mine1, other1, bias, qkv, proj, *vectors):
    i, x = info[0], info[1]
    for group, mine, other in ((0, mine0, other0), (1, mine1, other1)):
        for line, half, column in ((1, 0, 0), (0, 0, 768), (0, 1, 1536), (1, 1, None)):
            a, b = mine[line].astype(f32), other[line].astype(f32)
            value = jnp.where(x == half, a, b)
            if column is None:
                proj[:, 384 * group : 384 * group + 384] = value
            else:
                qkv[:, column + 384 * group : column + 384 * group + 384] = value

    def cut(rows, start, width):
        feature = lax.broadcasted_iota(jnp.int32, (WIDE, width), 0)
        lane = lax.broadcasted_iota(jnp.int32, (WIDE, width), 1)
        chosen = (feature == lane + start).astype(f32)
        return lax.dot_general(
            rows, chosen, (NN, ((), ())), precision=lax.Precision.HIGHEST, preferred_element_type=f32
        )

    narrow = cut(bias[0:8, :], i * 48, 128)
    for k in range(8):
        vectors[k][...] = narrow[k, 0:48]
    wide = cut(bias[8:16, :], (i & 3) * 192, 256)
    chosen = lax.broadcasted_iota(jnp.int32, (8, 256), 0) == (i >> 2)
    vectors[8][...] = jnp.sum(jnp.where(chosen, wide, 0.0), axis=0)[0:192]


def whole(shape):
    return pl.BlockSpec(shape, lambda *_: (0,) * len(shape))


def rowwise(width):
    return pl.BlockSpec((256, width), lambda r, info: (r, 0))


def steps(shape):
    return pl.BlockSpec((1,) + shape, lambda t, info: (t, 0, 0))


def run_kernel(kernel, grid, info, operands, outs, scratch, microseconds, alias=None):
    return pl.pallas_call(
        kernel,
        grid_spec=pltpu.PrefetchScalarGridSpec(
            num_scalar_prefetch=1,
            grid=(grid,),
            in_specs=[spec or whole(array.shape) for spec, array in operands],
            out_specs=[spec or whole(shape) for spec, shape, _ in outs],
            scratch_shapes=[pltpu.VMEM(shape, dtype) for shape, dtype in scratch],
        ),
        out_shape=[jax.ShapeDtypeStruct(shape, dtype) for _, shape, dtype in outs],
        input_output_aliases=alias or {},
        compiler_params=pltpu.CompilerParams(
            dimension_semantics=("arbitrary",), vmem_limit_bytes=VMEM_BYTES
        ),
        cost_estimate=pl.CostEstimate(
            flops=int(microseconds * 1.15e9), bytes_accessed=1 << 20, transcendentals=0
        ),
    )(info, *[array for _, array in operands])


def fast_device(
    tokens,
    lengths,
    keep_mask,
    cotangent,
    ln1_gain,
    ln1_bias,
    qkv_weight,
    q_bias,
    v_bias,
    proj_weight,
    proj_bias,
    ln2_gain,
    ln2_bias,
    fc1_weight,
    fc1_bias,
    fc2_weight,
    fc2_bias,
):
    count = tokens.shape[0] * tokens.shape[1]
    i = lax.axis_index("fsdp")
    x = lax.axis_index("dp")
    info = jnp.concatenate(
        [jnp.stack([i, x]).astype(jnp.int32), lengths.reshape(-1), keep_mask.reshape(-1)]
    )
    tok = tokens.reshape(count, WIDE)
    cot = cotangent.reshape(count, WIDE)

    def full(*arrays):
        return [(None, array) for array in arrays]

    vectors = (ln1_gain, ln1_bias, q_bias, v_bias, proj_bias, ln2_gain, ln2_bias, fc2_bias, fc1_bias)
    pair, ahead, up, down = run_kernel(
        prepare_kernel,
        1,
        info,
        full(qkv_weight, fc1_weight, fc2_weight, *vectors),
        [
            (None, (2, PIECE, 384), bf16),
            (None, (1, 64, WIDE), bf16),
            (None, (2, PIECE, WIDE), bf16),
            (None, (2, PIECE, WIDE), bf16),
        ],
        [],
        2,
    )

    far = hop(pair, BIT_Z1)
    ahead = join(ahead, hop(ahead, BIT_Y))
    pair = jnp.stack([pair, far], axis=1)
    far = hop(pair, BIT_Z0)
    ahead_far = hop(ahead, BIT_Z1)
    ahead = join(ahead, ahead_far)
    line0, line1 = join(pair[0], far[0]), join(pair[1], far[1])
    wide0 = join(line0, hop(line0, BIT_Y))
    wide1 = join(line1, swap(line1))
    line0, line1, up = lax.optimization_barrier((line0, line1, up))
    got0, got1 = hop(line0, BIT_Y), swap(line1)
    up_far = hop(up, BIT_Z1)
    got0, got1, up_far = lax.optimization_barrier((got0, got1, up_far))
    wide0, wide1 = join(line0, got0), join(line1, got1)
    got0, got1, ahead_far = swap(wide0), hop(wide1, BIT_Y), hop(ahead, BIT_Z0)
    up = jnp.stack([up, up_far], axis=1)
    up_far = hop(up, BIT_Z0)
    down = tie(join(down, proj_weight[None]), got0, got1)
    ahead = join(ahead, ahead_far)
    got0, got1, up_far = lax.optimization_barrier((got0, got1, up_far))
    first = to_other_core((wide0, got0, wide1, got1))
    ahead_other = hop(ahead, BIT_C)

    up_line0, up_line1 = join(up[0], up_far[0]), join(up[1], up_far[1])
    up_got0, up_got1 = hop(up_line0, BIT_Y), swap(up_line1)
    down_far = hop(down, BIT_Z1)

    vectors = jnp.concatenate([ahead[:, PIECE : PIECE + 9, :192], ahead_other[:, PIECE : PIECE + 9, :192]])
    origin = jnp.array([(p >> 1 & 1) * 8 + (p >> 2 & 1) * 4 + (p & 1) * 2 + (p >> 3) for p in range(16)])
    turned = jnp.arange(16)[:, None] == (origin ^ i)[None, :]
    vectors = jnp.einsum("mp,pkl->kml", turned.astype(bf16), vectors, preferred_element_type=f32)
    small = jnp.concatenate(
        [vectors[:8, :, :48].reshape(8, WIDE), vectors[8].reshape(4, WIDE), jnp.zeros((4, WIDE), f32)]
    )

    packed, normed_one = run_kernel(
        qkv_kernel,
        1,
        info,
        full(tok, small, *first, ahead, ahead_other),
        [(None, (count, 3 * WIDE), bf16), (None, (count, WIDE), bf16)],
        [((3, WIDE, WIDE), bf16)],
        7,
    )

    up_got0, up_got1, down_far, _ = lax.optimization_barrier((up_got0, up_got1, down_far, packed))
    up_wide0, up_wide1 = join(up_line0, up_got0), join(up_line1, up_got1)
    up_got0, up_got1 = swap(up_wide0), hop(up_wide1, BIT_Y)
    down = jnp.stack([down, down_far], axis=1)
    down_far = hop(down, BIT_Z0)

    attended, grad_two, lse = run_kernel(
        attend_kernel,
        2,
        tie(info, up_wide0, up_wide1, down),
        [(rowwise(3 * WIDE), packed), (rowwise(WIDE), cot)],
        [
            (rowwise(WIDE), (count, WIDE), bf16),
            (rowwise(WIDE), (count, WIDE), bf16),
            (rowwise(128), (count, 128), f32),
        ],
        [],
        12,
    )

    up_got0, up_got1, down_far, _ = lax.optimization_barrier((up_got0, up_got1, down_far, lse))
    up = to_other_core((up_wide0, up_got0, up_wide1, up_got1))
    down_line0, down_line1, proj = (join(down[k], down_far[k]) for k in range(3))
    down_got0, down_got1 = hop(down_line0, BIT_Y), swap(down_line1)
    proj = join(proj, hop(proj, BIT_Y))
    proj_other = hop(proj, BIT_C)
    down_wide0, down_wide1 = join(down_line0, down_got0), join(down_line1, down_got1)
    down_got0, down_got1 = swap(down_wide0), hop(down_wide1, BIT_Y)

    parts = (4, 8, PIECE, WIDE)
    middle, normed_two, hidden, active, fc2_own, fc2_away = run_kernel(
        up_kernel,
        4,
        tie(info, down_wide0, down_wide1),
        full(attended, tok, grad_two, small, proj, proj_other, *up),
        [
            (None, (count, WIDE), f32),
            (None, (count, WIDE), bf16),
            (steps((count, WIDE)), (4, count, WIDE), f32),
            (steps((count, WIDE)), (4, count, WIDE), bf16),
            (None, parts, bf16),
            (None, parts, bf16),
        ],
        [((WIDE, WIDE), bf16)] * 3,
        16,
    )

    down_got0, down_got1, _ = lax.optimization_barrier((down_got0, down_got1, normed_two))
    down = to_other_core((down_wide0, down_got0, down_wide1, down_got1))
    fc2_came = hop(fc2_away, BIT_C)
    half = (2, 8, PIECE, WIDE)
    whole_f32 = (None, (count, WIDE), f32)
    whole_bf16 = (None, (count, WIDE), bf16)

    def down_back(line, info, more, outs, scratch):
        block = pl.BlockSpec((1, count, WIDE), lambda t, _: (2 * line + t, 0, 0))
        return run_kernel(
            functools.partial(down_kernel, line),
            2,
            info,
            full(normed_two, grad_two)
            + [(block, hidden), (block, active)]
            + full(small, *up[2 * line : 2 * line + 2], *up[4 + 2 * line : 6 + 2 * line], *down, *more),
            outs + [(None, (16, WIDE), f32), (None, half, bf16), (None, half, bf16)],
            [((WIDE, WIDE), bf16)] * 3 + scratch,
            13,
        )

    branch, grad_normed, bias, fc1_own0, fc1_away0 = down_back(0, info, (), [whole_f32] * 2, [])
    fc2_came, bias = lax.optimization_barrier((fc2_came, bias))
    two = core_sums(fc2_own, fc2_came)
    two_got = first_hops(two)
    one_came0 = hop(fc1_away0, BIT_C)
    output, grad_middle, grad_one, bias, fc1_own1, fc1_away1 = down_back(
        1,
        tie(info, *two),
        (branch, grad_normed, bias, middle, cot),
        [whole_bf16, whole_f32, whole_bf16],
        [((count, WIDE), f32)] * 2,
    )

    def attend_back(group, info, more, outs, scratch):
        def columns(k):
            return pl.BlockSpec((256, 384), lambda r, _, at=2 * k + group: (r, at))

        narrow = (4, 8, PIECE, 384)
        return run_kernel(
            functools.partial(attend_back_kernel, group),
            2,
            info,
            [(columns(k), packed) for k in range(3)]
            + [(rowwise(128), lse), (rowwise(WIDE), attended), (rowwise(WIDE), grad_one)]
            + full(normed_one, *more),
            [(None, (count, 1152), bf16), (None, narrow, bf16), (None, narrow, bf16)] + outs,
            [((2, 2, WIDE, 384), bf16)] + scratch,
            14,
        )

    two_got, one_came0, bias = lax.optimization_barrier((two_got, one_came0, bias))
    two = first_sums(two, two_got)
    two_got, one_came1 = second_hops(two), hop(fc1_away1, BIT_C)
    back0, head_own0, head_away0, proj_full, proj_rest = attend_back(
        0,
        tie(info, *two),
        (proj, proj_other),
        [(None, (WIDE, WIDE), bf16), (None, (WIDE, 384), bf16)],
        [((WIDE, WIDE), f32)],
    )

    two_got, one_came1, _ = lax.optimization_barrier((two_got, one_came1, proj_rest))
    two = second_sums(two, two_got)
    one = tuple(
        plus(own[k], came[k])
        for own, came in ((fc1_own0, one_came0), (fc1_own1, one_came1))
        for k in range(2)
    )
    one_got, two_got, zero_came = first_hops(one), third_hops(two), hop(head_away0, BIT_C)
    back1, head_own1, head_away1 = attend_back(1, tie(info, *two, *one), (proj_full, proj_rest), [], [])

    two_got, one_got, zero_came, _ = lax.optimization_barrier((two_got, one_got, zero_came, back1))
    two, one, zero = third_sums(two, two_got), first_sums(one, one_got), core_sums(head_own0, zero_came)
    last_came = hop(head_away1, BIT_C)
    two_got, one_got, zero_got = fourth_hops(two), second_hops(one), first_hops(zero)

    def tokens_back(r, info, more, alias):
        def row(width):
            return pl.BlockSpec((256, width), lambda _, __: (r, 0))

        return run_kernel(
            functools.partial(tokens_back_kernel, r),
            1,
            info,
            [(row(WIDE), tok), (row(1152), back0), (row(1152), back1), (row(WIDE), grad_middle)]
            + full(bias, small, *first, ahead, ahead_other)
            + more,
            [(row(WIDE), (count, WIDE), f32), (None, (16, WIDE), f32)],
            [((3, WIDE, WIDE), bf16)],
            6,
            alias,
        )

    tokens_grad, bias = tokens_back(0, tie(info, *two, *one, *zero), [], {})

    two_got, one_got, zero_got, last_came, bias = lax.optimization_barrier(
        (two_got, one_got, zero_got, last_came, bias)
    )
    last, two, one, zero = (
        core_sums(head_own1, last_came),
        fourth_sums(two, two_got),
        second_sums(one, one_got),
        first_sums(zero, zero_got),
    )
    last_got, one_got, zero_got, two_other = first_hops(last), third_hops(one), second_hops(zero), swap(two)
    tokens_grad, bias = tokens_back(
        1, tie(info, *last, two, *one, *zero), [(pl.BlockSpec(memory_space=pl.ANY), tokens_grad)], {17: 0}
    )

    last_got, one_got, zero_got, two_other, bias = lax.optimization_barrier(
        (last_got, one_got, zero_got, two_other, bias)
    )
    last, one, zero = first_sums(last, last_got), third_sums(one, one_got), second_sums(zero, zero_got)
    last_got, one_got, zero_got, bias_got = lax.optimization_barrier(
        (
            second_hops(last),
            fourth_hops(one),
            third_hops(zero),
            (hop(bias, BIT_C), hop(bias, BIT_Y), hop(bias, BIT_C | BIT_Y)),
        )
    )
    last, one, zero = second_sums(last, last_got), fourth_sums(one, one_got), third_sums(zero, zero_got)
    bias = (bias + bias_got[0]) + (bias_got[1] + bias_got[2])
    last_got, one_other, zero_got, bias_got = lax.optimization_barrier(
        (third_hops(last), swap(one), fourth_hops(zero), hop(bias, BIT_Z0))
    )
    last, zero, bias = third_sums(last, last_got), fourth_sums(zero, zero_got), bias + bias_got
    last_got, zero_other, bias_got = lax.optimization_barrier(
        (fourth_hops(last), swap(zero), hop(bias, BIT_Z1))
    )
    last, bias = fourth_sums(last, last_got), bias + bias_got
    last_other, bias_got = swap(last), swap(bias)
    bias = bias + bias_got
    qkv_grad, proj_grad, *narrow = run_kernel(
        results_kernel,
        1,
        info,
        full(zero, zero_other, last, last_other, bias),
        [(None, (PIECE, 3 * WIDE), f32), (None, (PIECE, WIDE), f32)]
        + [(None, (48,), f32)] * 8
        + [(None, (192,), f32)],
        [],
        3,
    )
    fc1_grad = jnp.concatenate([place(one, one_other, x, k >> 1, k & 1) for k in range(4)], axis=1)
    fc2_grad = jnp.concatenate([place(two, two_other, x, k >> 1, k & 1) for k in range(4)], axis=0)
    return (
        output.reshape(tokens.shape),
        tokens_grad.reshape(tokens.shape),
        narrow[0],
        narrow[1],
        qkv_grad,
        narrow[2],
        narrow[3],
        proj_grad,
        narrow[4],
        narrow[5],
        narrow[6],
        fc1_grad,
        narrow[8],
        fc2_grad,
        narrow[7],
    )


def solution(mesh):
    in_specs = (
        P(("dp", "fsdp"), None, None),
        P(("dp", "fsdp"), None),
        P(("dp", "fsdp"), None, None),
        P(("dp", "fsdp"), None, None),
        P("fsdp"),
        P("fsdp"),
        P("fsdp", None),
        P("fsdp"),
        P("fsdp"),
        P("fsdp", None),
        P("fsdp"),
        P("fsdp"),
        P("fsdp"),
        P("fsdp", None),
        P("fsdp"),
        P("fsdp", None),
        P("fsdp"),
    )
    out_specs = (
        P(("dp", "fsdp"), None, None),
        P(("dp", "fsdp"), None, None),
        P("fsdp"),
        P("fsdp"),
        P("fsdp", None),
        P("fsdp"),
        P("fsdp"),
        P("fsdp", None),
        P("fsdp"),
        P("fsdp"),
        P("fsdp"),
        P("fsdp", None),
        P("fsdp"),
        P("fsdp", None),
        P("fsdp"),
    )
    fits = mesh.shape["dp"] == 2 and mesh.shape["fsdp"] == 16
    return jax.shard_map(
        fast_device if fits else per_device, mesh=mesh, in_specs=in_specs, out_specs=out_specs, check_vma=False
    )
```

```python
import functools

import jax
import jax.numpy as jnp
from jax import lax
from jax.experimental import pallas as pl
from jax.experimental.pallas import tpu as pltpu
from jax.sharding import PartitionSpec as P

HEADS = 12


EPSILON = 1e-06
KEEP_RATE = 0.9
NEGATIVE = -1e30


def normalize(values, gain, shift):
    center = values - jnp.mean(values, axis=-1, keepdims=True)
    spread = jnp.mean(center * center, axis=-1, keepdims=True)
    return center * lax.rsqrt(spread + EPSILON) * gain + shift


def standardize(values):
    center = values - jnp.mean(values, axis=-1, keepdims=True)
    spread = jnp.mean(center * center, axis=-1, keepdims=True)
    return center * lax.rsqrt(spread + EPSILON)


def affine_low(unit_values, gain, shift):
    return (unit_values * gain.astype(jnp.float32) + shift.astype(jnp.float32)).astype(jnp.bfloat16)


def exact_gelu(values):
    return jax.nn.gelu(values, approximate=False)


def norm_back(values, gain, shift, incoming):
    _, pullback = jax.vjp(normalize, values, gain, shift)
    return pullback(incoming)


def inner_rows(left, right):
    return lax.dot_general(
        left, right, (((0,), (0,)), ((), ())), preferred_element_type=jnp.float32
    )


def times_transpose(left, right):
    return lax.dot_general(
        left, right, (((1,), (1,)), ((), ())), preferred_element_type=jnp.float32
    )


def layout(lengths, keep_mask, length):
    image_ends = jnp.cumsum(lengths, axis=-1, dtype=jnp.int32)
    position = jnp.arange(length, dtype=jnp.int32)
    segment = jnp.sum(
        (position[None, :, None] >= image_ends[:, None, :]).astype(jnp.int32),
        axis=-1,
        dtype=jnp.int32,
    )
    images = jnp.arange(lengths.shape[1], dtype=jnp.int32)
    member = (segment[:, :, None] == images[None, None, :]).astype(jnp.float32)
    keeping = keep_mask.astype(jnp.float32)
    scales = jnp.sum(member[:, :, :, None] * keeping[:, None, :, :], axis=2) / KEEP_RATE
    inside = jnp.sum(member, axis=-1)
    return (segment, scales, inside)


def attention_forward(packed, segment, rowset, length, head_size):
    split_view = packed.reshape(rowset, length, 3, HEADS, head_size)
    queries = split_view[:, :, 0]
    keys_all = split_view[:, :, 1]
    values_all = split_view[:, :, 2]
    scores = jnp.einsum(
        "rqhd,rkhd->rhqk", queries, keys_all, preferred_element_type=jnp.float32
    ) * head_size ** (-0.5)
    matching = segment[:, :, None] == segment[:, None, :]
    scores = jnp.where(matching[:, None], scores, NEGATIVE)
    raised = jnp.exp(scores - jnp.max(scores, axis=-1, keepdims=True))
    weighting = raised / jnp.sum(raised, axis=-1, keepdims=True)
    weighting_low = weighting.astype(jnp.bfloat16)
    attended = jnp.einsum(
        "rhqk,rkhd->rqhd", weighting_low, values_all, preferred_element_type=jnp.float32
    )
    attended = attended.reshape(rowset * length, HEADS * head_size).astype(jnp.bfloat16)
    return (queries, keys_all, values_all, weighting, weighting_low, attended)


def per_device(
    tokens,
    lengths,
    keep_mask,
    cotangent,
    ln1_gain,
    ln1_bias,
    qkv_weight,
    q_bias,
    v_bias,
    proj_weight,
    proj_bias,
    ln2_gain,
    ln2_bias,
    fc1_weight,
    fc1_bias,
    fc2_weight,
    fc2_bias,
):
    rowset, length, features = tokens.shape
    head_size = features // HEADS
    token_count = rowset * length
    segment, scales, inside = layout(lengths, keep_mask, length)
    scale_one = scales[:, :, 0].reshape(token_count, 1)
    scale_two = scales[:, :, 1].reshape(token_count, 1)
    inside_column = inside.reshape(token_count, 1)
    flattened = tokens.reshape(token_count, features).astype(jnp.float32)
    unit_one = standardize(flattened)
    qkv_full, proj_full, gain_one, shift_one, query_bias, value_bias, out_bias = (
        lax.all_gather(qkv_weight, "fsdp", axis=0, tiled=True),
        lax.all_gather(proj_weight, "fsdp", axis=0, tiled=True),
        lax.all_gather(ln1_gain, "fsdp", axis=0, tiled=True),
        lax.all_gather(ln1_bias, "fsdp", axis=0, tiled=True),
        lax.all_gather(q_bias, "fsdp", axis=0, tiled=True),
        lax.all_gather(v_bias, "fsdp", axis=0, tiled=True),
        lax.all_gather(proj_bias, "fsdp", axis=0, tiled=True),
    )
    normed_one = affine_low(unit_one, gain_one, shift_one)
    bias_all = jnp.concatenate(
        [
            query_bias.astype(jnp.float32),
            jnp.zeros((features,), jnp.float32),
            value_bias.astype(jnp.float32),
        ]
    )
    packed = (jnp.dot(normed_one, qkv_full, preferred_element_type=jnp.float32) + bias_all).astype(
        jnp.bfloat16
    )
    _, _, _, _, _, attended = attention_forward(packed, segment, rowset, length, head_size)
    branch_one = jnp.dot(attended, proj_full, preferred_element_type=jnp.float32) + out_bias.astype(
        jnp.float32
    )
    middle = flattened + scale_one * branch_one
    unit_two = standardize(middle)
    up_full, down_full, gain_two, shift_two, up_bias, down_bias = (
        lax.all_gather(fc1_weight, "fsdp", axis=0, tiled=True),
        lax.all_gather(fc2_weight, "fsdp", axis=0, tiled=True),
        lax.all_gather(ln2_gain, "fsdp", axis=0, tiled=True),
        lax.all_gather(ln2_bias, "fsdp", axis=0, tiled=True),
        lax.all_gather(fc1_bias, "fsdp", axis=0, tiled=True),
        lax.all_gather(fc2_bias, "fsdp", axis=0, tiled=True),
    )
    normed_two = affine_low(unit_two, gain_two, shift_two)
    hidden = jnp.dot(normed_two, up_full, preferred_element_type=jnp.float32) + up_bias.astype(
        jnp.float32
    )
    active = exact_gelu(hidden).astype(jnp.bfloat16)
    branch_two = jnp.dot(active, down_full, preferred_element_type=jnp.float32) + down_bias.astype(
        jnp.float32
    )
    output = (
        ((middle + scale_two * branch_two) * inside_column)
        .astype(jnp.bfloat16)
        .reshape(rowset, length, features)
    )
    up_full, down_full = (
        lax.all_gather(fc1_weight, "fsdp", axis=0, tiled=True),
        lax.all_gather(fc2_weight, "fsdp", axis=0, tiled=True),
    )
    gain_two_f = gain_two.astype(jnp.float32)
    shift_two_f = shift_two.astype(jnp.float32)
    grad_out = cotangent.reshape(token_count, features).astype(jnp.float32) * inside_column
    grad_two_low = (grad_out * scale_two).astype(jnp.bfloat16)
    fc2_grad = inner_rows(active, grad_two_low)
    fc2_bias_part = jnp.sum(grad_two_low.astype(jnp.float32), axis=0)
    grad_active = times_transpose(grad_two_low, down_full)
    _, gelu_pull = jax.vjp(exact_gelu, hidden)
    grad_hidden_low = gelu_pull(grad_active)[0].astype(jnp.bfloat16)
    fc1_grad = inner_rows(normed_two, grad_hidden_low)
    fc1_bias_part = jnp.sum(grad_hidden_low.astype(jnp.float32), axis=0)
    grad_normed_two = times_transpose(grad_hidden_low, up_full)
    grad_middle_norm, gain_two_part, shift_two_part = norm_back(
        middle, gain_two_f, shift_two_f, grad_normed_two
    )
    grad_middle = grad_out + grad_middle_norm
    qkv_full, proj_full = (
        lax.all_gather(qkv_weight, "fsdp", axis=0, tiled=True),
        lax.all_gather(proj_weight, "fsdp", axis=0, tiled=True),
    )
    gain_one_f = gain_one.astype(jnp.float32)
    shift_one_f = shift_one.astype(jnp.float32)
    queries, keys_all, values_all, weighting, weighting_low, attended = attention_forward(
        packed, segment, rowset, length, head_size
    )
    grad_one_low = (grad_middle * scale_one).astype(jnp.bfloat16)
    proj_grad = inner_rows(attended, grad_one_low)
    proj_bias_part = jnp.sum(grad_one_low.astype(jnp.float32), axis=0)
    grad_attended_low = times_transpose(grad_one_low, proj_full).astype(jnp.bfloat16)
    grad_attended_low = grad_attended_low.reshape(rowset, length, HEADS, head_size)
    grad_weighting = jnp.einsum(
        "rqhd,rkhd->rhqk", grad_attended_low, values_all, preferred_element_type=jnp.float32
    )
    value_grad = jnp.einsum(
        "rhqk,rqhd->rkhd", weighting_low, grad_attended_low, preferred_element_type=jnp.float32
    )
    row_inner = jnp.sum(grad_weighting * weighting, axis=-1, keepdims=True)
    grad_scores_low = (weighting * (grad_weighting - row_inner)).astype(jnp.bfloat16)
    key_scale = head_size ** (-0.5)
    query_grad = (
        jnp.einsum("rhqk,rkhd->rqhd", grad_scores_low, keys_all, preferred_element_type=jnp.float32)
        * key_scale
    )
    key_grad = (
        jnp.einsum("rhqk,rqhd->rkhd", grad_scores_low, queries, preferred_element_type=jnp.float32)
        * key_scale
    )
    grad_packed_low = (
        jnp.stack([query_grad, key_grad, value_grad], axis=2)
        .reshape(token_count, 3 * features)
        .astype(jnp.bfloat16)
    )
    qkv_grad = inner_rows(normed_one, grad_packed_low)
    column_sums = jnp.sum(grad_packed_low.astype(jnp.float32), axis=0)
    query_bias_part = column_sums[:features]
    value_bias_part = column_sums[2 * features :]
    grad_normed_one = times_transpose(grad_packed_low, qkv_full)
    grad_input_norm, gain_one_part, shift_one_part = norm_back(
        flattened, gain_one_f, shift_one_f, grad_normed_one
    )
    tokens_grad = (grad_middle + grad_input_norm).reshape(rowset, length, features)
    (
        gain_two_grad,
        shift_two_grad,
        fc1_weight_part,
        fc1_bias_shard,
        fc2_weight_part,
        fc2_bias_shard,
    ) = (
        lax.psum_scatter(gain_two_part, "fsdp", scatter_dimension=0, tiled=True),
        lax.psum_scatter(shift_two_part, "fsdp", scatter_dimension=0, tiled=True),
        lax.psum_scatter(fc1_grad, "fsdp", scatter_dimension=0, tiled=True),
        lax.psum_scatter(fc1_bias_part, "fsdp", scatter_dimension=0, tiled=True),
        lax.psum_scatter(fc2_grad, "fsdp", scatter_dimension=0, tiled=True),
        lax.psum_scatter(fc2_bias_part, "fsdp", scatter_dimension=0, tiled=True),
    )
    (
        gain_one_grad,
        shift_one_grad,
        qkv_weight_part,
        query_bias_shard,
        value_bias_shard,
        proj_weight_part,
        proj_bias_shard,
    ) = (
        lax.psum_scatter(gain_one_part, "fsdp", scatter_dimension=0, tiled=True),
        lax.psum_scatter(shift_one_part, "fsdp", scatter_dimension=0, tiled=True),
        lax.psum_scatter(qkv_grad, "fsdp", scatter_dimension=0, tiled=True),
        lax.psum_scatter(query_bias_part, "fsdp", scatter_dimension=0, tiled=True),
        lax.psum_scatter(value_bias_part, "fsdp", scatter_dimension=0, tiled=True),
        lax.psum_scatter(proj_grad, "fsdp", scatter_dimension=0, tiled=True),
        lax.psum_scatter(proj_bias_part, "fsdp", scatter_dimension=0, tiled=True),
    )
    summed = (
        lax.psum(gain_one_grad.astype(jnp.bfloat16), "dp").astype(jnp.float32),
        lax.psum(shift_one_grad.astype(jnp.bfloat16), "dp").astype(jnp.float32),
        lax.psum(qkv_weight_part.astype(jnp.bfloat16), "dp").astype(jnp.float32),
        lax.psum(query_bias_shard.astype(jnp.bfloat16), "dp").astype(jnp.float32),
        lax.psum(value_bias_shard.astype(jnp.bfloat16), "dp").astype(jnp.float32),
        lax.psum(proj_weight_part.astype(jnp.bfloat16), "dp").astype(jnp.float32),
        lax.psum(proj_bias_shard.astype(jnp.bfloat16), "dp").astype(jnp.float32),
        lax.psum(gain_two_grad.astype(jnp.bfloat16), "dp").astype(jnp.float32),
        lax.psum(shift_two_grad.astype(jnp.bfloat16), "dp").astype(jnp.float32),
        lax.psum(fc1_weight_part.astype(jnp.bfloat16), "dp").astype(jnp.float32),
        lax.psum(fc1_bias_shard.astype(jnp.bfloat16), "dp").astype(jnp.float32),
        lax.psum(fc2_weight_part.astype(jnp.bfloat16), "dp").astype(jnp.float32),
        lax.psum(fc2_bias_shard.astype(jnp.bfloat16), "dp").astype(jnp.float32),
    )
    return (
        output,
        tokens_grad,
        summed[0],
        summed[1],
        summed[2],
        summed[3],
        summed[4],
        summed[5],
        summed[6],
        summed[7],
        summed[8],
        summed[9],
        summed[10],
        summed[11],
        summed[12],
    )


BIT_Z1, BIT_Z0, BIT_Y, BIT_C = 8, 4, 2, 1
PIECE = 48
WIDE = 768
SCALE_ON = 1.0 / 0.9
VMEM_BYTES = 56 * 1024 * 1024
f32 = jnp.float32
bf16 = jnp.bfloat16


def hop(array, bit):
    return lax.ppermute(array, "fsdp", [(i, i ^ bit) for i in range(16)])


def swap(array):
    return lax.ppermute(array, "dp", [(0, 1), (1, 0)])


def cross(array):
    axes = ("dp", "fsdp")
    return lax.ppermute(array, axes, [(i, i ^ 16 ^ BIT_C) for i in range(32)])


def join(*arrays):
    return jnp.concatenate(arrays, axis=0)


def tie(array, *before):
    return lax.optimization_barrier((array,) + before)[0]


def to_other_core(own):
    return own + tuple(hop(part, BIT_C) for part in own)


def plus(left, right):
    return (left.astype(f32) + right.astype(f32)).astype(bf16)


def core_sums(own, came):
    return tuple(plus(own[a], came[a]) for a in range(4))


def first_hops(parts):
    return swap(parts[1]), hop(parts[3], BIT_Y)


def together(move, *arrays):
    flat = [array.reshape(-1, PIECE, 384) for array in arrays]
    came, at, out = move(join(*flat)), 0, []
    for array, part in zip(arrays, flat):
        out.append(came[at : at + part.shape[0]].reshape(array.shape))
        at += part.shape[0]
    return out


def hop_y(array):
    return hop(array, BIT_Y)


def first_sums(parts, got):
    return (
        plus(parts[0][:4], got[0][:4]),
        plus(parts[0][4:], got[0][4:]),
        plus(parts[2][:4], got[1][:4]),
        plus(parts[2][4:], got[1][4:]),
    )


def second_hops(parts):
    return hop(parts[1], BIT_Y), swap(parts[3])


def second_sums(parts, got):
    return tuple(
        jnp.stack([plus(parts[0][half], got[0][half]), plus(parts[2][half], got[1][half])])
        for half in (slice(0, 2), slice(2, 4))
    )


def third_hops(parts):
    return (hop(parts[1], BIT_Z0),)


def third_sums(parts, got):
    return plus(parts[0][:, 0], got[0][:, 0]), plus(parts[0][:, 1], got[0][:, 1])


def fourth_hops(parts):
    return (hop(parts[1], BIT_Z1),)


def fourth_sums(parts, got):
    return plus(parts[0], got[0])


def product(left, right, dims):
    return lax.dot_general(left, right, (dims, ((), ())), preferred_element_type=f32)


NN = ((1,), (0,))
NT = ((1,), (1,))
TN = ((0,), (0,))


def slot(line, xr, yr):
    return (xr, yr) if line == 0 else (2 + yr, xr)


def rel_places():
    return [(m, m & 1, (m >> 1) & 1, ((m >> 2) & 1) * 2 + (m >> 3)) for m in range(16)]


def rows_of(i, m):
    return pl.ds(pl.multiple_of((i ^ m) * PIECE, 16), PIECE)


def load_line(store, halves, i, columns=slice(None)):
    for m, c, yr, z in rel_places():
        ref, first = halves[c][yr]
        store[rows_of(i, m), columns] = ref[first + z, 0:PIECE, :]


def save_chunk(value, outs, i, line, xr):
    for m in range(16):
        c, yr, z0r, z1r = m & 1, (m >> 1) & 1, (m >> 2) & 1, (m >> 3) & 1
        array, part = slot(line, xr, yr) if isinstance(xr, int) else (2 + yr, xr)
        row = pl.multiple_of((i ^ m) * PIECE, 16)
        outs[c][array, part * 4 + z0r * 2 + z1r] = value[pl.ds(row, PIECE), :]


def row_facts(info, r):
    first = info[2 + 3 * r]
    second = first + info[3 + 3 * r]
    third = second + info[4 + 3 * r]

    def segment(shape, axis):
        t = lax.broadcasted_iota(jnp.int32, shape, axis)
        return (t >= first).astype(jnp.int32) + (t >= second).astype(jnp.int32) + (t >= third).astype(jnp.int32)

    column = segment((256, 1), 0)

    def scale(branch):
        keeps = [info[8 + 6 * r + 2 * j + branch].astype(f32) * SCALE_ON for j in range(3)]
        return jnp.where(
            column == 0, keeps[0], jnp.where(column == 1, keeps[1], jnp.where(column == 2, keeps[2], 0.0))
        )

    inside = jnp.where(column < 3, 1.0, 0.0).astype(f32)
    return column, segment((1, 256), 1), scale, inside


def unit_of(values):
    center = values - jnp.mean(values, axis=-1, keepdims=True)
    spread = jnp.mean(center * center, axis=-1, keepdims=True)
    root = lax.rsqrt(spread + EPSILON)
    return center * root, root


def unit_back(unit, root, gain, incoming):
    eg = incoming * gain
    return root * (
        eg - jnp.mean(eg, axis=-1, keepdims=True) - unit * jnp.mean(eg * unit, axis=-1, keepdims=True)
    )


def sums(values):
    return jnp.sum(values, axis=0, keepdims=True)


def load_direct(store, own, other, i, spots):
    for m in range(16):
        spot = spots[0] * (m >> 3) + spots[1] * (m >> 2 & 1) + spots[2] * (m >> 1 & 1)
        row = pl.multiple_of((i ^ m) * PIECE, 16)
        store[pl.ds(row, PIECE), :] = (other if m & 1 else own)[spot, 0:PIECE, :]


def prepare_kernel(info, qkv, fc1, fc2, *rest):
    vectors, (lead, *groups) = rest[:9], rest[9:]
    x = info[1]
    at = pl.multiple_of(WIDE + WIDE * x, 128)
    lead[0, 0:48, :] = qkv[:, pl.ds(at + 384, 384)]
    lead[0, 48:96, :] = qkv[:, pl.ds(pl.multiple_of(384 * x, 128), 384)]
    lead[0, 96:144, :] = qkv[:, pl.ds(at, 384)]
    rows = [v[...].astype(f32).reshape(1, -1) for v in vectors]
    rows = rows[:8] + [rows[8][:, 48 * k : 48 * k + 48] for k in range(4)]
    rows = [jnp.pad(row, ((0, 0), (0, 336))) for row in rows]
    lead[0, 144:160, :] = jnp.concatenate(rows + [jnp.zeros((4, 384), f32)]).astype(bf16)
    for half in range(2):

        @pl.when(x == half)
        def _():
            for s in range(2):
                first = 48 * (2 * half + s)
                cuts = [fc1[:, 192 * j + first : 192 * j + first + 48] for j in range(16)]
                groups[s][0] = jnp.concatenate(cuts, axis=1)
                groups[s][1] = fc2[first : first + 48, :]


def load_qkv(weight, refs, i, x):
    for xr in range(2):
        h = x ^ xr
        a = [[(refs[6 * c + xr], 4 * yr) for yr in range(2)] for c in range(2)]
        b = [[(refs[6 * c + 2 + yr], 4 * xr) for yr in range(2)] for c in range(2)]
        q = [[(refs[6 * c + 4 + xr], 4 * yr) for yr in range(2)] for c in range(2)]
        load_line(weight.at[1 + h], a, i, slice(0, 384))
        load_line(weight.at[1 + h], b, i, slice(384, 768))
        load_line(weight.at[0], q, i, pl.ds(pl.multiple_of(384 * h, 128), 384))


def qkv_kernel(info, tok, small, *rest):
    refs, (packed, normed, weight) = rest[:12], rest[12:]
    i, x = info[0], info[1]
    load_qkv(weight, refs, i, x)
    for r in range(2):
        rows = slice(256 * r, 256 * r + 256)
        unit, _ = unit_of(tok[rows, :].astype(f32))
        normed[rows, :] = (unit * small[0:1, :] + small[1:2, :]).astype(bf16)
    for r in range(2):
        rows = slice(256 * r, 256 * r + 256)
        low = normed[rows, :]
        packed[rows, 0:768] = (product(low, weight[0], NN) + small[2:3, :]).astype(bf16)
        packed[rows, 768:1536] = product(low, weight[1], NN).astype(bf16)
        packed[rows, 1536:2304] = (product(low, weight[2], NN) + small[3:4, :]).astype(bf16)


def attend_kernel(info, packed, cot, attended, grad_two, lse, scores, weighting):
    r = pl.program_id(0)
    column, across, scale, inside = row_facts(info, r)
    same = column == across
    lane = lax.broadcasted_iota(jnp.int32, (256, 128), 1)
    kept = jnp.zeros((256, 128), f32)
    for g in range(HEADS):
        query = packed[:, 64 * g : 64 * g + 64] * 0.125
        scores[g] = product(query, packed[:, 768 + 64 * g : 832 + 64 * g], NT)
    for g in range(HEADS):
        masked = jnp.where(same, scores[g], NEGATIVE)
        top = jnp.max(masked, axis=-1, keepdims=True)
        raised = jnp.exp(masked - top)
        total = jnp.sum(raised, axis=-1, keepdims=True)
        weighting[g] = (raised * (1.0 / total)).astype(bf16)
        kept = jnp.where(lane == g, top + jnp.log(total), kept)
    lse[...] = kept
    for h in range(0, HEADS, 2):
        pair = [
            product(weighting[g], packed[:, 1536 + 64 * g : 1600 + 64 * g], NN).astype(bf16)
            for g in (h, h + 1)
        ]
        attended[:, 64 * h : 64 * h + 128] = jnp.concatenate(pair, axis=1)
    grad_two[...] = (cot[...].astype(f32) * inside * scale(1)).astype(bf16)


def hidden_units(block, normed, grad_two, small, branch, grad_normed, bias, weights, scratch):
    active, low = scratch[:2]
    for r in range(2):
        rows = slice(256 * r, 256 * r + 256)
        value = product(normed[rows, :], weights[0], NN) + small[pl.ds(8 + block, 1), :]
        share = 0.5 * (1.0 + lax.erf(value * (0.5**0.5)))
        active[rows, :] = (value * share).astype(bf16)
        slope = share + value * (jnp.exp(-0.5 * value * value) * 0.3989422804014327)
        low[rows, :] = (product(grad_two[rows, :], weights[1], NT) * slope).astype(bf16)
    bias[pl.ds(8 + block, 1), :] = sums(low[...].astype(f32))
    for r in range(2):
        rows = slice(256 * r, 256 * r + 256)
        branch[rows, :] += product(active[rows, :], weights[1], NN)
        grad_normed[rows, :] += product(low[rows, :], weights[0], NT)
    scratch[2][...] = product(normed[...], low[...], TN).astype(bf16)
    scratch[3][...] = product(active[...], grad_two[...], TN).astype(bf16)


def load_units(scratch, refs, i, t):
    for step in range(2):

        @pl.when(t == step)
        def _():
            up = [[(refs[4 * c + step], 4 * yr) for yr in range(2)] for c in range(2)]
            down = [[(refs[4 * c + 2 + yr], 4 * step) for yr in range(2)] for c in range(2)]
            load_line(scratch[4], up, i)
            load_line(scratch[5], down, i)

    return scratch[4][...], scratch[5][...]


def save_units(scratch, own, away, i, t):
    for m, c, yr, z in rel_places():
        for part in range(2):
            here = slice(384 * part, 384 * part + 384)
            (own, away)[c][t, 4 * yr + z, part] = scratch[2][rows_of(i, m), here]
            (own, away)[c][2 + yr, 4 * t + z, part] = scratch[3][rows_of(i, m), here]


def first_units_kernel(info, attended, tok, grad_two, small, proj_own, proj_other, *rest):
    refs, (middle, normed, branch, grad_normed, bias, own, away, proj, *scratch) = rest[:8], rest[8:]
    i, x, t = info[0], info[1], pl.program_id(0)

    @pl.when(t == 0)
    def _():
        load_direct(proj, proj_own, proj_other, i, (2, 4, 1))
        for r in range(2):
            rows = slice(256 * r, 256 * r + 256)
            _, _, scale, _ = row_facts(info, r)
            after = tok[rows, :].astype(f32) + scale(0) * (
                product(attended[rows, :], proj[...], NN) + small[4:5, :]
            )
            middle[rows, :] = after
            unit, _ = unit_of(after)
            normed[rows, :] = (unit * small[5:6, :] + small[6:7, :]).astype(bf16)
        branch[...] = jnp.zeros_like(branch)
        grad_normed[...] = jnp.zeros_like(grad_normed)
        bias[...] = jnp.zeros_like(bias)
        bias[7:8, :] = sums(grad_two[...].astype(f32))

    weights = load_units(scratch, refs, i, t)
    hidden_units(2 * (t ^ x), normed, grad_two, small, branch, grad_normed, bias, weights, scratch)
    save_units(scratch, own, away, i, t)


def second_units_kernel(
    info, normed, grad_two, small, branch_in, grad_normed_in, bias_in, middle, cot, *rest
):
    refs, (result, grad_middle, grad_one, bias, own, away, branch, grad_normed, *scratch) = rest[:8], rest[8:]
    i, x, t = info[0], info[1], pl.program_id(0)

    @pl.when(t == 0)
    def _():
        branch[...] = branch_in[...]
        grad_normed[...] = grad_normed_in[...]
        bias[...] = bias_in[...]

    weights = load_units(scratch, refs, i, t)
    hidden_units(2 * (t ^ x) + 1, normed, grad_two, small, branch, grad_normed, bias, weights, scratch)
    save_units(scratch, own, away, i, t)

    @pl.when(t == 1)
    def _():
        for r in range(2):
            rows = slice(256 * r, 256 * r + 256)
            _, _, scale, inside = row_facts(info, r)
            after = middle[rows, :]
            result[rows, :] = (
                (after + scale(1) * (branch[rows, :] + small[7:8, :])) * inside
            ).astype(bf16)
            unit, root = unit_of(after)
            incoming = grad_normed[rows, :]
            bias[5:6, :] += sums(incoming * unit)
            bias[6:7, :] += sums(incoming)
            total = cot[rows, :].astype(f32) * inside + unit_back(unit, root, small[5:6, :], incoming)
            grad_middle[rows, :] = total
            low_one = (total * scale(0)).astype(bf16)
            grad_one[rows, :] = low_one
            bias[4:5, :] += sums(low_one.astype(f32))


def attend_back_kernel(group, info, queries, keys, values, lse, attended, grad_one, normed, *rest):
    if group == 0:
        proj_own, proj_other, grad_packed, own, away, weight, proj_rest, grad, *heads, total = rest
    else:
        weight, proj_rest, grad_packed, own, away, grad, *heads = rest
    i, x, r = info[0], info[1], pl.program_id(0)
    if group == 0:

        @pl.when(r == 0)
        def _():
            load_direct(weight, proj_own, proj_other, i, (2, 4, 1))
            total[...] = jnp.zeros_like(total)

        total[...] += product(attended[...], grad_one[...], TN)

    column, across, _, _ = row_facts(info, r)
    same = column == across
    grad_attended = product(grad_one[...], weight[384 * group : 384 * group + 384, :], NT).astype(bf16)
    rows = pl.ds(pl.multiple_of(r * 256, 256), 256)
    scores, backs, lows, highs = heads
    queried = [queries[:, 64 * g : 64 * g + 64] * 0.125 for g in range(6)]
    returned = [grad_attended[:, 64 * g : 64 * g + 64] for g in range(6)]
    for g in range(6):
        here = slice(64 * g, 64 * g + 64)
        scores[g] = product(queried[g], keys[:, here], NT)
        backs[g] = product(returned[g], values[:, here], NT)
    for g in range(6):
        head = 6 * group + g
        weighting = jnp.where(same, jnp.exp(scores[g] - lse[:, head : head + 1]), 0.0)
        highs[g] = weighting.astype(bf16)
        share = backs[g] * weighting
        inner = jnp.sum(share, axis=-1, keepdims=True)
        lows[g] = (share - weighting * inner).astype(bf16)
    for h in range(0, 6, 2):
        pairs = ([], [], [])
        for g in (h, h + 1):
            pairs[0].append(product(lows[g], keys[:, 64 * g : 64 * g + 64], NN) * 0.125)
            pairs[1].append(product(lows[g], queried[g], TN))
            pairs[2].append(product(highs[g], returned[g], TN))
        for k in range(3):
            grad_packed[rows, 384 * k + 64 * h : 384 * k + 64 * h + 128] = jnp.concatenate(
                pairs[k], axis=1
            ).astype(bf16)

    @pl.when(r == 1)
    def _():
        low = normed[...]
        grad[1, 0] = product(low, grad_packed[:, 0:384], TN).astype(bf16)
        grad[0, 0] = product(low, grad_packed[:, 384:768], TN).astype(bf16)
        grad[0, 1] = product(low, grad_packed[:, 768:1152], TN).astype(bf16)
        if group == 0:
            grad[1, 1] = total[:, 0:384].astype(bf16)
            proj_rest[...] = total[:, 384:768].astype(bf16)
        else:
            grad[1, 1] = proj_rest[...]
        for line in range(2):
            for xr in range(2):
                save_chunk(grad.at[line, x ^ xr], (own, away), i, line, xr)


def tokens_back_kernel(r, info, tok, back0, back1, grad_middle, bias_in, small, *rest):
    refs, (tokens_grad, bias, weight) = rest[:12], rest[-3:]
    i, x = info[0], info[1]
    load_qkv(weight, refs, i, x)
    bias[...] = bias_in[...]
    for part, back in ((0, back0), (1, back1)):
        columns = slice(384 * part, 384 * part + 384)
        bias[2:3, columns] += sums(back[:, 0:384].astype(f32))
        bias[3:4, columns] += sums(back[:, 768:1152].astype(f32))
    incoming = jnp.zeros((256, WIDE), f32)
    for k in range(3):
        here = slice(384 * k, 384 * k + 384)
        joined = jnp.concatenate([back0[:, here], back1[:, here]], axis=1)
        incoming += product(joined, weight[k], NT)
    unit, root = unit_of(tok[...].astype(f32))
    bias[0:1, :] += sums(incoming * unit)
    bias[1:2, :] += sums(incoming)
    tokens_grad[...] = grad_middle[...] + unit_back(unit, root, small[0:1, :], incoming)


def results_kernel(info, mine0, other0, mine1, other1, bias, qkv, proj, *vectors):
    i, x = info[0], info[1]
    for group, mine, other in ((0, mine0, other0), (1, mine1, other1)):
        for line, half, column in ((1, 0, 0), (0, 0, 768), (0, 1, 1536), (1, 1, None)):
            a, b = mine[line].astype(f32), other[line].astype(f32)
            value = jnp.where(x == half, a, b)
            if column is None:
                proj[:, 384 * group : 384 * group + 384] = value
            else:
                qkv[:, column + 384 * group : column + 384 * group + 384] = value

    def cut(rows, start, width):
        feature = lax.broadcasted_iota(jnp.int32, (WIDE, width), 0)
        lane = lax.broadcasted_iota(jnp.int32, (WIDE, width), 1)
        chosen = (feature == lane + start).astype(f32)
        return lax.dot_general(
            rows, chosen, (NN, ((), ())), precision=lax.Precision.HIGHEST, preferred_element_type=f32
        )

    narrow = cut(bias[...], i * 48, 128)
    for k in range(8):
        vectors[k][...] = narrow[k, 0:48]
    broad = jnp.concatenate([narrow[8 + k : 9 + k, 0:48] for k in range(4)], axis=1)
    vectors[8][...] = broad[0]


def units_results_kernel(info, mine0, other0, mine1, other1, fc1, fc2):
    x = info[1]
    blocks = []
    for half in range(2):
        for mine, other in ((mine0, other0), (mine1, other1)):
            pieces = [
                jnp.concatenate(
                    [jnp.where(x == half, mine[k, p].astype(f32), other[k, p].astype(f32)) for p in range(2)],
                    axis=1,
                )
                for k in range(2)
            ]
            fc2[48 * len(blocks) : 48 * len(blocks) + 48, :] = pieces[1]
            blocks.append(pieces[0])
    for j in range(0, 16, 2):
        cuts = [b[:, 48 * k : 48 * k + 48] for k in (j, j + 1) for b in blocks]
        fc1[:, 192 * j : 192 * j + 384] = jnp.concatenate(cuts, axis=1)


def whole(shape):
    return pl.BlockSpec(shape, lambda *_: (0,) * len(shape))


def rowwise(width):
    return pl.BlockSpec((256, width), lambda r, info: (r, 0))


def run_kernel(kernel, grid, info, operands, outs, scratch, microseconds, alias=None):
    return pl.pallas_call(
        kernel,
        grid_spec=pltpu.PrefetchScalarGridSpec(
            num_scalar_prefetch=1,
            grid=(grid,),
            in_specs=[spec or whole(array.shape) for spec, array in operands],
            out_specs=[spec or whole(shape) for spec, shape, _ in outs],
            scratch_shapes=[pltpu.VMEM(shape, dtype) for shape, dtype in scratch],
        ),
        out_shape=[jax.ShapeDtypeStruct(shape, dtype) for _, shape, dtype in outs],
        input_output_aliases=alias or {},
        compiler_params=pltpu.CompilerParams(
            dimension_semantics=("arbitrary",), vmem_limit_bytes=VMEM_BYTES
        ),
        cost_estimate=pl.CostEstimate(
            flops=int(microseconds * 1.15e9), bytes_accessed=1 << 20, transcendentals=0
        ),
    )(info, *[array for _, array in operands])


def fast_device(
    tokens,
    lengths,
    keep_mask,
    cotangent,
    ln1_gain,
    ln1_bias,
    qkv_weight,
    q_bias,
    v_bias,
    proj_weight,
    proj_bias,
    ln2_gain,
    ln2_bias,
    fc1_weight,
    fc1_bias,
    fc2_weight,
    fc2_bias,
):
    count = tokens.shape[0] * tokens.shape[1]
    i = lax.axis_index("fsdp")
    x = lax.axis_index("dp")
    info = jnp.concatenate(
        [jnp.stack([i, x]).astype(jnp.int32), lengths.reshape(-1), keep_mask.reshape(-1)]
    )
    tok = tokens.reshape(count, WIDE)
    cot = cotangent.reshape(count, WIDE)

    def full(*arrays):
        return [(None, array) for array in arrays]

    vectors = (ln1_gain, ln1_bias, q_bias, v_bias, proj_bias, ln2_gain, ln2_bias, fc2_bias, fc1_bias)
    lead, units0, units1 = run_kernel(
        prepare_kernel,
        1,
        jnp.stack([i, x]),
        full(qkv_weight, fc1_weight, fc2_weight, *vectors),
        [(None, (1, 160, 384), bf16), (None, (2, PIECE, WIDE), bf16), (None, (2, PIECE, WIDE), bf16)],
        [],
        2,
    )

    proj = tie(proj_weight[None], lead)
    proj = join(proj, hop(proj, BIT_Y))

    pair = join(lead, hop(lead, BIT_Z1))
    far = hop(pair, BIT_Z0)
    line_b, line_q, line_a = (join(pair[:, k], far[:, k]) for k in (slice(0, 48), slice(48, 96), slice(96, 160)))
    line_a, line_b, line_q, units0 = lax.optimization_barrier((line_a, line_b, line_q, units0))
    got_a, got_b, got_q = hop(line_a, BIT_Y), swap(line_b), hop(line_q, BIT_Y)
    units_far = hop(units0, BIT_Z1)
    got_a, got_b = lax.optimization_barrier((got_a, got_b))
    wide_a, wide_b = join(line_a, got_a), join(line_b, got_b)
    got_a, got_b = swap(wide_a[:, :PIECE]), hop(wide_b, BIT_Y)
    wide_q = join(line_q, got_q)
    got_q = swap(wide_q)
    units_far = tie(units_far, wide_a, wide_b)
    units0 = jnp.stack([units0, units_far], axis=1)
    units_far = hop(units0, BIT_Z0)
    units1 = tie(units1, wide_a, wide_b, units0)
    next_far = hop(units1, BIT_Z1)
    got_a, got_b, got_q, units_far, next_far, proj = lax.optimization_barrier(
        (got_a, got_b, got_q, units_far, next_far, proj)
    )
    first = to_other_core((wide_a, got_a, wide_b, got_b, wide_q, got_q))

    units_line = join(units0[0], units_far[0]), join(units0[1], units_far[1])
    units_got = hop(units_line[0], BIT_Y), swap(units_line[1])
    units1 = jnp.stack([units1, next_far], axis=1)
    next_far = hop(units1, BIT_Z0)
    proj_far = hop(proj, BIT_Z1)

    vectors = jnp.concatenate([first[k][:, PIECE : PIECE + 12, :PIECE] for k in (0, 6)])
    origin = jnp.array([(p & 1) * 8 + (p >> 1 & 1) * 4 + (p >> 2 & 1) * 2 + (p >> 3) for p in range(16)])
    turned = jnp.arange(16)[:, None] == (origin ^ i)[None, :]
    vectors = jnp.einsum("mp,pkl->kml", turned.astype(bf16), vectors, preferred_element_type=f32)
    small = jnp.concatenate([vectors.reshape(12, WIDE), jnp.zeros((4, WIDE), f32)])

    packed, normed_one = run_kernel(
        qkv_kernel,
        1,
        info,
        full(tok, small, *first),
        [(None, (count, 3 * WIDE), bf16), (None, (count, WIDE), bf16)],
        [((3, WIDE, WIDE), bf16)],
        7,
    )

    units_got, next_far, proj_far, _ = lax.optimization_barrier((units_got, next_far, proj_far, packed))
    units_wide = tuple(join(line, got) for line, got in zip(units_line, units_got))
    units_got = swap(units_wide[0]), hop(units_wide[1], BIT_Y)
    next_line = tuple(join(units1[k], next_far[k]) for k in range(2))
    next_got = hop(next_line[0], BIT_Y), swap(next_line[1])
    proj = join(proj, proj_far)
    proj_far = hop(proj, BIT_Z0)

    attended, grad_two, lse = run_kernel(
        attend_kernel,
        2,
        tie(info, *units_wide, *next_line, proj),
        [(rowwise(3 * WIDE), packed), (rowwise(WIDE), cot)],
        [
            (rowwise(WIDE), (count, WIDE), bf16),
            (rowwise(WIDE), (count, WIDE), bf16),
            (rowwise(128), (count, 128), f32),
        ],
        [((HEADS, 256, 256), f32), ((HEADS, 256, 256), bf16)],
        10,
    )

    units_got, next_got, proj_far, _ = lax.optimization_barrier((units_got, next_got, proj_far, lse))
    proj = join(proj, proj_far)
    proj_other = hop(proj, BIT_C)
    units = to_other_core((units_wide[0], units_got[0], units_wide[1], units_got[1]))
    next_wide = tuple(join(line, got) for line, got in zip(next_line, next_got))
    next_got = swap(next_wide[0]), hop(next_wide[1], BIT_Y)

    wide_f32 = (None, (count, WIDE), f32)
    wide_bf16 = (None, (count, WIDE), bf16)
    vectors_f32 = (None, (16, WIDE), f32)
    parts = (None, (4, 8, 2, PIECE, 384), bf16)
    unit_scratch = [((count, WIDE), bf16)] * 2 + [((WIDE, WIDE), bf16)] * 4
    middle, normed_two, branch, grad_normed, bias, units_own, units_away = run_kernel(
        first_units_kernel,
        2,
        tie(info, *next_wide),
        full(attended, tok, grad_two, small, proj, proj_other, *units),
        [wide_f32, wide_bf16, wide_f32, wide_f32, vectors_f32, parts, parts],
        [((WIDE, WIDE), bf16)] + unit_scratch,
        16,
    )
    next_got, bias, units_away = lax.optimization_barrier((next_got, bias, units_away))
    units = to_other_core((next_wide[0], next_got[0], next_wide[1], next_got[1]))
    two = core_sums(units_own, hop(units_away, BIT_C))
    two_got = first_hops(two)
    output, grad_middle, grad_one, bias, units_own, units_away = run_kernel(
        second_units_kernel,
        2,
        tie(info, *two),
        full(normed_two, grad_two, small, branch, grad_normed, bias, middle, cot, *units),
        [wide_bf16, wide_f32, wide_bf16, vectors_f32, parts, parts],
        [((count, WIDE), f32)] * 2 + unit_scratch,
        18,
    )

    def attend_back(group, info, more, outs, scratch):
        def columns(k):
            return pl.BlockSpec((256, 384), lambda r, _, at=2 * k + group: (r, at))

        narrow = (4, 8, PIECE, 384)
        return run_kernel(
            functools.partial(attend_back_kernel, group),
            2,
            info,
            [(columns(k), packed) for k in range(3)]
            + [(rowwise(128), lse), (rowwise(WIDE), attended), (rowwise(WIDE), grad_one)]
            + full(normed_one, *more),
            [(None, (count, 1152), bf16), (None, narrow, bf16), (None, narrow, bf16)] + outs,
            [((2, 2, WIDE, 384), bf16)]
            + [((6, 256, 256), f32)] * 2
            + [((6, 256, 256), bf16)] * 2
            + scratch,
            14,
        )

    two_got, bias, units_away = lax.optimization_barrier((two_got, bias, units_away))
    two = first_sums(two, two_got)
    two_got, one_came = second_hops(two), hop(units_away, BIT_C)
    back0, head_own0, head_away0, proj_full, proj_rest = attend_back(
        0,
        tie(info, *two),
        (proj, proj_other),
        [(None, (WIDE, WIDE), bf16), (None, (WIDE, 384), bf16)],
        [((WIDE, WIDE), f32)],
    )

    two_got, one_came, proj_rest, head_away0 = lax.optimization_barrier(
        (two_got, one_came, proj_rest, head_away0)
    )
    two = second_sums(two, two_got)
    one = core_sums(units_own, one_came)
    one_got, two_got, zero_came = first_hops(one), third_hops(two), hop(head_away0, BIT_C)
    back1, head_own1, head_away1 = attend_back(1, tie(info, *two, *one), (proj_full, proj_rest), [], [])

    two_got, one_got, zero_came, head_away1 = lax.optimization_barrier(
        (two_got, one_got, zero_came, head_away1)
    )
    two, one, zero = third_sums(two, two_got), first_sums(one, one_got), core_sums(head_own0, zero_came)
    last_came = hop(head_away1, BIT_C)
    two_got = fourth_hops(two)
    got_x, got_y = together(swap, one[3], zero[1]), together(hop_y, one[1], zero[3])
    one_got, zero_got = (got_y[0], got_x[0]), (got_x[1], got_y[1])

    def tokens_back(r, info, more, alias):
        def row(width):
            return pl.BlockSpec((256, width), lambda _, __: (r, 0))

        return run_kernel(
            functools.partial(tokens_back_kernel, r),
            1,
            info,
            [(row(WIDE), tok), (row(1152), back0), (row(1152), back1), (row(WIDE), grad_middle)]
            + full(bias, small, *first)
            + more,
            [(row(WIDE), (count, WIDE), f32), (None, (16, WIDE), f32)],
            [((3, WIDE, WIDE), bf16)],
            6,
            alias,
        )

    tokens_grad, bias = tokens_back(0, tie(info, *two, *one, *zero), [], {})

    two_got, one_got, zero_got, last_came, bias = lax.optimization_barrier(
        (two_got, one_got, zero_got, last_came, bias)
    )
    last, two, one, zero = (
        core_sums(head_own1, last_came),
        fourth_sums(two, two_got),
        second_sums(one, one_got),
        first_sums(zero, zero_got),
    )
    one_got = third_hops(one)
    got_x, got_y = together(swap, last[1], zero[3], two), together(hop_y, last[3], zero[1])
    last_got, zero_got, two_other = (got_x[0], got_y[0]), (got_y[1], got_x[1]), got_x[2]
    tokens_grad, bias = tokens_back(
        1, tie(info, *last, two, *one, *zero), [(pl.BlockSpec(memory_space=pl.ANY), tokens_grad)], {19: 0}
    )

    last_got, one_got, zero_got, two_other, bias = lax.optimization_barrier(
        (last_got, one_got, zero_got, two_other, bias)
    )
    last, one, zero = first_sums(last, last_got), third_sums(one, one_got), second_sums(zero, zero_got)
    last_got, one_got, zero_got, bias_got = lax.optimization_barrier(
        (
            second_hops(last),
            fourth_hops(one),
            third_hops(zero),
            hop(bias, BIT_Y),
        )
    )
    last, one, zero = second_sums(last, last_got), fourth_sums(one, one_got), third_sums(zero, zero_got)
    bias = bias + bias_got
    last_got, one_other, zero_got, bias_got = lax.optimization_barrier(
        (third_hops(last), swap(one), fourth_hops(zero), hop(bias, BIT_Z0))
    )
    last, zero, bias = third_sums(last, last_got), fourth_sums(zero, zero_got), bias + bias_got
    last_got, zero_other, bias_got = lax.optimization_barrier(
        (fourth_hops(last), swap(zero), hop(bias, BIT_Z1))
    )
    fc1_grad, fc2_grad = run_kernel(
        units_results_kernel,
        1,
        info,
        full(two, two_other, one, one_other),
        [(None, (PIECE, 4 * WIDE), f32), (None, (4 * PIECE, WIDE), f32)],
        [],
        3,
    )
    last, bias = fourth_sums(last, last_got), bias + bias_got
    last_other, bias_got = swap(last), (swap(bias), hop(bias, BIT_C), cross(bias))
    bias = (bias + bias_got[0]) + (bias_got[1] + bias_got[2])
    qkv_grad, proj_grad, *narrow = run_kernel(
        results_kernel,
        1,
        info,
        full(zero, zero_other, last, last_other, bias),
        [(None, (PIECE, 3 * WIDE), f32), (None, (PIECE, WIDE), f32)]
        + [(None, (48,), f32)] * 8
        + [(None, (192,), f32)],
        [],
        3,
    )
    return (
        output.reshape(tokens.shape),
        tokens_grad.reshape(tokens.shape),
        narrow[0],
        narrow[1],
        qkv_grad,
        narrow[2],
        narrow[3],
        proj_grad,
        narrow[4],
        narrow[5],
        narrow[6],
        fc1_grad,
        narrow[8],
        fc2_grad,
        narrow[7],
    )


def solution(mesh):
    in_specs = (
        P(("dp", "fsdp"), None, None),
        P(("dp", "fsdp"), None),
        P(("dp", "fsdp"), None, None),
        P(("dp", "fsdp"), None, None),
        P("fsdp"),
        P("fsdp"),
        P("fsdp", None),
        P("fsdp"),
        P("fsdp"),
        P("fsdp", None),
        P("fsdp"),
        P("fsdp"),
        P("fsdp"),
        P("fsdp", None),
        P("fsdp"),
        P("fsdp", None),
        P("fsdp"),
    )
    out_specs = (
        P(("dp", "fsdp"), None, None),
        P(("dp", "fsdp"), None, None),
        P("fsdp"),
        P("fsdp"),
        P("fsdp", None),
        P("fsdp"),
        P("fsdp"),
        P("fsdp", None),
        P("fsdp"),
        P("fsdp"),
        P("fsdp"),
        P("fsdp", None),
        P("fsdp"),
        P("fsdp", None),
        P("fsdp"),
    )
    fits = mesh.shape["dp"] == 2 and mesh.shape["fsdp"] == 16
    return jax.shard_map(
        fast_device if fits else per_device, mesh=mesh, in_specs=in_specs, out_specs=out_specs, check_vma=False
    )
```

```python
import functools

import jax
import jax.numpy as jnp
from jax import lax
from jax.experimental import pallas as pl
from jax.experimental.pallas import tpu as pltpu
from jax.sharding import PartitionSpec as P

HEADS = 12


EPSILON = 1e-06
KEEP_RATE = 0.9
NEGATIVE = -1e30


def normalize(values, gain, shift):
    center = values - jnp.mean(values, axis=-1, keepdims=True)
    spread = jnp.mean(center * center, axis=-1, keepdims=True)
    return center * lax.rsqrt(spread + EPSILON) * gain + shift


def standardize(values):
    center = values - jnp.mean(values, axis=-1, keepdims=True)
    spread = jnp.mean(center * center, axis=-1, keepdims=True)
    return center * lax.rsqrt(spread + EPSILON)


def affine_low(unit_values, gain, shift):
    return (unit_values * gain.astype(jnp.float32) + shift.astype(jnp.float32)).astype(jnp.bfloat16)


def exact_gelu(values):
    return jax.nn.gelu(values, approximate=False)


def norm_back(values, gain, shift, incoming):
    _, pullback = jax.vjp(normalize, values, gain, shift)
    return pullback(incoming)


def inner_rows(left, right):
    return lax.dot_general(
        left, right, (((0,), (0,)), ((), ())), preferred_element_type=jnp.float32
    )


def times_transpose(left, right):
    return lax.dot_general(
        left, right, (((1,), (1,)), ((), ())), preferred_element_type=jnp.float32
    )


def layout(lengths, keep_mask, length):
    image_ends = jnp.cumsum(lengths, axis=-1, dtype=jnp.int32)
    position = jnp.arange(length, dtype=jnp.int32)
    segment = jnp.sum(
        (position[None, :, None] >= image_ends[:, None, :]).astype(jnp.int32),
        axis=-1,
        dtype=jnp.int32,
    )
    images = jnp.arange(lengths.shape[1], dtype=jnp.int32)
    member = (segment[:, :, None] == images[None, None, :]).astype(jnp.float32)
    keeping = keep_mask.astype(jnp.float32)
    scales = jnp.sum(member[:, :, :, None] * keeping[:, None, :, :], axis=2) / KEEP_RATE
    inside = jnp.sum(member, axis=-1)
    return (segment, scales, inside)


def attention_forward(packed, segment, rowset, length, head_size):
    split_view = packed.reshape(rowset, length, 3, HEADS, head_size)
    queries = split_view[:, :, 0]
    keys_all = split_view[:, :, 1]
    values_all = split_view[:, :, 2]
    scores = jnp.einsum(
        "rqhd,rkhd->rhqk", queries, keys_all, preferred_element_type=jnp.float32
    ) * head_size ** (-0.5)
    matching = segment[:, :, None] == segment[:, None, :]
    scores = jnp.where(matching[:, None], scores, NEGATIVE)
    raised = jnp.exp(scores - jnp.max(scores, axis=-1, keepdims=True))
    weighting = raised / jnp.sum(raised, axis=-1, keepdims=True)
    weighting_low = weighting.astype(jnp.bfloat16)
    attended = jnp.einsum(
        "rhqk,rkhd->rqhd", weighting_low, values_all, preferred_element_type=jnp.float32
    )
    attended = attended.reshape(rowset * length, HEADS * head_size).astype(jnp.bfloat16)
    return (queries, keys_all, values_all, weighting, weighting_low, attended)


def per_device(
    tokens,
    lengths,
    keep_mask,
    cotangent,
    ln1_gain,
    ln1_bias,
    qkv_weight,
    q_bias,
    v_bias,
    proj_weight,
    proj_bias,
    ln2_gain,
    ln2_bias,
    fc1_weight,
    fc1_bias,
    fc2_weight,
    fc2_bias,
):
    rowset, length, features = tokens.shape
    head_size = features // HEADS
    token_count = rowset * length
    segment, scales, inside = layout(lengths, keep_mask, length)
    scale_one = scales[:, :, 0].reshape(token_count, 1)
    scale_two = scales[:, :, 1].reshape(token_count, 1)
    inside_column = inside.reshape(token_count, 1)
    flattened = tokens.reshape(token_count, features).astype(jnp.float32)
    unit_one = standardize(flattened)
    qkv_full, proj_full, gain_one, shift_one, query_bias, value_bias, out_bias = (
        lax.all_gather(qkv_weight, "fsdp", axis=0, tiled=True),
        lax.all_gather(proj_weight, "fsdp", axis=0, tiled=True),
        lax.all_gather(ln1_gain, "fsdp", axis=0, tiled=True),
        lax.all_gather(ln1_bias, "fsdp", axis=0, tiled=True),
        lax.all_gather(q_bias, "fsdp", axis=0, tiled=True),
        lax.all_gather(v_bias, "fsdp", axis=0, tiled=True),
        lax.all_gather(proj_bias, "fsdp", axis=0, tiled=True),
    )
    normed_one = affine_low(unit_one, gain_one, shift_one)
    bias_all = jnp.concatenate(
        [
            query_bias.astype(jnp.float32),
            jnp.zeros((features,), jnp.float32),
            value_bias.astype(jnp.float32),
        ]
    )
    packed = (jnp.dot(normed_one, qkv_full, preferred_element_type=jnp.float32) + bias_all).astype(
        jnp.bfloat16
    )
    _, _, _, _, _, attended = attention_forward(packed, segment, rowset, length, head_size)
    branch_one = jnp.dot(attended, proj_full, preferred_element_type=jnp.float32) + out_bias.astype(
        jnp.float32
    )
    middle = flattened + scale_one * branch_one
    unit_two = standardize(middle)
    up_full, down_full, gain_two, shift_two, up_bias, down_bias = (
        lax.all_gather(fc1_weight, "fsdp", axis=0, tiled=True),
        lax.all_gather(fc2_weight, "fsdp", axis=0, tiled=True),
        lax.all_gather(ln2_gain, "fsdp", axis=0, tiled=True),
        lax.all_gather(ln2_bias, "fsdp", axis=0, tiled=True),
        lax.all_gather(fc1_bias, "fsdp", axis=0, tiled=True),
        lax.all_gather(fc2_bias, "fsdp", axis=0, tiled=True),
    )
    normed_two = affine_low(unit_two, gain_two, shift_two)
    hidden = jnp.dot(normed_two, up_full, preferred_element_type=jnp.float32) + up_bias.astype(
        jnp.float32
    )
    active = exact_gelu(hidden).astype(jnp.bfloat16)
    branch_two = jnp.dot(active, down_full, preferred_element_type=jnp.float32) + down_bias.astype(
        jnp.float32
    )
    output = (
        ((middle + scale_two * branch_two) * inside_column)
        .astype(jnp.bfloat16)
        .reshape(rowset, length, features)
    )
    up_full, down_full = (
        lax.all_gather(fc1_weight, "fsdp", axis=0, tiled=True),
        lax.all_gather(fc2_weight, "fsdp", axis=0, tiled=True),
    )
    gain_two_f = gain_two.astype(jnp.float32)
    shift_two_f = shift_two.astype(jnp.float32)
    grad_out = cotangent.reshape(token_count, features).astype(jnp.float32) * inside_column
    grad_two_low = (grad_out * scale_two).astype(jnp.bfloat16)
    fc2_grad = inner_rows(active, grad_two_low)
    fc2_bias_part = jnp.sum(grad_two_low.astype(jnp.float32), axis=0)
    grad_active = times_transpose(grad_two_low, down_full)
    _, gelu_pull = jax.vjp(exact_gelu, hidden)
    grad_hidden_low = gelu_pull(grad_active)[0].astype(jnp.bfloat16)
    fc1_grad = inner_rows(normed_two, grad_hidden_low)
    fc1_bias_part = jnp.sum(grad_hidden_low.astype(jnp.float32), axis=0)
    grad_normed_two = times_transpose(grad_hidden_low, up_full)
    grad_middle_norm, gain_two_part, shift_two_part = norm_back(
        middle, gain_two_f, shift_two_f, grad_normed_two
    )
    grad_middle = grad_out + grad_middle_norm
    qkv_full, proj_full = (
        lax.all_gather(qkv_weight, "fsdp", axis=0, tiled=True),
        lax.all_gather(proj_weight, "fsdp", axis=0, tiled=True),
    )
    gain_one_f = gain_one.astype(jnp.float32)
    shift_one_f = shift_one.astype(jnp.float32)
    queries, keys_all, values_all, weighting, weighting_low, attended = attention_forward(
        packed, segment, rowset, length, head_size
    )
    grad_one_low = (grad_middle * scale_one).astype(jnp.bfloat16)
    proj_grad = inner_rows(attended, grad_one_low)
    proj_bias_part = jnp.sum(grad_one_low.astype(jnp.float32), axis=0)
    grad_attended_low = times_transpose(grad_one_low, proj_full).astype(jnp.bfloat16)
    grad_attended_low = grad_attended_low.reshape(rowset, length, HEADS, head_size)
    grad_weighting = jnp.einsum(
        "rqhd,rkhd->rhqk", grad_attended_low, values_all, preferred_element_type=jnp.float32
    )
    value_grad = jnp.einsum(
        "rhqk,rqhd->rkhd", weighting_low, grad_attended_low, preferred_element_type=jnp.float32
    )
    row_inner = jnp.sum(grad_weighting * weighting, axis=-1, keepdims=True)
    grad_scores_low = (weighting * (grad_weighting - row_inner)).astype(jnp.bfloat16)
    key_scale = head_size ** (-0.5)
    query_grad = (
        jnp.einsum("rhqk,rkhd->rqhd", grad_scores_low, keys_all, preferred_element_type=jnp.float32)
        * key_scale
    )
    key_grad = (
        jnp.einsum("rhqk,rqhd->rkhd", grad_scores_low, queries, preferred_element_type=jnp.float32)
        * key_scale
    )
    grad_packed_low = (
        jnp.stack([query_grad, key_grad, value_grad], axis=2)
        .reshape(token_count, 3 * features)
        .astype(jnp.bfloat16)
    )
    qkv_grad = inner_rows(normed_one, grad_packed_low)
    column_sums = jnp.sum(grad_packed_low.astype(jnp.float32), axis=0)
    query_bias_part = column_sums[:features]
    value_bias_part = column_sums[2 * features :]
    grad_normed_one = times_transpose(grad_packed_low, qkv_full)
    grad_input_norm, gain_one_part, shift_one_part = norm_back(
        flattened, gain_one_f, shift_one_f, grad_normed_one
    )
    tokens_grad = (grad_middle + grad_input_norm).reshape(rowset, length, features)
    (
        gain_two_grad,
        shift_two_grad,
        fc1_weight_part,
        fc1_bias_shard,
        fc2_weight_part,
        fc2_bias_shard,
    ) = (
        lax.psum_scatter(gain_two_part, "fsdp", scatter_dimension=0, tiled=True),
        lax.psum_scatter(shift_two_part, "fsdp", scatter_dimension=0, tiled=True),
        lax.psum_scatter(fc1_grad, "fsdp", scatter_dimension=0, tiled=True),
        lax.psum_scatter(fc1_bias_part, "fsdp", scatter_dimension=0, tiled=True),
        lax.psum_scatter(fc2_grad, "fsdp", scatter_dimension=0, tiled=True),
        lax.psum_scatter(fc2_bias_part, "fsdp", scatter_dimension=0, tiled=True),
    )
    (
        gain_one_grad,
        shift_one_grad,
        qkv_weight_part,
        query_bias_shard,
        value_bias_shard,
        proj_weight_part,
        proj_bias_shard,
    ) = (
        lax.psum_scatter(gain_one_part, "fsdp", scatter_dimension=0, tiled=True),
        lax.psum_scatter(shift_one_part, "fsdp", scatter_dimension=0, tiled=True),
        lax.psum_scatter(qkv_grad, "fsdp", scatter_dimension=0, tiled=True),
        lax.psum_scatter(query_bias_part, "fsdp", scatter_dimension=0, tiled=True),
        lax.psum_scatter(value_bias_part, "fsdp", scatter_dimension=0, tiled=True),
        lax.psum_scatter(proj_grad, "fsdp", scatter_dimension=0, tiled=True),
        lax.psum_scatter(proj_bias_part, "fsdp", scatter_dimension=0, tiled=True),
    )
    summed = (
        lax.psum(gain_one_grad.astype(jnp.bfloat16), "dp").astype(jnp.float32),
        lax.psum(shift_one_grad.astype(jnp.bfloat16), "dp").astype(jnp.float32),
        lax.psum(qkv_weight_part.astype(jnp.bfloat16), "dp").astype(jnp.float32),
        lax.psum(query_bias_shard.astype(jnp.bfloat16), "dp").astype(jnp.float32),
        lax.psum(value_bias_shard.astype(jnp.bfloat16), "dp").astype(jnp.float32),
        lax.psum(proj_weight_part.astype(jnp.bfloat16), "dp").astype(jnp.float32),
        lax.psum(proj_bias_shard.astype(jnp.bfloat16), "dp").astype(jnp.float32),
        lax.psum(gain_two_grad.astype(jnp.bfloat16), "dp").astype(jnp.float32),
        lax.psum(shift_two_grad.astype(jnp.bfloat16), "dp").astype(jnp.float32),
        lax.psum(fc1_weight_part.astype(jnp.bfloat16), "dp").astype(jnp.float32),
        lax.psum(fc1_bias_shard.astype(jnp.bfloat16), "dp").astype(jnp.float32),
        lax.psum(fc2_weight_part.astype(jnp.bfloat16), "dp").astype(jnp.float32),
        lax.psum(fc2_bias_shard.astype(jnp.bfloat16), "dp").astype(jnp.float32),
    )
    return (
        output,
        tokens_grad,
        summed[0],
        summed[1],
        summed[2],
        summed[3],
        summed[4],
        summed[5],
        summed[6],
        summed[7],
        summed[8],
        summed[9],
        summed[10],
        summed[11],
        summed[12],
    )


BIT_Z1, BIT_Z0, BIT_Y, BIT_C = 8, 4, 2, 1
PIECE = 48
WIDE = 768
SCALE_ON = 1.0 / 0.9
MIB = 1024 * 1024
f32 = jnp.float32
bf16 = jnp.bfloat16


def hop(array, bit):
    return lax.ppermute(array, "fsdp", [(i, i ^ bit) for i in range(16)])


def swap(array):
    return lax.ppermute(array, "dp", [(0, 1), (1, 0)])


def cross(array):
    axes = ("dp", "fsdp")
    return lax.ppermute(array, axes, [(i, i ^ 16 ^ BIT_C) for i in range(32)])


def join(*arrays):
    return jnp.concatenate(arrays, axis=0)


def tie(array, *before):
    return lax.optimization_barrier((array,) + before)[0]


def to_other_core(own):
    return own + tuple(hop(part, BIT_C) for part in own)


def plus(left, right):
    return (left.astype(f32) + right.astype(f32)).astype(bf16)


def core_sums(own, came):
    return tuple(plus(own[a], came[a]) for a in range(4))


def first_hops(parts):
    return swap(parts[1]), hop(parts[3], BIT_Y)


def together(move, *arrays):
    flat = [array.reshape(-1, PIECE, 384) for array in arrays]
    came, at, out = move(join(*flat)), 0, []
    for array, part in zip(arrays, flat):
        out.append(came[at : at + part.shape[0]].reshape(array.shape))
        at += part.shape[0]
    return out


def hop_y(array):
    return hop(array, BIT_Y)


def hop_z0(array):
    return hop(array, BIT_Z0)


def hop_z1(array):
    return hop(array, BIT_Z1)


def first_sums(parts, got):
    return (
        plus(parts[0][:4], got[0][:4]),
        plus(parts[0][4:], got[0][4:]),
        plus(parts[2][:4], got[1][:4]),
        plus(parts[2][4:], got[1][4:]),
    )


def second_hops(parts):
    return hop(parts[1], BIT_Y), swap(parts[3])


def second_sums(parts, got):
    return tuple(
        jnp.stack([plus(parts[0][half], got[0][half]), plus(parts[2][half], got[1][half])])
        for half in (slice(0, 2), slice(2, 4))
    )


def third_hops(parts):
    return (hop(parts[1], BIT_Z0),)


def third_sums(parts, got):
    return plus(parts[0][:, 0], got[0][:, 0]), plus(parts[0][:, 1], got[0][:, 1])


def fourth_hops(parts):
    return (hop(parts[1], BIT_Z1),)


def fourth_sums(parts, got):
    return plus(parts[0], got[0])


def product(left, right, dims):
    return lax.dot_general(left, right, (dims, ((), ())), preferred_element_type=f32)


NN = ((1,), (0,))
NT = ((1,), (1,))
TN = ((0,), (0,))


def slot(line, xr, yr):
    return (xr, yr) if line == 0 else (2 + yr, xr)


def rel_places():
    return [(m, m & 1, (m >> 1) & 1, ((m >> 2) & 1) * 2 + (m >> 3)) for m in range(16)]


def rows_of(i, m):
    return pl.ds(pl.multiple_of((i ^ m) * PIECE, 16), PIECE)


def load_line(store, halves, i, columns=slice(None)):
    for m, c, yr, z in rel_places():
        ref, first = halves[c][yr]
        store[rows_of(i, m), columns] = ref[first + z, 0:PIECE, :]


def save_chunk(value, outs, i, line, xr):
    for m in range(16):
        c, yr, z0r, z1r = m & 1, (m >> 1) & 1, (m >> 2) & 1, (m >> 3) & 1
        array, part = slot(line, xr, yr) if isinstance(xr, int) else (2 + yr, xr)
        row = pl.multiple_of((i ^ m) * PIECE, 16)
        outs[c][array, part * 4 + z0r * 2 + z1r] = value[pl.ds(row, PIECE), :]


def row_facts(info, r):
    first = info[2 + 3 * r]
    second = first + info[3 + 3 * r]
    third = second + info[4 + 3 * r]

    def segment(shape, axis):
        t = lax.broadcasted_iota(jnp.int32, shape, axis)
        return (t >= first).astype(jnp.int32) + (t >= second).astype(jnp.int32) + (t >= third).astype(jnp.int32)

    column = segment((256, 1), 0)

    def scale(branch):
        keeps = [info[8 + 6 * r + 2 * j + branch].astype(f32) * SCALE_ON for j in range(3)]
        return jnp.where(
            column == 0, keeps[0], jnp.where(column == 1, keeps[1], jnp.where(column == 2, keeps[2], 0.0))
        )

    inside = jnp.where(column < 3, 1.0, 0.0).astype(f32)
    return column, segment((1, 256), 1), scale, inside


def unit_of(values):
    center = values - jnp.mean(values, axis=-1, keepdims=True)
    spread = jnp.mean(center * center, axis=-1, keepdims=True)
    root = lax.rsqrt(spread + EPSILON)
    return center * root, root


def unit_back(unit, root, gain, incoming):
    eg = incoming * gain
    return root * (
        eg - jnp.mean(eg, axis=-1, keepdims=True) - unit * jnp.mean(eg * unit, axis=-1, keepdims=True)
    )


def sums(values):
    return jnp.sum(values, axis=0, keepdims=True)


def load_direct(store, own, other, i, spots):
    for m in range(16):
        spot = spots[0] * (m >> 3) + spots[1] * (m >> 2 & 1) + spots[2] * (m >> 1 & 1)
        row = pl.multiple_of((i ^ m) * PIECE, 16)
        store[pl.ds(row, PIECE), :] = (other if m & 1 else own)[spot, 0:PIECE, :]


def prepare_kernel(info, qkv, fc1, fc2, *rest):
    vectors, (lead, *groups) = rest[:9], rest[9:]
    x = info[1]
    at = pl.multiple_of(WIDE + WIDE * x, 128)
    lead[0, 0:48, :] = qkv[:, pl.ds(at + 384, 384)]
    lead[0, 48:96, :] = qkv[:, pl.ds(pl.multiple_of(384 * x, 128), 384)]
    lead[0, 96:144, :] = qkv[:, pl.ds(at, 384)]
    rows = [v[...].astype(f32).reshape(1, -1) for v in vectors]
    rows = rows[:8] + [rows[8][:, 48 * k : 48 * k + 48] for k in range(4)]
    rows = [jnp.pad(row, ((0, 0), (0, 336))) for row in rows]
    lead[0, 144:160, :] = jnp.concatenate(rows + [jnp.zeros((4, 384), f32)]).astype(bf16)
    for half in range(2):

        @pl.when(x == half)
        def _():
            for s in range(2):
                first = 48 * (2 * half + s)
                cuts = [fc1[:, 192 * j + first : 192 * j + first + 48] for j in range(16)]
                groups[s][0] = jnp.concatenate(cuts, axis=1)
                groups[s][1] = fc2[first : first + 48, :]


def load_qkv(weight, refs, i, x):
    for xr in range(2):
        h = x ^ xr
        a = [[(refs[6 * c + xr], 4 * yr) for yr in range(2)] for c in range(2)]
        b = [[(refs[6 * c + 2 + yr], 4 * xr) for yr in range(2)] for c in range(2)]
        q = [[(refs[6 * c + 4 + xr], 4 * yr) for yr in range(2)] for c in range(2)]
        load_line(weight.at[1 + h], a, i, slice(0, 384))
        load_line(weight.at[1 + h], b, i, slice(384, 768))
        load_line(weight.at[0], q, i, pl.ds(pl.multiple_of(384 * h, 128), 384))


def qkv_kernel(info, tok, small, *rest):
    refs, (packed, normed, weight) = rest[:12], rest[12:]
    i, x = info[0], info[1]
    load_qkv(weight, refs, i, x)
    for r in range(2):
        rows = slice(256 * r, 256 * r + 256)
        unit, _ = unit_of(tok[rows, :].astype(f32))
        normed[rows, :] = (unit * small[0:1, :] + small[1:2, :]).astype(bf16)
    for r in range(2):
        rows = slice(256 * r, 256 * r + 256)
        low = normed[rows, :]
        packed[rows, 0:768] = (product(low, weight[0], NN) + small[2:3, :]).astype(bf16)
        packed[rows, 768:1536] = product(low, weight[1], NN).astype(bf16)
        packed[rows, 1536:2304] = (product(low, weight[2], NN) + small[3:4, :]).astype(bf16)


def attend_kernel(info, packed, cot, attended, grad_two, lse, scores, weighting):
    r = pl.program_id(0)
    column, across, scale, inside = row_facts(info, r)
    same = column == across
    lane = lax.broadcasted_iota(jnp.int32, (256, 128), 1)
    kept = jnp.zeros((256, 128), f32)
    for g in range(HEADS):
        query = packed[:, 64 * g : 64 * g + 64] * 0.125
        scores[g] = product(query, packed[:, 768 + 64 * g : 832 + 64 * g], NT)
    for g in range(HEADS):
        masked = jnp.where(same, scores[g], NEGATIVE)
        top = jnp.max(masked, axis=-1, keepdims=True)
        raised = jnp.exp(masked - top)
        total = jnp.sum(raised, axis=-1, keepdims=True)
        weighting[g] = (raised * (1.0 / total)).astype(bf16)
        kept = jnp.where(lane == g, top + jnp.log(total), kept)
    lse[...] = kept
    for h in range(0, HEADS, 2):
        pair = [
            product(weighting[g], packed[:, 1536 + 64 * g : 1600 + 64 * g], NN).astype(bf16)
            for g in (h, h + 1)
        ]
        attended[:, 64 * h : 64 * h + 128] = jnp.concatenate(pair, axis=1)
    grad_two[...] = (cot[...].astype(f32) * inside * scale(1)).astype(bf16)


def hidden_units(block, normed, turned, grad_two, small, branch, grad_normed, bias, weights, scratch):
    active, low = scratch[:2]
    for r in range(2):
        rows = slice(256 * r, 256 * r + 256)
        value = product(normed[rows, :], weights[0], NN) + small[pl.ds(8 + block, 1), :]
        share = 0.5 * (1.0 + lax.erf(value * (0.5**0.5)))
        active[rows, :] = (value * share).astype(bf16)
        slope = share + value * (jnp.exp(-0.5 * value * value) * 0.3989422804014327)
        low[rows, :] = (product(grad_two[rows, :], weights[1], NT) * slope).astype(bf16)
    bias[pl.ds(8 + block, 1), :] = sums(low[...].astype(f32))
    for r in range(2):
        rows = slice(256 * r, 256 * r + 256)
        branch[rows, :] += product(active[rows, :], weights[1], NN)
        grad_normed[rows, :] += product(low[rows, :], weights[0], NT)
    scratch[2][...] = product(turned[...], low[...], NN).astype(bf16)
    scratch[3][...] = product(active[...], grad_two[...], TN).astype(bf16)


def load_units(scratch, refs, i, t):
    for step in range(2):

        @pl.when(t == step)
        def _():
            up = [[(refs[4 * c + step], 4 * yr) for yr in range(2)] for c in range(2)]
            down = [[(refs[4 * c + 2 + yr], 4 * step) for yr in range(2)] for c in range(2)]
            load_line(scratch[4], up, i)
            load_line(scratch[5], down, i)

    return scratch[4][...], scratch[5][...]


def save_units(scratch, own, away, i, t):
    for m, c, yr, z in rel_places():
        for part in range(2):
            here = slice(384 * part, 384 * part + 384)
            (own, away)[c][t, 4 * yr + z, part] = scratch[2][rows_of(i, m), here]
            (own, away)[c][2 + yr, 4 * t + z, part] = scratch[3][rows_of(i, m), here]


def first_units_kernel(info, attended, tok, grad_two, small, proj_own, proj_other, *rest):
    refs, (middle, normed, turned, branch, grad_normed, bias, own, away, proj, *scratch) = rest[:8], rest[8:]
    i, x, t = info[0], info[1], pl.program_id(0)

    @pl.when(t == 0)
    def _():
        load_direct(proj, proj_own, proj_other, i, (2, 4, 1))
        for r in range(2):
            rows = slice(256 * r, 256 * r + 256)
            _, _, scale, _ = row_facts(info, r)
            after = tok[rows, :].astype(f32) + scale(0) * (
                product(attended[rows, :], proj[...], NN) + small[4:5, :]
            )
            middle[rows, :] = after
            unit, _ = unit_of(after)
            normed[rows, :] = (unit * small[5:6, :] + small[6:7, :]).astype(bf16)
        turned[...] = normed[...].T
        branch[...] = jnp.zeros_like(branch)
        grad_normed[...] = jnp.zeros_like(grad_normed)
        bias[...] = jnp.zeros_like(bias)
        bias[7:8, :] = sums(grad_two[...].astype(f32))

    weights = load_units(scratch, refs, i, t)
    hidden_units(2 * (t ^ x), normed, turned, grad_two, small, branch, grad_normed, bias, weights, scratch)
    save_units(scratch, own, away, i, t)


def second_units_kernel(
    info, normed, turned, grad_two, small, branch_in, grad_normed_in, bias_in, middle, cot, *rest
):
    refs, (result, grad_middle, grad_one, bias, own, away, branch, grad_normed, *scratch) = rest[:8], rest[8:]
    i, x, t = info[0], info[1], pl.program_id(0)

    @pl.when(t == 0)
    def _():
        branch[...] = branch_in[...]
        grad_normed[...] = grad_normed_in[...]
        bias[...] = bias_in[...]

    weights = load_units(scratch, refs, i, t)
    hidden_units(2 * (t ^ x) + 1, normed, turned, grad_two, small, branch, grad_normed, bias, weights, scratch)
    save_units(scratch, own, away, i, t)

    @pl.when(t == 1)
    def _():
        for r in range(2):
            rows = slice(256 * r, 256 * r + 256)
            _, _, scale, inside = row_facts(info, r)
            after = middle[rows, :]
            result[rows, :] = (
                (after + scale(1) * (branch[rows, :] + small[7:8, :])) * inside
            ).astype(bf16)
            unit, root = unit_of(after)
            incoming = grad_normed[rows, :]
            bias[5:6, :] += sums(incoming * unit)
            bias[6:7, :] += sums(incoming)
            total = cot[rows, :].astype(f32) * inside + unit_back(unit, root, small[5:6, :], incoming)
            grad_middle[rows, :] = total
            low_one = (total * scale(0)).astype(bf16)
            grad_one[rows, :] = low_one
            bias[4:5, :] += sums(low_one.astype(f32))


def attend_back_kernel(group, info, queries, keys, values, lse, attended, grad_one, normed, *rest):
    if group == 0:
        proj_own, proj_other, grad_packed, own, away, weight, proj_rest, grad, *heads, total = rest
    else:
        weight, proj_rest, grad_packed, own, away, grad, *heads = rest
    i, x, r = info[0], info[1], pl.program_id(0)
    if group == 0:

        @pl.when(r == 0)
        def _():
            load_direct(weight, proj_own, proj_other, i, (2, 4, 1))
            total[...] = jnp.zeros_like(total)

        total[...] += product(attended[...], grad_one[...], TN)

    column, across, _, _ = row_facts(info, r)
    same = column == across
    grad_attended = product(grad_one[...], weight[384 * group : 384 * group + 384, :], NT).astype(bf16)
    rows = pl.ds(pl.multiple_of(r * 256, 256), 256)
    scores, backs, lows, highs = heads
    queried = [queries[:, 64 * g : 64 * g + 64] * 0.125 for g in range(6)]
    returned = [grad_attended[:, 64 * g : 64 * g + 64] for g in range(6)]
    for g in range(6):
        here = slice(64 * g, 64 * g + 64)
        scores[g] = product(queried[g], keys[:, here], NT)
        backs[g] = product(returned[g], values[:, here], NT)
    for g in range(6):
        head = 6 * group + g
        weighting = jnp.where(same, jnp.exp(scores[g] - lse[:, head : head + 1]), 0.0)
        highs[g] = weighting.astype(bf16)
        share = backs[g] * weighting
        inner = jnp.sum(share, axis=-1, keepdims=True)
        lows[g] = (share - weighting * inner).astype(bf16)
    for h in range(0, 6, 2):
        pairs = ([], [], [])
        for g in (h, h + 1):
            pairs[0].append(product(lows[g], keys[:, 64 * g : 64 * g + 64], NN) * 0.125)
            pairs[1].append(product(lows[g], queried[g], TN))
            pairs[2].append(product(highs[g], returned[g], TN))
        for k in range(3):
            grad_packed[rows, 384 * k + 64 * h : 384 * k + 64 * h + 128] = jnp.concatenate(
                pairs[k], axis=1
            ).astype(bf16)

    @pl.when(r == 1)
    def _():
        turned = normed[...].T
        grad[1, 0] = product(turned, grad_packed[:, 0:384], NN).astype(bf16)
        grad[0, 0] = product(turned, grad_packed[:, 384:768], NN).astype(bf16)
        grad[0, 1] = product(turned, grad_packed[:, 768:1152], NN).astype(bf16)
        if group == 0:
            grad[1, 1] = total[:, 0:384].astype(bf16)
            proj_rest[...] = total[:, 384:768].astype(bf16)
        else:
            grad[1, 1] = proj_rest[...]
        for line in range(2):
            for xr in range(2):
                save_chunk(grad.at[line, x ^ xr], (own, away), i, line, xr)


def tokens_back_kernel(r, info, tok, back0, back1, grad_middle, bias_in, small, *rest):
    refs, (tokens_grad, bias, weight) = rest[:12], rest[-3:]
    i, x = info[0], info[1]
    load_qkv(weight, refs, i, x)
    bias[...] = bias_in[...]
    for part, back in ((0, back0), (1, back1)):
        columns = slice(384 * part, 384 * part + 384)
        bias[2:3, columns] += sums(back[:, 0:384].astype(f32))
        bias[3:4, columns] += sums(back[:, 768:1152].astype(f32))
    incoming = jnp.zeros((256, WIDE), f32)
    for k in range(3):
        here = slice(384 * k, 384 * k + 384)
        joined = jnp.concatenate([back0[:, here], back1[:, here]], axis=1)
        incoming += product(joined, weight[k], NT)
    unit, root = unit_of(tok[...].astype(f32))
    bias[0:1, :] += sums(incoming * unit)
    bias[1:2, :] += sums(incoming)
    tokens_grad[...] = grad_middle[...] + unit_back(unit, root, small[0:1, :], incoming)


def results_kernel(info, mine0, other0, mine1, other1, bias, qkv, proj, *vectors):
    i, x = info[0], info[1]
    for group, mine, other in ((0, mine0, other0), (1, mine1, other1)):
        for line, half, column in ((1, 0, 0), (0, 0, 768), (0, 1, 1536), (1, 1, None)):
            a, b = mine[line].astype(f32), other[line].astype(f32)
            value = jnp.where(x == half, a, b)
            if column is None:
                proj[:, 384 * group : 384 * group + 384] = value
            else:
                qkv[:, column + 384 * group : column + 384 * group + 384] = value

    def cut(rows, start, width):
        feature = lax.broadcasted_iota(jnp.int32, (WIDE, width), 0)
        lane = lax.broadcasted_iota(jnp.int32, (WIDE, width), 1)
        chosen = (feature == lane + start).astype(f32)
        return lax.dot_general(
            rows, chosen, (NN, ((), ())), precision=lax.Precision.HIGHEST, preferred_element_type=f32
        )

    narrow = cut(bias[...], i * 48, 128)
    for k in range(8):
        vectors[k][...] = narrow[k, 0:48]
    broad = jnp.concatenate([narrow[8 + k : 9 + k, 0:48] for k in range(4)], axis=1)
    vectors[8][...] = broad[0]


def units_results_kernel(info, mine0, other0, mine1, other1, fc1, fc2):
    x = info[1]
    blocks = []
    for half in range(2):
        for mine, other in ((mine0, other0), (mine1, other1)):
            pieces = [
                jnp.concatenate(
                    [jnp.where(x == half, mine[k, p].astype(f32), other[k, p].astype(f32)) for p in range(2)],
                    axis=1,
                )
                for k in range(2)
            ]
            fc2[48 * len(blocks) : 48 * len(blocks) + 48, :] = pieces[1]
            blocks.append(pieces[0])
    for j in range(0, 16, 2):
        cuts = [b[:, 48 * k : 48 * k + 48] for k in (j, j + 1) for b in blocks]
        fc1[:, 192 * j : 192 * j + 384] = jnp.concatenate(cuts, axis=1)


def whole(shape):
    return pl.BlockSpec(shape, lambda *_: (0,) * len(shape))


def once(shape):
    return pl.BlockSpec(shape, lambda *_: (0,) * len(shape), pipeline_mode=pl.Buffered(1))


def rowwise(width):
    return pl.BlockSpec((256, width), lambda r, info: (r, 0))


def run_kernel(kernel, grid, info, operands, outs, scratch, microseconds, vmem, alias=None):
    return pl.pallas_call(
        kernel,
        grid_spec=pltpu.PrefetchScalarGridSpec(
            num_scalar_prefetch=1,
            grid=(grid,),
            in_specs=[spec or once(array.shape) for spec, array in operands],
            out_specs=[spec or whole(shape) for spec, shape, _ in outs],
            scratch_shapes=[pltpu.VMEM(shape, dtype) for shape, dtype in scratch],
        ),
        out_shape=[jax.ShapeDtypeStruct(shape, dtype) for _, shape, dtype in outs],
        input_output_aliases=alias or {},
        compiler_params=pltpu.CompilerParams(
            dimension_semantics=("arbitrary",), vmem_limit_bytes=vmem * MIB
        ),
        cost_estimate=pl.CostEstimate(
            flops=int(microseconds * 1.15e9), bytes_accessed=1 << 20, transcendentals=0
        ),
    )(info, *[array for _, array in operands])


def fast_device(
    tokens,
    lengths,
    keep_mask,
    cotangent,
    ln1_gain,
    ln1_bias,
    qkv_weight,
    q_bias,
    v_bias,
    proj_weight,
    proj_bias,
    ln2_gain,
    ln2_bias,
    fc1_weight,
    fc1_bias,
    fc2_weight,
    fc2_bias,
):
    count = tokens.shape[0] * tokens.shape[1]
    i = lax.axis_index("fsdp")
    x = lax.axis_index("dp")
    info = jnp.concatenate(
        [jnp.stack([i, x]).astype(jnp.int32), lengths.reshape(-1), keep_mask.reshape(-1)]
    )
    tok = tokens.reshape(count, WIDE)
    cot = cotangent.reshape(count, WIDE)

    def full(*arrays):
        return [(None, array) for array in arrays]

    vectors = (ln1_gain, ln1_bias, q_bias, v_bias, proj_bias, ln2_gain, ln2_bias, fc2_bias, fc1_bias)
    lead, units0, units1 = run_kernel(
        prepare_kernel,
        1,
        jnp.stack([i, x]),
        full(qkv_weight, fc1_weight, fc2_weight, *vectors),
        [(None, (1, 160, 384), bf16), (None, (2, PIECE, WIDE), bf16), (None, (2, PIECE, WIDE), bf16)],
        [],
        2,
        60,
    )

    proj = tie(proj_weight[None], lead)
    proj = join(proj, hop(proj, BIT_Y))

    pair = join(lead, hop(lead, BIT_Z1))
    far = hop(pair, BIT_Z0)
    line_b, line_q, line_a = (join(pair[:, k], far[:, k]) for k in (slice(0, 48), slice(48, 96), slice(96, 160)))
    line_a, line_b, line_q, units0 = lax.optimization_barrier((line_a, line_b, line_q, units0))
    got_a, got_b, got_q = hop(line_a, BIT_Y), swap(line_b), hop(line_q, BIT_Y)
    units_far = hop(units0, BIT_Z1)
    got_a, got_b = lax.optimization_barrier((got_a, got_b))
    wide_a, wide_b = join(line_a, got_a), join(line_b, got_b)
    got_a, got_b = swap(wide_a[:, :PIECE]), hop(wide_b, BIT_Y)
    wide_q = join(line_q, got_q)
    got_q = swap(wide_q)
    units_far = tie(units_far, wide_a, wide_b)
    units0 = jnp.stack([units0, units_far], axis=1)
    units_far = hop(units0, BIT_Z0)
    units1 = tie(units1, wide_a, wide_b, units0)
    next_far = hop(units1, BIT_Z1)
    got_a, got_b, got_q, units_far, next_far, proj = lax.optimization_barrier(
        (got_a, got_b, got_q, units_far, next_far, proj)
    )
    first = to_other_core((wide_a, got_a, wide_b, got_b, wide_q, got_q))

    units_line = join(units0[0], units_far[0]), join(units0[1], units_far[1])
    units_got = hop(units_line[0], BIT_Y), swap(units_line[1])
    units1 = jnp.stack([units1, next_far], axis=1)
    next_far = hop(units1, BIT_Z0)
    proj_far = hop(proj, BIT_Z1)

    vectors = jnp.concatenate([first[k][:, PIECE : PIECE + 12, :PIECE] for k in (0, 6)])
    origin = jnp.array([(p & 1) * 8 + (p >> 1 & 1) * 4 + (p >> 2 & 1) * 2 + (p >> 3) for p in range(16)])
    turned = jnp.arange(16)[:, None] == (origin ^ i)[None, :]
    vectors = jnp.einsum("mp,pkl->kml", turned.astype(bf16), vectors, preferred_element_type=f32)
    small = jnp.concatenate([vectors.reshape(12, WIDE), jnp.zeros((4, WIDE), f32)])

    packed, normed_one = run_kernel(
        qkv_kernel,
        1,
        info,
        full(tok, small, *first),
        [(None, (count, 3 * WIDE), bf16), (None, (count, WIDE), bf16)],
        [((3, WIDE, WIDE), bf16)],
        5,
        40,
    )

    units_got, next_far, proj_far, _ = lax.optimization_barrier((units_got, next_far, proj_far, packed))
    units_wide = tuple(join(line, got) for line, got in zip(units_line, units_got))
    units_got = swap(units_wide[0]), hop(units_wide[1], BIT_Y)
    next_line = tuple(join(units1[k], next_far[k]) for k in range(2))
    next_got = hop(next_line[0], BIT_Y), swap(next_line[1])
    proj = join(proj, proj_far)
    proj_far = hop(proj, BIT_Z0)

    attended, grad_two, lse = run_kernel(
        attend_kernel,
        2,
        tie(info, *units_wide, *next_line, proj),
        [(rowwise(3 * WIDE), packed), (rowwise(WIDE), cot)],
        [
            (rowwise(WIDE), (count, WIDE), bf16),
            (rowwise(WIDE), (count, WIDE), bf16),
            (rowwise(128), (count, 128), f32),
        ],
        [((HEADS, 256, 256), f32), ((HEADS, 256, 256), bf16)],
        6,
        40,
    )

    units_got, next_got, proj_far, _ = lax.optimization_barrier((units_got, next_got, proj_far, lse))
    proj = join(proj, proj_far)
    proj_other = hop(proj, BIT_C)
    units = to_other_core((units_wide[0], units_got[0], units_wide[1], units_got[1]))
    next_wide = tuple(join(line, got) for line, got in zip(next_line, next_got))
    next_got = swap(next_wide[0]), hop(next_wide[1], BIT_Y)

    wide_f32 = (None, (count, WIDE), f32)
    wide_bf16 = (None, (count, WIDE), bf16)
    vectors_f32 = (None, (16, WIDE), f32)
    parts = (None, (4, 8, 2, PIECE, 384), bf16)
    unit_scratch = [((count, WIDE), bf16)] * 2 + [((WIDE, WIDE), bf16)] * 4
    middle, normed_two, turned_two, branch, grad_normed, bias, units_own, units_away = run_kernel(
        first_units_kernel,
        2,
        tie(info, *next_wide),
        full(attended, tok, grad_two, small, proj, proj_other, *units),
        [wide_f32, wide_bf16, (None, (WIDE, count), bf16), wide_f32, wide_f32, vectors_f32, parts, parts],
        [((WIDE, WIDE), bf16)] + unit_scratch,
        13,
        40,
    )
    next_got, bias, units_away = lax.optimization_barrier((next_got, bias, units_away))
    units = to_other_core((next_wide[0], next_got[0], next_wide[1], next_got[1]))
    two = core_sums(units_own, hop(units_away, BIT_C))
    two_got = first_hops(two)
    output, grad_middle, grad_one, bias, units_own, units_away = run_kernel(
        second_units_kernel,
        2,
        tie(info, *two),
        full(normed_two, turned_two, grad_two, small, branch, grad_normed, bias, middle, cot, *units),
        [wide_bf16, wide_f32, wide_bf16, vectors_f32, parts, parts],
        [((count, WIDE), f32)] * 2 + unit_scratch,
        15,
        40,
    )

    def attend_back(group, info, more, outs, scratch):
        def columns(k):
            return pl.BlockSpec((256, 384), lambda r, _, at=2 * k + group: (r, at))

        narrow = (4, 8, PIECE, 384)
        return run_kernel(
            functools.partial(attend_back_kernel, group),
            2,
            info,
            [(columns(k), packed) for k in range(3)]
            + [(rowwise(128), lse), (rowwise(WIDE), attended), (rowwise(WIDE), grad_one)]
            + full(normed_one, *more),
            [(None, (count, 1152), bf16), (None, narrow, bf16), (None, narrow, bf16)] + outs,
            [((2, 2, WIDE, 384), bf16)]
            + [((6, 256, 256), f32)] * 2
            + [((6, 256, 256), bf16)] * 2
            + scratch,
            8,
            40,
        )

    two_got, bias, units_away = lax.optimization_barrier((two_got, bias, units_away))
    two = first_sums(two, two_got)
    two_got, one_came = second_hops(two), hop(units_away, BIT_C)
    back0, head_own0, head_away0, proj_full, proj_rest = attend_back(
        0,
        tie(info, *two),
        (proj, proj_other),
        [(None, (WIDE, WIDE), bf16), (None, (WIDE, 384), bf16)],
        [((WIDE, WIDE), f32)],
    )

    two_got, one_came, proj_rest, head_away0 = lax.optimization_barrier(
        (two_got, one_came, proj_rest, head_away0)
    )
    two = second_sums(two, two_got)
    one = core_sums(units_own, one_came)
    one_got, two_got, zero_came = first_hops(one), third_hops(two), hop(head_away0, BIT_C)
    back1, head_own1, head_away1 = attend_back(1, tie(info, *two, *one), (proj_full, proj_rest), [], [])

    two_got, one_got, zero_came, head_away1 = lax.optimization_barrier(
        (two_got, one_got, zero_came, head_away1)
    )
    two, one, zero = third_sums(two, two_got), first_sums(one, one_got), core_sums(head_own0, zero_came)
    last_came = hop(head_away1, BIT_C)
    zero_got, one_got = first_hops(zero), second_hops(one)

    def tokens_back(r, info, more, alias):
        def row(width):
            return pl.BlockSpec((256, width), lambda _, __: (r, 0))

        return run_kernel(
            functools.partial(tokens_back_kernel, r),
            1,
            info,
            [(row(WIDE), tok), (row(1152), back0), (row(1152), back1), (row(WIDE), grad_middle)]
            + full(bias, small, *first)
            + more,
            [(row(WIDE), (count, WIDE), f32), (None, (16, WIDE), f32)],
            [((3, WIDE, WIDE), bf16)],
            5,
            40,
            alias,
        )

    tokens_grad, bias = tokens_back(0, tie(info, *two, *one, *zero), [], {})

    zero_got, last_came, bias = lax.optimization_barrier((zero_got, last_came, bias))
    last, zero = core_sums(head_own1, last_came), first_sums(zero, zero_got)
    two_got = fourth_hops(two)
    got_x, got_y = together(swap, last[1], zero[3]), together(hop_y, last[3], zero[1])
    last_got, zero_got = (got_x[0], got_y[0]), (got_y[1], got_x[1])
    tokens_grad, bias = tokens_back(
        1, tie(info, *last, *zero), [(pl.BlockSpec(memory_space=pl.ANY), tokens_grad)], {19: 0}
    )

    last_got, zero_got, two_got, one_got, bias = lax.optimization_barrier(
        (last_got, zero_got, two_got, one_got, bias)
    )
    last, zero, two, one = (
        first_sums(last, last_got),
        second_sums(zero, zero_got),
        fourth_sums(two, two_got),
        second_sums(one, one_got),
    )
    last_got, got, two_other, bias_got = lax.optimization_barrier(
        (second_hops(last), together(hop_z0, one[1], zero[1]), swap(two), hop(bias, BIT_Y))
    )
    last, one, zero = second_sums(last, last_got), third_sums(one, got[:1]), third_sums(zero, got[1:])
    bias = bias + bias_got
    last_got, got, bias_got = lax.optimization_barrier(
        (third_hops(last), together(hop_z1, one[1], zero[1]), hop(bias, BIT_Z0))
    )
    last, one, zero = third_sums(last, last_got), fourth_sums(one, got[:1]), fourth_sums(zero, got[1:])
    bias = bias + bias_got
    last_got, got, bias_got = lax.optimization_barrier(
        (fourth_hops(last), together(swap, one, zero), hop(bias, BIT_Z1))
    )
    one_other, zero_other = got
    last, bias = fourth_sums(last, last_got), bias + bias_got
    last_other, bias_got = swap(last), (swap(bias), hop(bias, BIT_C), cross(bias))
    fc1_grad, fc2_grad = run_kernel(
        units_results_kernel,
        1,
        info,
        full(two, two_other, one, one_other),
        [(None, (PIECE, 4 * WIDE), f32), (None, (4 * PIECE, WIDE), f32)],
        [],
        3,
        40,
    )
    bias = (bias + bias_got[0]) + (bias_got[1] + bias_got[2])
    qkv_grad, proj_grad, *narrow = run_kernel(
        results_kernel,
        1,
        info,
        full(zero, zero_other, last, last_other, bias),
        [(None, (PIECE, 3 * WIDE), f32), (None, (PIECE, WIDE), f32)]
        + [(None, (48,), f32)] * 8
        + [(None, (192,), f32)],
        [],
        3,
        40,
    )
    return (
        output.reshape(tokens.shape),
        tokens_grad.reshape(tokens.shape),
        narrow[0],
        narrow[1],
        qkv_grad,
        narrow[2],
        narrow[3],
        proj_grad,
        narrow[4],
        narrow[5],
        narrow[6],
        fc1_grad,
        narrow[8],
        fc2_grad,
        narrow[7],
    )


def solution(mesh):
    in_specs = (
        P(("dp", "fsdp"), None, None),
        P(("dp", "fsdp"), None),
        P(("dp", "fsdp"), None, None),
        P(("dp", "fsdp"), None, None),
        P("fsdp"),
        P("fsdp"),
        P("fsdp", None),
        P("fsdp"),
        P("fsdp"),
        P("fsdp", None),
        P("fsdp"),
        P("fsdp"),
        P("fsdp"),
        P("fsdp", None),
        P("fsdp"),
        P("fsdp", None),
        P("fsdp"),
    )
    out_specs = (
        P(("dp", "fsdp"), None, None),
        P(("dp", "fsdp"), None, None),
        P("fsdp"),
        P("fsdp"),
        P("fsdp", None),
        P("fsdp"),
        P("fsdp"),
        P("fsdp", None),
        P("fsdp"),
        P("fsdp"),
        P("fsdp"),
        P("fsdp", None),
        P("fsdp"),
        P("fsdp", None),
        P("fsdp"),
    )
    fits = mesh.shape["dp"] == 2 and mesh.shape["fsdp"] == 16
    return jax.shard_map(
        fast_device if fits else per_device, mesh=mesh, in_specs=in_specs, out_specs=out_specs, check_vma=False
    )
```

```python
import functools

import jax
import jax.numpy as jnp
from jax import lax
from jax.experimental import pallas as pl
from jax.experimental.pallas import tpu as pltpu
from jax.sharding import PartitionSpec as P

HEADS = 12


EPSILON = 1e-06
KEEP_RATE = 0.9
NEGATIVE = -1e30


def normalize(values, gain, shift):
    center = values - jnp.mean(values, axis=-1, keepdims=True)
    spread = jnp.mean(center * center, axis=-1, keepdims=True)
    return center * lax.rsqrt(spread + EPSILON) * gain + shift


def standardize(values):
    center = values - jnp.mean(values, axis=-1, keepdims=True)
    spread = jnp.mean(center * center, axis=-1, keepdims=True)
    return center * lax.rsqrt(spread + EPSILON)


def affine_low(unit_values, gain, shift):
    return (unit_values * gain.astype(jnp.float32) + shift.astype(jnp.float32)).astype(jnp.bfloat16)


def exact_gelu(values):
    return jax.nn.gelu(values, approximate=False)


def norm_back(values, gain, shift, incoming):
    _, pullback = jax.vjp(normalize, values, gain, shift)
    return pullback(incoming)


def inner_rows(left, right):
    return lax.dot_general(
        left, right, (((0,), (0,)), ((), ())), preferred_element_type=jnp.float32
    )


def times_transpose(left, right):
    return lax.dot_general(
        left, right, (((1,), (1,)), ((), ())), preferred_element_type=jnp.float32
    )


def layout(lengths, keep_mask, length):
    image_ends = jnp.cumsum(lengths, axis=-1, dtype=jnp.int32)
    position = jnp.arange(length, dtype=jnp.int32)
    segment = jnp.sum(
        (position[None, :, None] >= image_ends[:, None, :]).astype(jnp.int32),
        axis=-1,
        dtype=jnp.int32,
    )
    images = jnp.arange(lengths.shape[1], dtype=jnp.int32)
    member = (segment[:, :, None] == images[None, None, :]).astype(jnp.float32)
    keeping = keep_mask.astype(jnp.float32)
    scales = jnp.sum(member[:, :, :, None] * keeping[:, None, :, :], axis=2) / KEEP_RATE
    inside = jnp.sum(member, axis=-1)
    return (segment, scales, inside)


def attention_forward(packed, segment, rowset, length, head_size):
    split_view = packed.reshape(rowset, length, 3, HEADS, head_size)
    queries = split_view[:, :, 0]
    keys_all = split_view[:, :, 1]
    values_all = split_view[:, :, 2]
    scores = jnp.einsum(
        "rqhd,rkhd->rhqk", queries, keys_all, preferred_element_type=jnp.float32
    ) * head_size ** (-0.5)
    matching = segment[:, :, None] == segment[:, None, :]
    scores = jnp.where(matching[:, None], scores, NEGATIVE)
    raised = jnp.exp(scores - jnp.max(scores, axis=-1, keepdims=True))
    weighting = raised / jnp.sum(raised, axis=-1, keepdims=True)
    weighting_low = weighting.astype(jnp.bfloat16)
    attended = jnp.einsum(
        "rhqk,rkhd->rqhd", weighting_low, values_all, preferred_element_type=jnp.float32
    )
    attended = attended.reshape(rowset * length, HEADS * head_size).astype(jnp.bfloat16)
    return (queries, keys_all, values_all, weighting, weighting_low, attended)


def per_device(
    tokens,
    lengths,
    keep_mask,
    cotangent,
    ln1_gain,
    ln1_bias,
    qkv_weight,
    q_bias,
    v_bias,
    proj_weight,
    proj_bias,
    ln2_gain,
    ln2_bias,
    fc1_weight,
    fc1_bias,
    fc2_weight,
    fc2_bias,
):
    rowset, length, features = tokens.shape
    head_size = features // HEADS
    token_count = rowset * length
    segment, scales, inside = layout(lengths, keep_mask, length)
    scale_one = scales[:, :, 0].reshape(token_count, 1)
    scale_two = scales[:, :, 1].reshape(token_count, 1)
    inside_column = inside.reshape(token_count, 1)
    flattened = tokens.reshape(token_count, features).astype(jnp.float32)
    unit_one = standardize(flattened)
    qkv_full, proj_full, gain_one, shift_one, query_bias, value_bias, out_bias = (
        lax.all_gather(qkv_weight, "fsdp", axis=0, tiled=True),
        lax.all_gather(proj_weight, "fsdp", axis=0, tiled=True),
        lax.all_gather(ln1_gain, "fsdp", axis=0, tiled=True),
        lax.all_gather(ln1_bias, "fsdp", axis=0, tiled=True),
        lax.all_gather(q_bias, "fsdp", axis=0, tiled=True),
        lax.all_gather(v_bias, "fsdp", axis=0, tiled=True),
        lax.all_gather(proj_bias, "fsdp", axis=0, tiled=True),
    )
    normed_one = affine_low(unit_one, gain_one, shift_one)
    bias_all = jnp.concatenate(
        [
            query_bias.astype(jnp.float32),
            jnp.zeros((features,), jnp.float32),
            value_bias.astype(jnp.float32),
        ]
    )
    packed = (jnp.dot(normed_one, qkv_full, preferred_element_type=jnp.float32) + bias_all).astype(
        jnp.bfloat16
    )
    _, _, _, _, _, attended = attention_forward(packed, segment, rowset, length, head_size)
    branch_one = jnp.dot(attended, proj_full, preferred_element_type=jnp.float32) + out_bias.astype(
        jnp.float32
    )
    middle = flattened + scale_one * branch_one
    unit_two = standardize(middle)
    up_full, down_full, gain_two, shift_two, up_bias, down_bias = (
        lax.all_gather(fc1_weight, "fsdp", axis=0, tiled=True),
        lax.all_gather(fc2_weight, "fsdp", axis=0, tiled=True),
        lax.all_gather(ln2_gain, "fsdp", axis=0, tiled=True),
        lax.all_gather(ln2_bias, "fsdp", axis=0, tiled=True),
        lax.all_gather(fc1_bias, "fsdp", axis=0, tiled=True),
        lax.all_gather(fc2_bias, "fsdp", axis=0, tiled=True),
    )
    normed_two = affine_low(unit_two, gain_two, shift_two)
    hidden = jnp.dot(normed_two, up_full, preferred_element_type=jnp.float32) + up_bias.astype(
        jnp.float32
    )
    active = exact_gelu(hidden).astype(jnp.bfloat16)
    branch_two = jnp.dot(active, down_full, preferred_element_type=jnp.float32) + down_bias.astype(
        jnp.float32
    )
    output = (
        ((middle + scale_two * branch_two) * inside_column)
        .astype(jnp.bfloat16)
        .reshape(rowset, length, features)
    )
    up_full, down_full = (
        lax.all_gather(fc1_weight, "fsdp", axis=0, tiled=True),
        lax.all_gather(fc2_weight, "fsdp", axis=0, tiled=True),
    )
    gain_two_f = gain_two.astype(jnp.float32)
    shift_two_f = shift_two.astype(jnp.float32)
    grad_out = cotangent.reshape(token_count, features).astype(jnp.float32) * inside_column
    grad_two_low = (grad_out * scale_two).astype(jnp.bfloat16)
    fc2_grad = inner_rows(active, grad_two_low)
    fc2_bias_part = jnp.sum(grad_two_low.astype(jnp.float32), axis=0)
    grad_active = times_transpose(grad_two_low, down_full)
    _, gelu_pull = jax.vjp(exact_gelu, hidden)
    grad_hidden_low = gelu_pull(grad_active)[0].astype(jnp.bfloat16)
    fc1_grad = inner_rows(normed_two, grad_hidden_low)
    fc1_bias_part = jnp.sum(grad_hidden_low.astype(jnp.float32), axis=0)
    grad_normed_two = times_transpose(grad_hidden_low, up_full)
    grad_middle_norm, gain_two_part, shift_two_part = norm_back(
        middle, gain_two_f, shift_two_f, grad_normed_two
    )
    grad_middle = grad_out + grad_middle_norm
    qkv_full, proj_full = (
        lax.all_gather(qkv_weight, "fsdp", axis=0, tiled=True),
        lax.all_gather(proj_weight, "fsdp", axis=0, tiled=True),
    )
    gain_one_f = gain_one.astype(jnp.float32)
    shift_one_f = shift_one.astype(jnp.float32)
    queries, keys_all, values_all, weighting, weighting_low, attended = attention_forward(
        packed, segment, rowset, length, head_size
    )
    grad_one_low = (grad_middle * scale_one).astype(jnp.bfloat16)
    proj_grad = inner_rows(attended, grad_one_low)
    proj_bias_part = jnp.sum(grad_one_low.astype(jnp.float32), axis=0)
    grad_attended_low = times_transpose(grad_one_low, proj_full).astype(jnp.bfloat16)
    grad_attended_low = grad_attended_low.reshape(rowset, length, HEADS, head_size)
    grad_weighting = jnp.einsum(
        "rqhd,rkhd->rhqk", grad_attended_low, values_all, preferred_element_type=jnp.float32
    )
    value_grad = jnp.einsum(
        "rhqk,rqhd->rkhd", weighting_low, grad_attended_low, preferred_element_type=jnp.float32
    )
    row_inner = jnp.sum(grad_weighting * weighting, axis=-1, keepdims=True)
    grad_scores_low = (weighting * (grad_weighting - row_inner)).astype(jnp.bfloat16)
    key_scale = head_size ** (-0.5)
    query_grad = (
        jnp.einsum("rhqk,rkhd->rqhd", grad_scores_low, keys_all, preferred_element_type=jnp.float32)
        * key_scale
    )
    key_grad = (
        jnp.einsum("rhqk,rqhd->rkhd", grad_scores_low, queries, preferred_element_type=jnp.float32)
        * key_scale
    )
    grad_packed_low = (
        jnp.stack([query_grad, key_grad, value_grad], axis=2)
        .reshape(token_count, 3 * features)
        .astype(jnp.bfloat16)
    )
    qkv_grad = inner_rows(normed_one, grad_packed_low)
    column_sums = jnp.sum(grad_packed_low.astype(jnp.float32), axis=0)
    query_bias_part = column_sums[:features]
    value_bias_part = column_sums[2 * features :]
    grad_normed_one = times_transpose(grad_packed_low, qkv_full)
    grad_input_norm, gain_one_part, shift_one_part = norm_back(
        flattened, gain_one_f, shift_one_f, grad_normed_one
    )
    tokens_grad = (grad_middle + grad_input_norm).reshape(rowset, length, features)
    (
        gain_two_grad,
        shift_two_grad,
        fc1_weight_part,
        fc1_bias_shard,
        fc2_weight_part,
        fc2_bias_shard,
    ) = (
        lax.psum_scatter(gain_two_part, "fsdp", scatter_dimension=0, tiled=True),
        lax.psum_scatter(shift_two_part, "fsdp", scatter_dimension=0, tiled=True),
        lax.psum_scatter(fc1_grad, "fsdp", scatter_dimension=0, tiled=True),
        lax.psum_scatter(fc1_bias_part, "fsdp", scatter_dimension=0, tiled=True),
        lax.psum_scatter(fc2_grad, "fsdp", scatter_dimension=0, tiled=True),
        lax.psum_scatter(fc2_bias_part, "fsdp", scatter_dimension=0, tiled=True),
    )
    (
        gain_one_grad,
        shift_one_grad,
        qkv_weight_part,
        query_bias_shard,
        value_bias_shard,
        proj_weight_part,
        proj_bias_shard,
    ) = (
        lax.psum_scatter(gain_one_part, "fsdp", scatter_dimension=0, tiled=True),
        lax.psum_scatter(shift_one_part, "fsdp", scatter_dimension=0, tiled=True),
        lax.psum_scatter(qkv_grad, "fsdp", scatter_dimension=0, tiled=True),
        lax.psum_scatter(query_bias_part, "fsdp", scatter_dimension=0, tiled=True),
        lax.psum_scatter(value_bias_part, "fsdp", scatter_dimension=0, tiled=True),
        lax.psum_scatter(proj_grad, "fsdp", scatter_dimension=0, tiled=True),
        lax.psum_scatter(proj_bias_part, "fsdp", scatter_dimension=0, tiled=True),
    )
    summed = (
        lax.psum(gain_one_grad.astype(jnp.bfloat16), "dp").astype(jnp.float32),
        lax.psum(shift_one_grad.astype(jnp.bfloat16), "dp").astype(jnp.float32),
        lax.psum(qkv_weight_part.astype(jnp.bfloat16), "dp").astype(jnp.float32),
        lax.psum(query_bias_shard.astype(jnp.bfloat16), "dp").astype(jnp.float32),
        lax.psum(value_bias_shard.astype(jnp.bfloat16), "dp").astype(jnp.float32),
        lax.psum(proj_weight_part.astype(jnp.bfloat16), "dp").astype(jnp.float32),
        lax.psum(proj_bias_shard.astype(jnp.bfloat16), "dp").astype(jnp.float32),
        lax.psum(gain_two_grad.astype(jnp.bfloat16), "dp").astype(jnp.float32),
        lax.psum(shift_two_grad.astype(jnp.bfloat16), "dp").astype(jnp.float32),
        lax.psum(fc1_weight_part.astype(jnp.bfloat16), "dp").astype(jnp.float32),
        lax.psum(fc1_bias_shard.astype(jnp.bfloat16), "dp").astype(jnp.float32),
        lax.psum(fc2_weight_part.astype(jnp.bfloat16), "dp").astype(jnp.float32),
        lax.psum(fc2_bias_shard.astype(jnp.bfloat16), "dp").astype(jnp.float32),
    )
    return (
        output,
        tokens_grad,
        summed[0],
        summed[1],
        summed[2],
        summed[3],
        summed[4],
        summed[5],
        summed[6],
        summed[7],
        summed[8],
        summed[9],
        summed[10],
        summed[11],
        summed[12],
    )


BIT_Z1, BIT_Z0, BIT_Y, BIT_C = 8, 4, 2, 1
PIECE = 48
WIDE = 768
SCALE_ON = 1.0 / 0.9
MIB = 1024 * 1024
f32 = jnp.float32
bf16 = jnp.bfloat16


def hop(array, bit):
    return lax.ppermute(array, "fsdp", [(i, i ^ bit) for i in range(16)])


def swap(array):
    return lax.ppermute(array, "dp", [(0, 1), (1, 0)])


def cross(array):
    axes = ("dp", "fsdp")
    return lax.ppermute(array, axes, [(i, i ^ 16 ^ BIT_C) for i in range(32)])


def join(*arrays):
    return jnp.concatenate(arrays, axis=0)


def tie(array, *before):
    return lax.optimization_barrier((array,) + before)[0]


def to_other_core(own):
    return own + tuple(hop(part, BIT_C) for part in own)


def plus(left, right):
    return (left.astype(f32) + right.astype(f32)).astype(bf16)


def core_sums(own, came):
    return tuple(plus(own[a], came[a]) for a in range(4))


def first_hops(parts):
    return swap(parts[1]), hop(parts[3], BIT_Y)


def together(move, *arrays):
    flat = [array.reshape(-1, PIECE, 384) for array in arrays]
    came, at, out = move(join(*flat)), 0, []
    for array, part in zip(arrays, flat):
        out.append(came[at : at + part.shape[0]].reshape(array.shape))
        at += part.shape[0]
    return out


def hop_y(array):
    return hop(array, BIT_Y)


def first_sums(parts, got):
    return (
        plus(parts[0][:4], got[0][:4]),
        plus(parts[0][4:], got[0][4:]),
        plus(parts[2][:4], got[1][:4]),
        plus(parts[2][4:], got[1][4:]),
    )


def second_hops(parts):
    return hop(parts[1], BIT_Y), swap(parts[3])


def second_sums(parts, got):
    return tuple(
        jnp.stack([plus(parts[0][half], got[0][half]), plus(parts[2][half], got[1][half])])
        for half in (slice(0, 2), slice(2, 4))
    )


def third_hops(parts):
    return (hop(parts[1], BIT_Z0),)


def third_sums(parts, got):
    return plus(parts[0][:, 0], got[0][:, 0]), plus(parts[0][:, 1], got[0][:, 1])


def fourth_hops(parts):
    return (hop(parts[1], BIT_Z1),)


def fourth_sums(parts, got):
    return plus(parts[0], got[0])


def product(left, right, dims):
    return lax.dot_general(left, right, (dims, ((), ())), preferred_element_type=f32)


NN = ((1,), (0,))
NT = ((1,), (1,))
TN = ((0,), (0,))


def slot(line, xr, yr):
    return (xr, yr) if line == 0 else (2 + yr, xr)


def rel_places():
    return [(m, m & 1, (m >> 1) & 1, ((m >> 2) & 1) * 2 + (m >> 3)) for m in range(16)]


def rows_of(i, m):
    return pl.ds(pl.multiple_of((i ^ m) * PIECE, 16), PIECE)


def load_line(store, halves, i, columns=slice(None)):
    for m, c, yr, z in rel_places():
        ref, first = halves[c][yr]
        store[rows_of(i, m), columns] = ref[first + z, 0:PIECE, :]


def save_chunk(value, outs, i, line, xr):
    for m in range(16):
        c, yr, z0r, z1r = m & 1, (m >> 1) & 1, (m >> 2) & 1, (m >> 3) & 1
        array, part = slot(line, xr, yr) if isinstance(xr, int) else (2 + yr, xr)
        row = pl.multiple_of((i ^ m) * PIECE, 16)
        outs[c][array, part * 4 + z0r * 2 + z1r] = value[pl.ds(row, PIECE), :]


def row_facts(info, r):
    first = info[2 + 3 * r]
    second = first + info[3 + 3 * r]
    third = second + info[4 + 3 * r]

    def segment(shape, axis):
        t = lax.broadcasted_iota(jnp.int32, shape, axis)
        return (t >= first).astype(jnp.int32) + (t >= second).astype(jnp.int32) + (t >= third).astype(jnp.int32)

    column = segment((256, 1), 0)

    def scale(branch):
        keeps = [info[8 + 6 * r + 2 * j + branch].astype(f32) * SCALE_ON for j in range(3)]
        return jnp.where(
            column == 0, keeps[0], jnp.where(column == 1, keeps[1], jnp.where(column == 2, keeps[2], 0.0))
        )

    inside = jnp.where(column < 3, 1.0, 0.0).astype(f32)
    return column, segment((1, 256), 1), scale, inside


def unit_of(values):
    center = values - jnp.mean(values, axis=-1, keepdims=True)
    spread = jnp.mean(center * center, axis=-1, keepdims=True)
    root = lax.rsqrt(spread + EPSILON)
    return center * root, root


def unit_back(unit, root, gain, incoming):
    eg = incoming * gain
    return root * (
        eg - jnp.mean(eg, axis=-1, keepdims=True) - unit * jnp.mean(eg * unit, axis=-1, keepdims=True)
    )


def sums(values):
    return jnp.sum(values, axis=0, keepdims=True)


def load_direct(store, own, other, i, spots):
    for m in range(16):
        spot = spots[0] * (m >> 3) + spots[1] * (m >> 2 & 1) + spots[2] * (m >> 1 & 1)
        row = pl.multiple_of((i ^ m) * PIECE, 16)
        store[pl.ds(row, PIECE), :] = (other if m & 1 else own)[spot, 0:PIECE, :]


def prepare_kernel(info, qkv, fc1, fc2, *rest):
    vectors, (lead, *groups) = rest[:9], rest[9:]
    x = info[1]
    at = pl.multiple_of(WIDE + WIDE * x, 128)
    lead[0, 0:48, :] = qkv[:, pl.ds(at + 384, 384)]
    lead[0, 48:96, :] = qkv[:, pl.ds(pl.multiple_of(384 * x, 128), 384)]
    lead[0, 96:144, :] = qkv[:, pl.ds(at, 384)]
    rows = [v[...].astype(f32).reshape(1, -1) for v in vectors]
    rows = rows[:8] + [rows[8][:, 48 * k : 48 * k + 48] for k in range(4)]
    rows = [jnp.pad(row, ((0, 0), (0, 336))) for row in rows]
    lead[0, 144:160, :] = jnp.concatenate(rows + [jnp.zeros((4, 384), f32)]).astype(bf16)
    for half in range(2):

        @pl.when(x == half)
        def _():
            for s in range(2):
                first = 48 * (2 * half + s)
                cuts = [fc1[:, 192 * j + first : 192 * j + first + 48] for j in range(16)]
                groups[s][0] = jnp.concatenate(cuts, axis=1)
                groups[s][1] = fc2[first : first + 48, :]


def load_qkv(weight, refs, i, x):
    for xr in range(2):
        h = x ^ xr
        a = [[(refs[6 * c + xr], 4 * yr) for yr in range(2)] for c in range(2)]
        b = [[(refs[6 * c + 2 + yr], 4 * xr) for yr in range(2)] for c in range(2)]
        q = [[(refs[6 * c + 4 + xr], 4 * yr) for yr in range(2)] for c in range(2)]
        load_line(weight.at[1 + h], a, i, slice(0, 384))
        load_line(weight.at[1 + h], b, i, slice(384, 768))
        load_line(weight.at[0], q, i, pl.ds(pl.multiple_of(384 * h, 128), 384))


def qkv_kernel(info, tok, small, *rest):
    refs, (packed, normed, weight) = rest[:12], rest[12:]
    i, x = info[0], info[1]
    load_qkv(weight, refs, i, x)
    for r in range(2):
        rows = slice(256 * r, 256 * r + 256)
        unit, _ = unit_of(tok[rows, :].astype(f32))
        normed[rows, :] = (unit * small[0:1, :] + small[1:2, :]).astype(bf16)
    for r in range(2):
        rows = slice(256 * r, 256 * r + 256)
        low = normed[rows, :]
        packed[rows, 0:768] = (product(low, weight[0], NN) + small[2:3, :]).astype(bf16)
        packed[rows, 768:1536] = product(low, weight[1], NN).astype(bf16)
        packed[rows, 1536:2304] = (product(low, weight[2], NN) + small[3:4, :]).astype(bf16)


def attend_kernel(info, packed, cot, attended, grad_two, lse, scores, weighting):
    r = pl.program_id(0)
    column, across, scale, inside = row_facts(info, r)
    same = column == across
    lane = lax.broadcasted_iota(jnp.int32, (256, 128), 1)
    kept = jnp.zeros((256, 128), f32)
    for g in range(HEADS):
        query = packed[:, 64 * g : 64 * g + 64] * 0.125
        scores[g] = product(query, packed[:, 768 + 64 * g : 832 + 64 * g], NT)
    for g in range(HEADS):
        masked = jnp.where(same, scores[g], NEGATIVE)
        top = jnp.max(masked, axis=-1, keepdims=True)
        raised = jnp.exp(masked - top)
        total = jnp.sum(raised, axis=-1, keepdims=True)
        weighting[g] = (raised * (1.0 / total)).astype(bf16)
        kept = jnp.where(lane == g, top + jnp.log(total), kept)
    lse[...] = kept
    for h in range(0, HEADS, 2):
        pair = [
            product(weighting[g], packed[:, 1536 + 64 * g : 1600 + 64 * g], NN).astype(bf16)
            for g in (h, h + 1)
        ]
        attended[:, 64 * h : 64 * h + 128] = jnp.concatenate(pair, axis=1)
    grad_two[...] = (cot[...].astype(f32) * inside * scale(1)).astype(bf16)


def hidden_units(block, normed, turned, grad_two, small, branch, grad_normed, bias, weights, scratch):
    active, low = scratch[:2]
    for r in range(2):
        rows = slice(256 * r, 256 * r + 256)
        value = product(normed[rows, :], weights[0], NN) + small[pl.ds(8 + block, 1), :]
        share = 0.5 * (1.0 + lax.erf(value * (0.5**0.5)))
        active[rows, :] = (value * share).astype(bf16)
        slope = share + value * (jnp.exp(-0.5 * value * value) * 0.3989422804014327)
        low[rows, :] = (product(grad_two[rows, :], weights[1], NT) * slope).astype(bf16)
    bias[pl.ds(8 + block, 1), :] = sums(low[...].astype(f32))
    for r in range(2):
        rows = slice(256 * r, 256 * r + 256)
        branch[rows, :] += product(active[rows, :], weights[1], NN)
        grad_normed[rows, :] += product(low[rows, :], weights[0], NT)
    scratch[2][...] = product(turned[...], low[...], NN).astype(bf16)
    scratch[3][...] = product(active[...], grad_two[...], TN).astype(bf16)


def load_units(scratch, refs, i, t):
    for step in range(2):

        @pl.when(t == step)
        def _():
            up = [[(refs[4 * c + step], 4 * yr) for yr in range(2)] for c in range(2)]
            down = [[(refs[4 * c + 2 + yr], 4 * step) for yr in range(2)] for c in range(2)]
            load_line(scratch[4], up, i)
            load_line(scratch[5], down, i)

    return scratch[4][...], scratch[5][...]


def save_units(scratch, own, away, i, t):
    for m, c, yr, z in rel_places():
        for part in range(2):
            here = slice(384 * part, 384 * part + 384)
            (own, away)[c][t, 4 * yr + z, part] = scratch[2][rows_of(i, m), here]
            (own, away)[c][2 + yr, 4 * t + z, part] = scratch[3][rows_of(i, m), here]


def first_units_kernel(xr, info, left, grad_two, small, *rest):
    refs, rest = rest[:6], rest[6:]
    i, x = info[0], info[1]
    if xr == 0:
        tok, proj_own, proj_other, middle, normed, turned, branch, grad_normed, bias, own, away, proj = rest[:12]
        scratch = rest[12:]
        load_direct(proj, proj_own, proj_other, i, (2, 4, 1))
        for r in range(2):
            rows = slice(256 * r, 256 * r + 256)
            _, _, scale, _ = row_facts(info, r)
            after = tok[rows, :].astype(f32) + scale(0) * (
                product(left[rows, :], proj[...], NN) + small[4:5, :]
            )
            middle[rows, :] = after
            unit, _ = unit_of(after)
            normed[rows, :] = (unit * small[5:6, :] + small[6:7, :]).astype(bf16)
        turned[...] = normed[...].T
        branch[...] = jnp.zeros_like(branch)
        grad_normed[...] = jnp.zeros_like(grad_normed)
        bias[...] = jnp.zeros_like(bias)
        bias[7:8, :] = sums(grad_two[...].astype(f32))
    else:
        turned, branch_in, grad_normed_in, bias_in, branch, grad_normed, bias, own, away, *scratch = rest
        normed = left
        branch[...] = branch_in[...]
        grad_normed[...] = grad_normed_in[...]
        bias[...] = bias_in[...]
    load_line(scratch[4], [[(refs[c], 4 * yr) for yr in range(2)] for c in range(2)], i)
    load_line(scratch[5], [[(refs[2 + 2 * c + yr], 0) for yr in range(2)] for c in range(2)], i)
    weights = (scratch[4][...], scratch[5][...])
    hidden_units(2 * (x ^ xr), normed, turned, grad_two, small, branch, grad_normed, bias, weights, scratch)
    for m, c, yr, z in rel_places():
        for part in range(2):
            here = slice(384 * part, 384 * part + 384)
            for k in range(2):
                (own, away)[c][k, 4 * yr + z, part] = scratch[2 + k][rows_of(i, m), here]


def second_units_kernel(
    info, normed, turned, grad_two, small, branch_in, grad_normed_in, bias_in, middle, cot, *rest
):
    refs, (result, grad_middle, grad_one, bias, own, away, branch, grad_normed, *scratch) = rest[:8], rest[8:]
    i, x, t = info[0], info[1], pl.program_id(0)

    @pl.when(t == 0)
    def _():
        branch[...] = branch_in[...]
        grad_normed[...] = grad_normed_in[...]
        bias[...] = bias_in[...]

    weights = load_units(scratch, refs, i, t)
    hidden_units(2 * (t ^ x) + 1, normed, turned, grad_two, small, branch, grad_normed, bias, weights, scratch)
    save_units(scratch, own, away, i, t)

    @pl.when(t == 1)
    def _():
        for r in range(2):
            rows = slice(256 * r, 256 * r + 256)
            _, _, scale, inside = row_facts(info, r)
            after = middle[rows, :]
            result[rows, :] = (
                (after + scale(1) * (branch[rows, :] + small[7:8, :])) * inside
            ).astype(bf16)
            unit, root = unit_of(after)
            incoming = grad_normed[rows, :]
            bias[5:6, :] += sums(incoming * unit)
            bias[6:7, :] += sums(incoming)
            total = cot[rows, :].astype(f32) * inside + unit_back(unit, root, small[5:6, :], incoming)
            grad_middle[rows, :] = total
            low_one = (total * scale(0)).astype(bf16)
            grad_one[rows, :] = low_one
            bias[4:5, :] += sums(low_one.astype(f32))


def attend_back_kernel(group, info, queries, keys, values, lse, attended, grad_one, normed, *rest):
    if group == 0:
        proj_own, proj_other, grad_packed, own, away, weight, proj_rest, grad, *heads, total = rest
    else:
        weight, proj_rest, grad_packed, own, away, grad, *heads = rest
    i, x, r = info[0], info[1], pl.program_id(0)
    if group == 0:

        @pl.when(r == 0)
        def _():
            load_direct(weight, proj_own, proj_other, i, (2, 4, 1))
            total[...] = jnp.zeros_like(total)

        total[...] += product(attended[...], grad_one[...], TN)

    column, across, _, _ = row_facts(info, r)
    same = column == across
    grad_attended = product(grad_one[...], weight[384 * group : 384 * group + 384, :], NT).astype(bf16)
    rows = pl.ds(pl.multiple_of(r * 256, 256), 256)
    scores, backs, lows, highs = heads
    queried = [queries[:, 64 * g : 64 * g + 64] * 0.125 for g in range(6)]
    returned = [grad_attended[:, 64 * g : 64 * g + 64] for g in range(6)]
    for g in range(6):
        here = slice(64 * g, 64 * g + 64)
        scores[g] = product(queried[g], keys[:, here], NT)
        backs[g] = product(returned[g], values[:, here], NT)
    for g in range(6):
        head = 6 * group + g
        weighting = jnp.where(same, jnp.exp(scores[g] - lse[:, head : head + 1]), 0.0)
        highs[g] = weighting.astype(bf16)
        share = backs[g] * weighting
        inner = jnp.sum(share, axis=-1, keepdims=True)
        lows[g] = (share - weighting * inner).astype(bf16)
    for h in range(0, 6, 2):
        pairs = ([], [], [])
        for g in (h, h + 1):
            pairs[0].append(product(lows[g], keys[:, 64 * g : 64 * g + 64], NN) * 0.125)
            pairs[1].append(product(lows[g], queried[g], TN))
            pairs[2].append(product(highs[g], returned[g], TN))
        for k in range(3):
            grad_packed[rows, 384 * k + 64 * h : 384 * k + 64 * h + 128] = jnp.concatenate(
                pairs[k], axis=1
            ).astype(bf16)

    @pl.when(r == 1)
    def _():
        turned = normed[...].T
        grad[1, 0] = product(turned, grad_packed[:, 0:384], NN).astype(bf16)
        grad[0, 0] = product(turned, grad_packed[:, 384:768], NN).astype(bf16)
        grad[0, 1] = product(turned, grad_packed[:, 768:1152], NN).astype(bf16)
        if group == 0:
            grad[1, 1] = total[:, 0:384].astype(bf16)
            proj_rest[...] = total[:, 384:768].astype(bf16)
        else:
            grad[1, 1] = proj_rest[...]
        for line in range(2):
            for xr in range(2):
                save_chunk(grad.at[line, x ^ xr], (own, away), i, line, xr)


def tokens_back_kernel(r, info, tok, back0, back1, grad_middle, bias_in, small, *rest):
    refs, (tokens_grad, bias, weight) = rest[:12], rest[-3:]
    i, x = info[0], info[1]
    load_qkv(weight, refs, i, x)
    bias[...] = bias_in[...]
    for part, back in ((0, back0), (1, back1)):
        columns = slice(384 * part, 384 * part + 384)
        bias[2:3, columns] += sums(back[:, 0:384].astype(f32))
        bias[3:4, columns] += sums(back[:, 768:1152].astype(f32))
    incoming = jnp.zeros((256, WIDE), f32)
    for k in range(3):
        here = slice(384 * k, 384 * k + 384)
        joined = jnp.concatenate([back0[:, here], back1[:, here]], axis=1)
        incoming += product(joined, weight[k], NT)
    unit, root = unit_of(tok[...].astype(f32))
    bias[0:1, :] += sums(incoming * unit)
    bias[1:2, :] += sums(incoming)
    tokens_grad[...] = grad_middle[...] + unit_back(unit, root, small[0:1, :], incoming)


def results_kernel(info, mine0, other0, mine1, other1, bias, qkv, proj, *vectors):
    i, x = info[0], info[1]
    for group, mine, other in ((0, mine0, other0), (1, mine1, other1)):
        for line, half, column in ((1, 0, 0), (0, 0, 768), (0, 1, 1536), (1, 1, None)):
            a, b = mine[line].astype(f32), other[line].astype(f32)
            value = jnp.where(x == half, a, b)
            if column is None:
                proj[:, 384 * group : 384 * group + 384] = value
            else:
                qkv[:, column + 384 * group : column + 384 * group + 384] = value

    def cut(rows, start, width):
        feature = lax.broadcasted_iota(jnp.int32, (WIDE, width), 0)
        lane = lax.broadcasted_iota(jnp.int32, (WIDE, width), 1)
        chosen = (feature == lane + start).astype(f32)
        return lax.dot_general(
            rows, chosen, (NN, ((), ())), precision=lax.Precision.HIGHEST, preferred_element_type=f32
        )

    narrow = cut(bias[...], i * 48, 128)
    for k in range(8):
        vectors[k][...] = narrow[k, 0:48]
    broad = jnp.concatenate([narrow[8 + k : 9 + k, 0:48] for k in range(4)], axis=1)
    vectors[8][...] = broad[0]


def units_results_kernel(info, mine0, other0, mine1, other1, fc1, fc2):
    x = info[1]
    blocks = []
    for half in range(2):
        for mine, other in ((mine0, other0), (mine1, other1)):
            pieces = [
                jnp.concatenate(
                    [jnp.where(x == half, mine[k, p].astype(f32), other[k, p].astype(f32)) for p in range(2)],
                    axis=1,
                )
                for k in range(2)
            ]
            fc2[48 * len(blocks) : 48 * len(blocks) + 48, :] = pieces[1]
            blocks.append(pieces[0])
    for j in range(0, 16, 2):
        cuts = [b[:, 48 * k : 48 * k + 48] for k in (j, j + 1) for b in blocks]
        fc1[:, 192 * j : 192 * j + 384] = jnp.concatenate(cuts, axis=1)


def whole(shape):
    return pl.BlockSpec(shape, lambda *_: (0,) * len(shape))


def once(shape):
    return pl.BlockSpec(shape, lambda *_: (0,) * len(shape), pipeline_mode=pl.Buffered(1))


def rowwise(width):
    return pl.BlockSpec((256, width), lambda r, info: (r, 0))


def run_kernel(kernel, grid, info, operands, outs, scratch, microseconds, vmem, alias=None):
    return pl.pallas_call(
        kernel,
        grid_spec=pltpu.PrefetchScalarGridSpec(
            num_scalar_prefetch=1,
            grid=(grid,),
            in_specs=[spec or once(array.shape) for spec, array in operands],
            out_specs=[spec or whole(shape) for spec, shape, _ in outs],
            scratch_shapes=[pltpu.VMEM(shape, dtype) for shape, dtype in scratch],
        ),
        out_shape=[jax.ShapeDtypeStruct(shape, dtype) for _, shape, dtype in outs],
        input_output_aliases=alias or {},
        compiler_params=pltpu.CompilerParams(
            dimension_semantics=("arbitrary",), vmem_limit_bytes=vmem * MIB
        ),
        cost_estimate=pl.CostEstimate(
            flops=int(microseconds * 1.15e9), bytes_accessed=1 << 20, transcendentals=0
        ),
    )(info, *[array for _, array in operands])


def fast_device(
    tokens,
    lengths,
    keep_mask,
    cotangent,
    ln1_gain,
    ln1_bias,
    qkv_weight,
    q_bias,
    v_bias,
    proj_weight,
    proj_bias,
    ln2_gain,
    ln2_bias,
    fc1_weight,
    fc1_bias,
    fc2_weight,
    fc2_bias,
):
    count = tokens.shape[0] * tokens.shape[1]
    i = lax.axis_index("fsdp")
    x = lax.axis_index("dp")
    info = jnp.concatenate(
        [jnp.stack([i, x]).astype(jnp.int32), lengths.reshape(-1), keep_mask.reshape(-1)]
    )
    tok = tokens.reshape(count, WIDE)
    cot = cotangent.reshape(count, WIDE)

    def full(*arrays):
        return [(None, array) for array in arrays]

    vectors = (ln1_gain, ln1_bias, q_bias, v_bias, proj_bias, ln2_gain, ln2_bias, fc2_bias, fc1_bias)
    lead, units0, units1 = run_kernel(
        prepare_kernel,
        1,
        jnp.stack([i, x]),
        full(qkv_weight, fc1_weight, fc2_weight, *vectors),
        [(None, (1, 160, 384), bf16), (None, (2, PIECE, WIDE), bf16), (None, (2, PIECE, WIDE), bf16)],
        [],
        2,
        60,
    )

    proj = tie(proj_weight[None], lead)
    proj = join(proj, hop(proj, BIT_Y))

    pair = join(lead, hop(lead, BIT_Z1))
    far = hop(pair, BIT_Z0)
    line_b, line_q, line_a = (join(pair[:, k], far[:, k]) for k in (slice(0, 48), slice(48, 96), slice(96, 160)))
    line_a, line_b, line_q, units0 = lax.optimization_barrier((line_a, line_b, line_q, units0))
    got_a, got_b, got_q = hop(line_a, BIT_Y), swap(line_b), hop(line_q, BIT_Y)
    units_far = hop(units0, BIT_Z1)
    got_a, got_b = lax.optimization_barrier((got_a, got_b))
    wide_a, wide_b = join(line_a, got_a), join(line_b, got_b)
    got_a, got_b = swap(wide_a[:, :PIECE]), hop(wide_b, BIT_Y)
    wide_q = join(line_q, got_q)
    got_q = swap(wide_q)
    units_far = tie(units_far, wide_a, wide_b)
    units0 = jnp.stack([units0, units_far], axis=1)
    units_far = hop(units0, BIT_Z0)
    proj = tie(proj, wide_a, wide_b, units0)
    proj_far = hop(proj, BIT_Z1)
    got_a, got_b, got_q, units_far, units1, proj_far = lax.optimization_barrier(
        (got_a, got_b, got_q, units_far, units1, proj_far)
    )
    first = to_other_core((wide_a, got_a, wide_b, got_b, wide_q, got_q))

    units_line = join(units0[0], units_far[0]), join(units0[1], units_far[1])
    units_got = hop(units_line[0], BIT_Y), swap(units_line[1])
    next_far = hop(units1, BIT_Z1)
    proj = join(proj, proj_far)
    proj_far = hop(proj, BIT_Z0)

    vectors = jnp.concatenate([first[k][:, PIECE : PIECE + 12, :PIECE] for k in (0, 6)])
    origin = jnp.array([(p & 1) * 8 + (p >> 1 & 1) * 4 + (p >> 2 & 1) * 2 + (p >> 3) for p in range(16)])
    turned = jnp.arange(16)[:, None] == (origin ^ i)[None, :]
    vectors = jnp.einsum("mp,pkl->kml", turned.astype(bf16), vectors, preferred_element_type=f32)
    small = jnp.concatenate([vectors.reshape(12, WIDE), jnp.zeros((4, WIDE), f32)])

    packed, normed_one = run_kernel(
        qkv_kernel,
        1,
        info,
        full(tok, small, *first),
        [(None, (count, 3 * WIDE), bf16), (None, (count, WIDE), bf16)],
        [((3, WIDE, WIDE), bf16)],
        5,
        40,
    )

    units_got, next_far, proj_far, _ = lax.optimization_barrier((units_got, next_far, proj_far, packed))
    units_wide = tuple(join(line, got) for line, got in zip(units_line, units_got))
    units_got = swap(units_wide[0]), hop(units_wide[1], BIT_Y)
    units1 = jnp.stack([units1, next_far], axis=1)
    next_far = hop(units1, BIT_Z0)
    proj = join(proj, proj_far)
    proj_other = hop(proj, BIT_C)

    attended, grad_two, lse = run_kernel(
        attend_kernel,
        2,
        tie(info, *units_wide, units1, proj),
        [(rowwise(3 * WIDE), packed), (rowwise(WIDE), cot)],
        [
            (rowwise(WIDE), (count, WIDE), bf16),
            (rowwise(WIDE), (count, WIDE), bf16),
            (rowwise(128), (count, 128), f32),
        ],
        [((HEADS, 256, 256), f32), ((HEADS, 256, 256), bf16)],
        6,
        40,
    )

    units_got, next_far, proj_other, _ = lax.optimization_barrier((units_got, next_far, proj_other, lse))
    units = to_other_core((units_wide[0], units_got[0], units_wide[1], units_got[1]))
    next_line = tuple(join(units1[k], next_far[k]) for k in range(2))
    next_got = hop(next_line[0], BIT_Y), swap(next_line[1])

    wide_f32 = (None, (count, WIDE), f32)
    wide_bf16 = (None, (count, WIDE), bf16)
    vectors_f32 = (None, (16, WIDE), f32)
    parts = (None, (4, 8, 2, PIECE, 384), bf16)
    half = (None, (2, 8, 2, PIECE, 384), bf16)
    unit_scratch = [((count, WIDE), bf16)] * 2 + [((WIDE, WIDE), bf16)] * 4

    def first_units(xr, info, left, more, outs, scratch):
        part = pl.BlockSpec((4, PIECE, WIDE), lambda _, __: (xr, 0, 0))
        return run_kernel(
            functools.partial(first_units_kernel, xr),
            1,
            info,
            full(left, grad_two, small, units[xr], units[4 + xr])
            + [(part, units[k]) for k in (2, 3, 6, 7)]
            + full(*more),
            outs + [wide_f32, wide_f32, vectors_f32, half, half],
            scratch + unit_scratch,
            7,
            40,
        )

    middle, normed_two, turned_two, branch, grad_normed, bias, own0, away0 = first_units(
        0,
        tie(info, *next_line),
        attended,
        (tok, proj, proj_other),
        [wide_f32, wide_bf16, (None, (WIDE, count), bf16)],
        [((WIDE, WIDE), bf16)],
    )
    next_got, bias, away0 = lax.optimization_barrier((next_got, bias, away0))
    next_wide = tuple(join(line, got) for line, got in zip(next_line, next_got))
    next_got = swap(next_wide[0]), hop(next_wide[1], BIT_Y)
    came0 = hop(away0, BIT_C)
    branch, grad_normed, bias, own1, away1 = first_units(
        1, tie(info, *next_wide), normed_two, (turned_two, branch, grad_normed, bias), [], []
    )
    next_got, came0, bias, away1 = lax.optimization_barrier((next_got, came0, bias, away1))
    units = to_other_core((next_wide[0], next_got[0], next_wide[1], next_got[1]))
    came1 = hop(away1, BIT_C)
    two = (
        plus(own0[0], came0[0]),
        plus(own1[0], came1[0]),
        join(plus(own0[1, :4], came0[1, :4]), plus(own1[1, :4], came1[1, :4])),
        join(plus(own0[1, 4:], came0[1, 4:]), plus(own1[1, 4:], came1[1, 4:])),
    )
    two_got = first_hops(two)
    output, grad_middle, grad_one, bias, units_own, units_away = run_kernel(
        second_units_kernel,
        2,
        tie(info, *two),
        full(normed_two, turned_two, grad_two, small, branch, grad_normed, bias, middle, cot, *units),
        [wide_bf16, wide_f32, wide_bf16, vectors_f32, parts, parts],
        [((count, WIDE), f32)] * 2 + unit_scratch,
        15,
        40,
    )

    def attend_back(group, info, more, outs, scratch):
        def columns(k):
            return pl.BlockSpec((256, 384), lambda r, _, at=2 * k + group: (r, at))

        narrow = (4, 8, PIECE, 384)
        return run_kernel(
            functools.partial(attend_back_kernel, group),
            2,
            info,
            [(columns(k), packed) for k in range(3)]
            + [(rowwise(128), lse), (rowwise(WIDE), attended), (rowwise(WIDE), grad_one)]
            + full(normed_one, *more),
            [(None, (count, 1152), bf16), (None, narrow, bf16), (None, narrow, bf16)] + outs,
            [((2, 2, WIDE, 384), bf16)]
            + [((6, 256, 256), f32)] * 2
            + [((6, 256, 256), bf16)] * 2
            + scratch,
            8,
            40,
        )

    two_got, bias, units_away = lax.optimization_barrier((two_got, bias, units_away))
    two = first_sums(two, two_got)
    two_got, one_came = second_hops(two), hop(units_away, BIT_C)
    back0, head_own0, head_away0, proj_full, proj_rest = attend_back(
        0,
        tie(info, *two),
        (proj, proj_other),
        [(None, (WIDE, WIDE), bf16), (None, (WIDE, 384), bf16)],
        [((WIDE, WIDE), f32)],
    )

    two_got, one_came, proj_rest, head_away0 = lax.optimization_barrier(
        (two_got, one_came, proj_rest, head_away0)
    )
    two = second_sums(two, two_got)
    one = core_sums(units_own, one_came)
    one_got, two_got, zero_came = first_hops(one), third_hops(two), hop(head_away0, BIT_C)
    back1, head_own1, head_away1 = attend_back(1, tie(info, *two, *one), (proj_full, proj_rest), [], [])

    two_got, one_got, zero_came, head_away1 = lax.optimization_barrier(
        (two_got, one_got, zero_came, head_away1)
    )
    two, one, zero = third_sums(two, two_got), first_sums(one, one_got), core_sums(head_own0, zero_came)
    last_came = hop(head_away1, BIT_C)
    zero_got, one_got = first_hops(zero), second_hops(one)

    def tokens_back(r, info, more, alias):
        def row(width):
            return pl.BlockSpec((256, width), lambda _, __: (r, 0))

        return run_kernel(
            functools.partial(tokens_back_kernel, r),
            1,
            info,
            [(row(WIDE), tok), (row(1152), back0), (row(1152), back1), (row(WIDE), grad_middle)]
            + full(bias, small, *first)
            + more,
            [(row(WIDE), (count, WIDE), f32), (None, (16, WIDE), f32)],
            [((3, WIDE, WIDE), bf16)],
            5,
            40,
            alias,
        )

    tokens_grad, bias = tokens_back(0, tie(info, *two, *one, *zero), [], {})

    zero_got, one_got, last_came, bias = lax.optimization_barrier((zero_got, one_got, last_came, bias))
    last, zero, one = core_sums(head_own1, last_came), first_sums(zero, zero_got), second_sums(one, one_got)
    two_got, one_got = fourth_hops(two), third_hops(one)
    got_x, got_y = together(swap, last[1], zero[3]), together(hop_y, last[3], zero[1])
    last_got, zero_got = (got_x[0], got_y[0]), (got_y[1], got_x[1])
    tokens_grad, bias = tokens_back(
        1, tie(info, *last, *zero, *one), [(pl.BlockSpec(memory_space=pl.ANY), tokens_grad)], {19: 0}
    )

    last_got, zero_got, two_got, one_got, bias = lax.optimization_barrier(
        (last_got, zero_got, two_got, one_got, bias)
    )
    last, zero, two, one = (
        first_sums(last, last_got),
        second_sums(zero, zero_got),
        fourth_sums(two, two_got),
        third_sums(one, one_got),
    )
    last_got, zero_got, one_got, bias_got = lax.optimization_barrier(
        (second_hops(last), third_hops(zero), fourth_hops(one), hop(bias, BIT_Y))
    )
    last, one, zero = second_sums(last, last_got), fourth_sums(one, one_got), third_sums(zero, zero_got)
    bias = bias + bias_got
    last_got, zero_got, got, bias_got = lax.optimization_barrier(
        (third_hops(last), fourth_hops(zero), together(swap, one, two), hop(bias, BIT_Z0))
    )
    one_other, two_other = got
    last, zero, bias = third_sums(last, last_got), fourth_sums(zero, zero_got), bias + bias_got
    last_got, zero_other, bias_got = lax.optimization_barrier(
        (fourth_hops(last), swap(zero), hop(bias, BIT_Z1))
    )
    last, bias = fourth_sums(last, last_got), bias + bias_got
    last_other, bias_got = swap(last), (swap(bias), hop(bias, BIT_C), cross(bias))
    fc1_grad, fc2_grad = run_kernel(
        units_results_kernel,
        1,
        info,
        full(two, two_other, one, one_other),
        [(None, (PIECE, 4 * WIDE), f32), (None, (4 * PIECE, WIDE), f32)],
        [],
        3,
        40,
    )
    bias = (bias + bias_got[0]) + (bias_got[1] + bias_got[2])
    qkv_grad, proj_grad, *narrow = run_kernel(
        results_kernel,
        1,
        info,
        full(zero, zero_other, last, last_other, bias),
        [(None, (PIECE, 3 * WIDE), f32), (None, (PIECE, WIDE), f32)]
        + [(None, (48,), f32)] * 8
        + [(None, (192,), f32)],
        [],
        3,
        40,
    )
    return (
        output.reshape(tokens.shape),
        tokens_grad.reshape(tokens.shape),
        narrow[0],
        narrow[1],
        qkv_grad,
        narrow[2],
        narrow[3],
        proj_grad,
        narrow[4],
        narrow[5],
        narrow[6],
        fc1_grad,
        narrow[8],
        fc2_grad,
        narrow[7],
    )


def solution(mesh):
    in_specs = (
        P(("dp", "fsdp"), None, None),
        P(("dp", "fsdp"), None),
        P(("dp", "fsdp"), None, None),
        P(("dp", "fsdp"), None, None),
        P("fsdp"),
        P("fsdp"),
        P("fsdp", None),
        P("fsdp"),
        P("fsdp"),
        P("fsdp", None),
        P("fsdp"),
        P("fsdp"),
        P("fsdp"),
        P("fsdp", None),
        P("fsdp"),
        P("fsdp", None),
        P("fsdp"),
    )
    out_specs = (
        P(("dp", "fsdp"), None, None),
        P(("dp", "fsdp"), None, None),
        P("fsdp"),
        P("fsdp"),
        P("fsdp", None),
        P("fsdp"),
        P("fsdp"),
        P("fsdp", None),
        P("fsdp"),
        P("fsdp"),
        P("fsdp"),
        P("fsdp", None),
        P("fsdp"),
        P("fsdp", None),
        P("fsdp"),
    )
    fits = mesh.shape["dp"] == 2 and mesh.shape["fsdp"] == 16
    return jax.shard_map(
        fast_device if fits else per_device, mesh=mesh, in_specs=in_specs, out_specs=out_specs, check_vma=False
    )
```

```python
import functools

import jax
import jax.numpy as jnp
from jax import lax
from jax.experimental import pallas as pl
from jax.experimental.pallas import tpu as pltpu
from jax.sharding import PartitionSpec as P

HEADS = 12


EPSILON = 1e-06
KEEP_RATE = 0.9
NEGATIVE = -1e30


def normalize(values, gain, shift):
    center = values - jnp.mean(values, axis=-1, keepdims=True)
    spread = jnp.mean(center * center, axis=-1, keepdims=True)
    return center * lax.rsqrt(spread + EPSILON) * gain + shift


def standardize(values):
    center = values - jnp.mean(values, axis=-1, keepdims=True)
    spread = jnp.mean(center * center, axis=-1, keepdims=True)
    return center * lax.rsqrt(spread + EPSILON)


def affine_low(unit_values, gain, shift):
    return (unit_values * gain.astype(jnp.float32) + shift.astype(jnp.float32)).astype(jnp.bfloat16)


def exact_gelu(values):
    return jax.nn.gelu(values, approximate=False)


def norm_back(values, gain, shift, incoming):
    _, pullback = jax.vjp(normalize, values, gain, shift)
    return pullback(incoming)


def inner_rows(left, right):
    return lax.dot_general(
        left, right, (((0,), (0,)), ((), ())), preferred_element_type=jnp.float32
    )


def times_transpose(left, right):
    return lax.dot_general(
        left, right, (((1,), (1,)), ((), ())), preferred_element_type=jnp.float32
    )


def layout(lengths, keep_mask, length):
    image_ends = jnp.cumsum(lengths, axis=-1, dtype=jnp.int32)
    position = jnp.arange(length, dtype=jnp.int32)
    segment = jnp.sum(
        (position[None, :, None] >= image_ends[:, None, :]).astype(jnp.int32),
        axis=-1,
        dtype=jnp.int32,
    )
    images = jnp.arange(lengths.shape[1], dtype=jnp.int32)
    member = (segment[:, :, None] == images[None, None, :]).astype(jnp.float32)
    keeping = keep_mask.astype(jnp.float32)
    scales = jnp.sum(member[:, :, :, None] * keeping[:, None, :, :], axis=2) / KEEP_RATE
    inside = jnp.sum(member, axis=-1)
    return (segment, scales, inside)


def attention_forward(packed, segment, rowset, length, head_size):
    split_view = packed.reshape(rowset, length, 3, HEADS, head_size)
    queries = split_view[:, :, 0]
    keys_all = split_view[:, :, 1]
    values_all = split_view[:, :, 2]
    scores = jnp.einsum(
        "rqhd,rkhd->rhqk", queries, keys_all, preferred_element_type=jnp.float32
    ) * head_size ** (-0.5)
    matching = segment[:, :, None] == segment[:, None, :]
    scores = jnp.where(matching[:, None], scores, NEGATIVE)
    raised = jnp.exp(scores - jnp.max(scores, axis=-1, keepdims=True))
    weighting = raised / jnp.sum(raised, axis=-1, keepdims=True)
    weighting_low = weighting.astype(jnp.bfloat16)
    attended = jnp.einsum(
        "rhqk,rkhd->rqhd", weighting_low, values_all, preferred_element_type=jnp.float32
    )
    attended = attended.reshape(rowset * length, HEADS * head_size).astype(jnp.bfloat16)
    return (queries, keys_all, values_all, weighting, weighting_low, attended)


def per_device(
    tokens,
    lengths,
    keep_mask,
    cotangent,
    ln1_gain,
    ln1_bias,
    qkv_weight,
    q_bias,
    v_bias,
    proj_weight,
    proj_bias,
    ln2_gain,
    ln2_bias,
    fc1_weight,
    fc1_bias,
    fc2_weight,
    fc2_bias,
):
    rowset, length, features = tokens.shape
    head_size = features // HEADS
    token_count = rowset * length
    segment, scales, inside = layout(lengths, keep_mask, length)
    scale_one = scales[:, :, 0].reshape(token_count, 1)
    scale_two = scales[:, :, 1].reshape(token_count, 1)
    inside_column = inside.reshape(token_count, 1)
    flattened = tokens.reshape(token_count, features).astype(jnp.float32)
    unit_one = standardize(flattened)
    qkv_full, proj_full, gain_one, shift_one, query_bias, value_bias, out_bias = (
        lax.all_gather(qkv_weight, "fsdp", axis=0, tiled=True),
        lax.all_gather(proj_weight, "fsdp", axis=0, tiled=True),
        lax.all_gather(ln1_gain, "fsdp", axis=0, tiled=True),
        lax.all_gather(ln1_bias, "fsdp", axis=0, tiled=True),
        lax.all_gather(q_bias, "fsdp", axis=0, tiled=True),
        lax.all_gather(v_bias, "fsdp", axis=0, tiled=True),
        lax.all_gather(proj_bias, "fsdp", axis=0, tiled=True),
    )
    normed_one = affine_low(unit_one, gain_one, shift_one)
    bias_all = jnp.concatenate(
        [
            query_bias.astype(jnp.float32),
            jnp.zeros((features,), jnp.float32),
            value_bias.astype(jnp.float32),
        ]
    )
    packed = (jnp.dot(normed_one, qkv_full, preferred_element_type=jnp.float32) + bias_all).astype(
        jnp.bfloat16
    )
    _, _, _, _, _, attended = attention_forward(packed, segment, rowset, length, head_size)
    branch_one = jnp.dot(attended, proj_full, preferred_element_type=jnp.float32) + out_bias.astype(
        jnp.float32
    )
    middle = flattened + scale_one * branch_one
    unit_two = standardize(middle)
    up_full, down_full, gain_two, shift_two, up_bias, down_bias = (
        lax.all_gather(fc1_weight, "fsdp", axis=0, tiled=True),
        lax.all_gather(fc2_weight, "fsdp", axis=0, tiled=True),
        lax.all_gather(ln2_gain, "fsdp", axis=0, tiled=True),
        lax.all_gather(ln2_bias, "fsdp", axis=0, tiled=True),
        lax.all_gather(fc1_bias, "fsdp", axis=0, tiled=True),
        lax.all_gather(fc2_bias, "fsdp", axis=0, tiled=True),
    )
    normed_two = affine_low(unit_two, gain_two, shift_two)
    hidden = jnp.dot(normed_two, up_full, preferred_element_type=jnp.float32) + up_bias.astype(
        jnp.float32
    )
    active = exact_gelu(hidden).astype(jnp.bfloat16)
    branch_two = jnp.dot(active, down_full, preferred_element_type=jnp.float32) + down_bias.astype(
        jnp.float32
    )
    output = (
        ((middle + scale_two * branch_two) * inside_column)
        .astype(jnp.bfloat16)
        .reshape(rowset, length, features)
    )
    up_full, down_full = (
        lax.all_gather(fc1_weight, "fsdp", axis=0, tiled=True),
        lax.all_gather(fc2_weight, "fsdp", axis=0, tiled=True),
    )
    gain_two_f = gain_two.astype(jnp.float32)
    shift_two_f = shift_two.astype(jnp.float32)
    grad_out = cotangent.reshape(token_count, features).astype(jnp.float32) * inside_column
    grad_two_low = (grad_out * scale_two).astype(jnp.bfloat16)
    fc2_grad = inner_rows(active, grad_two_low)
    fc2_bias_part = jnp.sum(grad_two_low.astype(jnp.float32), axis=0)
    grad_active = times_transpose(grad_two_low, down_full)
    _, gelu_pull = jax.vjp(exact_gelu, hidden)
    grad_hidden_low = gelu_pull(grad_active)[0].astype(jnp.bfloat16)
    fc1_grad = inner_rows(normed_two, grad_hidden_low)
    fc1_bias_part = jnp.sum(grad_hidden_low.astype(jnp.float32), axis=0)
    grad_normed_two = times_transpose(grad_hidden_low, up_full)
    grad_middle_norm, gain_two_part, shift_two_part = norm_back(
        middle, gain_two_f, shift_two_f, grad_normed_two
    )
    grad_middle = grad_out + grad_middle_norm
    qkv_full, proj_full = (
        lax.all_gather(qkv_weight, "fsdp", axis=0, tiled=True),
        lax.all_gather(proj_weight, "fsdp", axis=0, tiled=True),
    )
    gain_one_f = gain_one.astype(jnp.float32)
    shift_one_f = shift_one.astype(jnp.float32)
    queries, keys_all, values_all, weighting, weighting_low, attended = attention_forward(
        packed, segment, rowset, length, head_size
    )
    grad_one_low = (grad_middle * scale_one).astype(jnp.bfloat16)
    proj_grad = inner_rows(attended, grad_one_low)
    proj_bias_part = jnp.sum(grad_one_low.astype(jnp.float32), axis=0)
    grad_attended_low = times_transpose(grad_one_low, proj_full).astype(jnp.bfloat16)
    grad_attended_low = grad_attended_low.reshape(rowset, length, HEADS, head_size)
    grad_weighting = jnp.einsum(
        "rqhd,rkhd->rhqk", grad_attended_low, values_all, preferred_element_type=jnp.float32
    )
    value_grad = jnp.einsum(
        "rhqk,rqhd->rkhd", weighting_low, grad_attended_low, preferred_element_type=jnp.float32
    )
    row_inner = jnp.sum(grad_weighting * weighting, axis=-1, keepdims=True)
    grad_scores_low = (weighting * (grad_weighting - row_inner)).astype(jnp.bfloat16)
    key_scale = head_size ** (-0.5)
    query_grad = (
        jnp.einsum("rhqk,rkhd->rqhd", grad_scores_low, keys_all, preferred_element_type=jnp.float32)
        * key_scale
    )
    key_grad = (
        jnp.einsum("rhqk,rqhd->rkhd", grad_scores_low, queries, preferred_element_type=jnp.float32)
        * key_scale
    )
    grad_packed_low = (
        jnp.stack([query_grad, key_grad, value_grad], axis=2)
        .reshape(token_count, 3 * features)
        .astype(jnp.bfloat16)
    )
    qkv_grad = inner_rows(normed_one, grad_packed_low)
    column_sums = jnp.sum(grad_packed_low.astype(jnp.float32), axis=0)
    query_bias_part = column_sums[:features]
    value_bias_part = column_sums[2 * features :]
    grad_normed_one = times_transpose(grad_packed_low, qkv_full)
    grad_input_norm, gain_one_part, shift_one_part = norm_back(
        flattened, gain_one_f, shift_one_f, grad_normed_one
    )
    tokens_grad = (grad_middle + grad_input_norm).reshape(rowset, length, features)
    (
        gain_two_grad,
        shift_two_grad,
        fc1_weight_part,
        fc1_bias_shard,
        fc2_weight_part,
        fc2_bias_shard,
    ) = (
        lax.psum_scatter(gain_two_part, "fsdp", scatter_dimension=0, tiled=True),
        lax.psum_scatter(shift_two_part, "fsdp", scatter_dimension=0, tiled=True),
        lax.psum_scatter(fc1_grad, "fsdp", scatter_dimension=0, tiled=True),
        lax.psum_scatter(fc1_bias_part, "fsdp", scatter_dimension=0, tiled=True),
        lax.psum_scatter(fc2_grad, "fsdp", scatter_dimension=0, tiled=True),
        lax.psum_scatter(fc2_bias_part, "fsdp", scatter_dimension=0, tiled=True),
    )
    (
        gain_one_grad,
        shift_one_grad,
        qkv_weight_part,
        query_bias_shard,
        value_bias_shard,
        proj_weight_part,
        proj_bias_shard,
    ) = (
        lax.psum_scatter(gain_one_part, "fsdp", scatter_dimension=0, tiled=True),
        lax.psum_scatter(shift_one_part, "fsdp", scatter_dimension=0, tiled=True),
        lax.psum_scatter(qkv_grad, "fsdp", scatter_dimension=0, tiled=True),
        lax.psum_scatter(query_bias_part, "fsdp", scatter_dimension=0, tiled=True),
        lax.psum_scatter(value_bias_part, "fsdp", scatter_dimension=0, tiled=True),
        lax.psum_scatter(proj_grad, "fsdp", scatter_dimension=0, tiled=True),
        lax.psum_scatter(proj_bias_part, "fsdp", scatter_dimension=0, tiled=True),
    )
    summed = (
        lax.psum(gain_one_grad.astype(jnp.bfloat16), "dp").astype(jnp.float32),
        lax.psum(shift_one_grad.astype(jnp.bfloat16), "dp").astype(jnp.float32),
        lax.psum(qkv_weight_part.astype(jnp.bfloat16), "dp").astype(jnp.float32),
        lax.psum(query_bias_shard.astype(jnp.bfloat16), "dp").astype(jnp.float32),
        lax.psum(value_bias_shard.astype(jnp.bfloat16), "dp").astype(jnp.float32),
        lax.psum(proj_weight_part.astype(jnp.bfloat16), "dp").astype(jnp.float32),
        lax.psum(proj_bias_shard.astype(jnp.bfloat16), "dp").astype(jnp.float32),
        lax.psum(gain_two_grad.astype(jnp.bfloat16), "dp").astype(jnp.float32),
        lax.psum(shift_two_grad.astype(jnp.bfloat16), "dp").astype(jnp.float32),
        lax.psum(fc1_weight_part.astype(jnp.bfloat16), "dp").astype(jnp.float32),
        lax.psum(fc1_bias_shard.astype(jnp.bfloat16), "dp").astype(jnp.float32),
        lax.psum(fc2_weight_part.astype(jnp.bfloat16), "dp").astype(jnp.float32),
        lax.psum(fc2_bias_shard.astype(jnp.bfloat16), "dp").astype(jnp.float32),
    )
    return (
        output,
        tokens_grad,
        summed[0],
        summed[1],
        summed[2],
        summed[3],
        summed[4],
        summed[5],
        summed[6],
        summed[7],
        summed[8],
        summed[9],
        summed[10],
        summed[11],
        summed[12],
    )


BIT_Z1, BIT_Z0, BIT_Y, BIT_C = 8, 4, 2, 1
PIECE = 48
WIDE = 768
SCALE_ON = 1.0 / 0.9
MIB = 1024 * 1024
f32 = jnp.float32
bf16 = jnp.bfloat16


def hop(array, bit):
    return lax.ppermute(array, "fsdp", [(i, i ^ bit) for i in range(16)])


def swap(array):
    return lax.ppermute(array, "dp", [(0, 1), (1, 0)])


def cross(array):
    axes = ("dp", "fsdp")
    return lax.ppermute(array, axes, [(i, i ^ 16 ^ BIT_C) for i in range(32)])


def join(*arrays):
    return jnp.concatenate(arrays, axis=0)


def tie(array, *before):
    return lax.optimization_barrier((array,) + before)[0]


def to_other_core(own):
    return own + tuple(hop(part, BIT_C) for part in own)


def plus(left, right):
    return (left.astype(f32) + right.astype(f32)).astype(bf16)


def core_sums(own, came):
    return tuple(plus(own[a], came[a]) for a in range(4))


def first_hops(parts):
    return swap(parts[1]), hop(parts[3], BIT_Y)


def together(move, *arrays):
    flat = [array.reshape(-1, PIECE, 384) for array in arrays]
    came, at, out = move(join(*flat)), 0, []
    for array, part in zip(arrays, flat):
        out.append(came[at : at + part.shape[0]].reshape(array.shape))
        at += part.shape[0]
    return out


def hop_y(array):
    return hop(array, BIT_Y)


def first_sums(parts, got):
    return (
        plus(parts[0][:4], got[0][:4]),
        plus(parts[0][4:], got[0][4:]),
        plus(parts[2][:4], got[1][:4]),
        plus(parts[2][4:], got[1][4:]),
    )


def second_hops(parts):
    return hop(parts[1], BIT_Y), swap(parts[3])


def second_sums(parts, got):
    return tuple(
        jnp.stack([plus(parts[0][half], got[0][half]), plus(parts[2][half], got[1][half])])
        for half in (slice(0, 2), slice(2, 4))
    )


def third_hops(parts):
    return (hop(parts[1], BIT_Z0),)


def third_sums(parts, got):
    return plus(parts[0][:, 0], got[0][:, 0]), plus(parts[0][:, 1], got[0][:, 1])


def fourth_hops(parts):
    return (hop(parts[1], BIT_Z1),)


def fourth_sums(parts, got):
    return plus(parts[0], got[0])


def product(left, right, dims):
    return lax.dot_general(left, right, (dims, ((), ())), preferred_element_type=f32)


NN = ((1,), (0,))
NT = ((1,), (1,))
TN = ((0,), (0,))


def slot(line, xr, yr):
    return (xr, yr) if line == 0 else (2 + yr, xr)


def rel_places():
    return [(m, m & 1, (m >> 1) & 1, ((m >> 2) & 1) * 2 + (m >> 3)) for m in range(16)]


def rows_of(i, m):
    return pl.ds(pl.multiple_of((i ^ m) * PIECE, 16), PIECE)


def load_line(store, halves, i, columns=slice(None)):
    for m, c, yr, z in rel_places():
        ref, first = halves[c][yr]
        store[rows_of(i, m), columns] = ref[first + z, 0:PIECE, :]


def save_chunk(value, outs, i, line, xr):
    for m in range(16):
        c, yr, z0r, z1r = m & 1, (m >> 1) & 1, (m >> 2) & 1, (m >> 3) & 1
        array, part = slot(line, xr, yr) if isinstance(xr, int) else (2 + yr, xr)
        row = pl.multiple_of((i ^ m) * PIECE, 16)
        outs[c][array, part * 4 + z0r * 2 + z1r] = value[pl.ds(row, PIECE), :]


def row_facts(info, r):
    first = info[2 + 3 * r]
    second = first + info[3 + 3 * r]
    third = second + info[4 + 3 * r]

    def segment(shape, axis):
        t = lax.broadcasted_iota(jnp.int32, shape, axis)
        return (t >= first).astype(jnp.int32) + (t >= second).astype(jnp.int32) + (t >= third).astype(jnp.int32)

    column = segment((256, 1), 0)

    def scale(branch):
        keeps = [info[8 + 6 * r + 2 * j + branch].astype(f32) * SCALE_ON for j in range(3)]
        return jnp.where(
            column == 0, keeps[0], jnp.where(column == 1, keeps[1], jnp.where(column == 2, keeps[2], 0.0))
        )

    inside = jnp.where(column < 3, 1.0, 0.0).astype(f32)
    return column, segment((1, 256), 1), scale, inside


def unit_of(values):
    center = values - jnp.mean(values, axis=-1, keepdims=True)
    spread = jnp.mean(center * center, axis=-1, keepdims=True)
    root = lax.rsqrt(spread + EPSILON)
    return center * root, root


def unit_back(unit, root, gain, incoming):
    eg = incoming * gain
    return root * (
        eg - jnp.mean(eg, axis=-1, keepdims=True) - unit * jnp.mean(eg * unit, axis=-1, keepdims=True)
    )


def sums(values):
    return jnp.sum(values, axis=0, keepdims=True)


def load_direct(store, own, other, i, spots):
    for m in range(16):
        spot = spots[0] * (m >> 3) + spots[1] * (m >> 2 & 1) + spots[2] * (m >> 1 & 1)
        row = pl.multiple_of((i ^ m) * PIECE, 16)
        store[pl.ds(row, PIECE), :] = (other if m & 1 else own)[spot, 0:PIECE, :]


def prepare_kernel(info, qkv, fc1, fc2, *rest):
    vectors, (lead, *groups) = rest[:9], rest[9:]
    x = info[1]
    at = pl.multiple_of(WIDE + WIDE * x, 128)
    lead[0, 0:48, :] = qkv[:, pl.ds(at + 384, 384)]
    lead[0, 48:96, :] = qkv[:, pl.ds(pl.multiple_of(384 * x, 128), 384)]
    lead[0, 96:144, :] = qkv[:, pl.ds(at, 384)]
    rows = [v[...].astype(f32).reshape(1, -1) for v in vectors]
    rows = rows[:8] + [rows[8][:, 48 * k : 48 * k + 48] for k in range(4)]
    rows = [jnp.pad(row, ((0, 0), (0, 336))) for row in rows]
    lead[0, 144:160, :] = jnp.concatenate(rows + [jnp.zeros((4, 384), f32)]).astype(bf16)
    for half in range(2):

        @pl.when(x == half)
        def _():
            for s in range(2):
                first = 48 * (2 * half + s)
                cuts = [fc1[:, 192 * j + first : 192 * j + first + 48] for j in range(16)]
                groups[s][0] = jnp.concatenate(cuts, axis=1)
                groups[s][1] = fc2[first : first + 48, :]


def load_qkv(weight, refs, i, x):
    for xr in range(2):
        h = x ^ xr
        a = [[(refs[6 * c + xr], 4 * yr) for yr in range(2)] for c in range(2)]
        b = [[(refs[6 * c + 2 + yr], 4 * xr) for yr in range(2)] for c in range(2)]
        q = [[(refs[6 * c + 4 + xr], 4 * yr) for yr in range(2)] for c in range(2)]
        load_line(weight.at[1 + h], a, i, slice(0, 384))
        load_line(weight.at[1 + h], b, i, slice(384, 768))
        load_line(weight.at[0], q, i, pl.ds(pl.multiple_of(384 * h, 128), 384))


def qkv_kernel(info, tok, small, *rest):
    refs, (packed, normed, weight) = rest[:12], rest[12:]
    i, x = info[0], info[1]
    load_qkv(weight, refs, i, x)
    for r in range(2):
        rows = slice(256 * r, 256 * r + 256)
        unit, _ = unit_of(tok[rows, :].astype(f32))
        normed[rows, :] = (unit * small[0:1, :] + small[1:2, :]).astype(bf16)
    for r in range(2):
        rows = slice(256 * r, 256 * r + 256)
        low = normed[rows, :]
        packed[rows, 0:768] = (product(low, weight[0], NN) + small[2:3, :]).astype(bf16)
        packed[rows, 768:1536] = product(low, weight[1], NN).astype(bf16)
        packed[rows, 1536:2304] = (product(low, weight[2], NN) + small[3:4, :]).astype(bf16)


def attend_kernel(info, packed, cot, attended, grad_two, lse, scores, weighting):
    r = pl.program_id(0)
    column, across, scale, inside = row_facts(info, r)
    same = column == across
    lane = lax.broadcasted_iota(jnp.int32, (256, 128), 1)
    kept = jnp.zeros((256, 128), f32)
    for g in range(HEADS):
        query = packed[:, 64 * g : 64 * g + 64] * 0.125
        scores[g] = product(query, packed[:, 768 + 64 * g : 832 + 64 * g], NT)
    for g in range(HEADS):
        masked = jnp.where(same, scores[g], NEGATIVE)
        top = jnp.max(masked, axis=-1, keepdims=True)
        raised = jnp.exp(masked - top)
        total = jnp.sum(raised, axis=-1, keepdims=True)
        weighting[g] = (raised * (1.0 / total)).astype(bf16)
        kept = jnp.where(lane == g, top + jnp.log(total), kept)
    lse[...] = kept
    for h in range(0, HEADS, 2):
        pair = [
            product(weighting[g], packed[:, 1536 + 64 * g : 1600 + 64 * g], NN).astype(bf16)
            for g in (h, h + 1)
        ]
        attended[:, 64 * h : 64 * h + 128] = jnp.concatenate(pair, axis=1)
    grad_two[...] = (cot[...].astype(f32) * inside * scale(1)).astype(bf16)


def hidden_units(block, normed, turned, grad_two, small, branch, grad_normed, bias, weights, scratch):
    active, low = scratch[:2]
    for r in range(2):
        rows = slice(256 * r, 256 * r + 256)
        value = product(normed[rows, :], weights[0], NN) + small[pl.ds(8 + block, 1), :]
        share = 0.5 * (1.0 + lax.erf(value * (0.5**0.5)))
        active[rows, :] = (value * share).astype(bf16)
        slope = share + value * (jnp.exp(-0.5 * value * value) * 0.3989422804014327)
        low[rows, :] = (product(grad_two[rows, :], weights[1], NT) * slope).astype(bf16)
    bias[pl.ds(8 + block, 1), :] = sums(low[...].astype(f32))
    for r in range(2):
        rows = slice(256 * r, 256 * r + 256)
        branch[rows, :] += product(active[rows, :], weights[1], NN)
        grad_normed[rows, :] += product(low[rows, :], weights[0], NT)
    scratch[2][...] = product(turned[...], low[...], NN).astype(bf16)
    scratch[3][...] = product(active[...], grad_two[...], TN).astype(bf16)


def load_units(scratch, refs, i, t):
    for step in range(2):

        @pl.when(t == step)
        def _():
            up = [[(refs[4 * c + step], 4 * yr) for yr in range(2)] for c in range(2)]
            down = [[(refs[4 * c + 2 + yr], 4 * step) for yr in range(2)] for c in range(2)]
            load_line(scratch[4], up, i)
            load_line(scratch[5], down, i)

    return scratch[4][...], scratch[5][...]


def save_units(scratch, own, away, i, t):
    for m, c, yr, z in rel_places():
        for part in range(2):
            here = slice(384 * part, 384 * part + 384)
            (own, away)[c][t, 4 * yr + z, part] = scratch[2][rows_of(i, m), here]
            (own, away)[c][2 + yr, 4 * t + z, part] = scratch[3][rows_of(i, m), here]


def first_units_kernel(xr, info, left, grad_two, small, *rest):
    refs, rest = rest[:6], rest[6:]
    i, x = info[0], info[1]
    if xr == 0:
        tok, proj_own, proj_other, middle, normed, turned, branch, grad_normed, bias, own, away, proj = rest[:12]
        scratch = rest[12:]
        load_direct(proj, proj_own, proj_other, i, (2, 4, 1))
        for r in range(2):
            rows = slice(256 * r, 256 * r + 256)
            _, _, scale, _ = row_facts(info, r)
            after = tok[rows, :].astype(f32) + scale(0) * (
                product(left[rows, :], proj[...], NN) + small[4:5, :]
            )
            middle[rows, :] = after
            unit, _ = unit_of(after)
            normed[rows, :] = (unit * small[5:6, :] + small[6:7, :]).astype(bf16)
        turned[...] = normed[...].T
        branch[...] = jnp.zeros_like(branch)
        grad_normed[...] = jnp.zeros_like(grad_normed)
        bias[...] = jnp.zeros_like(bias)
        bias[7:8, :] = sums(grad_two[...].astype(f32))
    else:
        turned, branch_in, grad_normed_in, bias_in, branch, grad_normed, bias, own, away, *scratch = rest
        normed = left
        branch[...] = branch_in[...]
        grad_normed[...] = grad_normed_in[...]
        bias[...] = bias_in[...]
    load_line(scratch[4], [[(refs[c], 4 * yr) for yr in range(2)] for c in range(2)], i)
    load_line(scratch[5], [[(refs[2 + 2 * c + yr], 0) for yr in range(2)] for c in range(2)], i)
    weights = (scratch[4][...], scratch[5][...])
    hidden_units(2 * (x ^ xr), normed, turned, grad_two, small, branch, grad_normed, bias, weights, scratch)
    for m, c, yr, z in rel_places():
        for part in range(2):
            here = slice(384 * part, 384 * part + 384)
            for k in range(2):
                (own, away)[c][k, 4 * yr + z, part] = scratch[2 + k][rows_of(i, m), here]


def second_units_kernel(
    info, normed, turned, grad_two, small, branch_in, grad_normed_in, bias_in, middle, cot, *rest
):
    refs, (result, grad_middle, grad_one, bias, own, away, branch, grad_normed, *scratch) = rest[:8], rest[8:]
    i, x, t = info[0], info[1], pl.program_id(0)

    @pl.when(t == 0)
    def _():
        branch[...] = branch_in[...]
        grad_normed[...] = grad_normed_in[...]
        bias[...] = bias_in[...]

    weights = load_units(scratch, refs, i, t)
    hidden_units(2 * (t ^ x) + 1, normed, turned, grad_two, small, branch, grad_normed, bias, weights, scratch)
    save_units(scratch, own, away, i, t)

    @pl.when(t == 1)
    def _():
        for r in range(2):
            rows = slice(256 * r, 256 * r + 256)
            _, _, scale, inside = row_facts(info, r)
            after = middle[rows, :]
            result[rows, :] = (
                (after + scale(1) * (branch[rows, :] + small[7:8, :])) * inside
            ).astype(bf16)
            unit, root = unit_of(after)
            incoming = grad_normed[rows, :]
            bias[5:6, :] += sums(incoming * unit)
            bias[6:7, :] += sums(incoming)
            total = cot[rows, :].astype(f32) * inside + unit_back(unit, root, small[5:6, :], incoming)
            grad_middle[rows, :] = total
            low_one = (total * scale(0)).astype(bf16)
            grad_one[rows, :] = low_one
            bias[4:5, :] += sums(low_one.astype(f32))


def attend_back_kernel(group, info, queries, keys, values, lse, attended, grad_one, normed, *rest):
    if group == 0:
        proj_own, proj_other, grad_packed, own, away, weight, proj_rest, grad, *heads, total = rest
    else:
        weight, proj_rest, grad_packed, own, away, grad, *heads = rest
    i, x, r = info[0], info[1], pl.program_id(0)
    if group == 0:

        @pl.when(r == 0)
        def _():
            load_direct(weight, proj_own, proj_other, i, (2, 4, 1))
            total[...] = jnp.zeros_like(total)

        total[...] += product(attended[...], grad_one[...], TN)

    column, across, _, _ = row_facts(info, r)
    same = column == across
    grad_attended = product(grad_one[...], weight[384 * group : 384 * group + 384, :], NT).astype(bf16)
    rows = pl.ds(pl.multiple_of(r * 256, 256), 256)
    scores, backs, lows, highs = heads
    queried = [queries[:, 64 * g : 64 * g + 64] * 0.125 for g in range(6)]
    returned = [grad_attended[:, 64 * g : 64 * g + 64] for g in range(6)]
    for g in range(6):
        here = slice(64 * g, 64 * g + 64)
        scores[g] = product(queried[g], keys[:, here], NT)
        backs[g] = product(returned[g], values[:, here], NT)
    for g in range(6):
        head = 6 * group + g
        weighting = jnp.where(same, jnp.exp(scores[g] - lse[:, head : head + 1]), 0.0)
        highs[g] = weighting.astype(bf16)
        share = backs[g] * weighting
        inner = jnp.sum(share, axis=-1, keepdims=True)
        lows[g] = (share - weighting * inner).astype(bf16)
    for h in range(0, 6, 2):
        pairs = ([], [], [])
        for g in (h, h + 1):
            pairs[0].append(product(lows[g], keys[:, 64 * g : 64 * g + 64], NN) * 0.125)
            pairs[1].append(product(lows[g], queried[g], TN))
            pairs[2].append(product(highs[g], returned[g], TN))
        for k in range(3):
            grad_packed[rows, 384 * k + 64 * h : 384 * k + 64 * h + 128] = jnp.concatenate(
                pairs[k], axis=1
            ).astype(bf16)

    @pl.when(r == 1)
    def _():
        turned = normed[...].T
        grad[1, 0] = product(turned, grad_packed[:, 0:384], NN).astype(bf16)
        grad[0, 0] = product(turned, grad_packed[:, 384:768], NN).astype(bf16)
        grad[0, 1] = product(turned, grad_packed[:, 768:1152], NN).astype(bf16)
        if group == 0:
            grad[1, 1] = total[:, 0:384].astype(bf16)
            proj_rest[...] = total[:, 384:768].astype(bf16)
        else:
            grad[1, 1] = proj_rest[...]
        for line in range(2):
            for xr in range(2):
                save_chunk(grad.at[line, x ^ xr], (own, away), i, line, xr)


def tokens_back_kernel(r, info, tok, back0, back1, grad_middle, bias_in, small, *rest):
    refs, (tokens_grad, bias, weight) = rest[:12], rest[-3:]
    i, x = info[0], info[1]
    load_qkv(weight, refs, i, x)
    bias[...] = bias_in[...]
    for part, back in ((0, back0), (1, back1)):
        columns = slice(384 * part, 384 * part + 384)
        bias[2:3, columns] += sums(back[:, 0:384].astype(f32))
        bias[3:4, columns] += sums(back[:, 768:1152].astype(f32))
    incoming = jnp.zeros((256, WIDE), f32)
    for k in range(3):
        here = slice(384 * k, 384 * k + 384)
        joined = jnp.concatenate([back0[:, here], back1[:, here]], axis=1)
        incoming += product(joined, weight[k], NT)
    unit, root = unit_of(tok[...].astype(f32))
    bias[0:1, :] += sums(incoming * unit)
    bias[1:2, :] += sums(incoming)
    tokens_grad[...] = grad_middle[...] + unit_back(unit, root, small[0:1, :], incoming)


def results_kernel(info, mine0, other0, mine1, other1, bias, qkv, proj, *vectors):
    i, x = info[0], info[1]
    for group, mine, other in ((0, mine0, other0), (1, mine1, other1)):
        for line, half, column in ((1, 0, 0), (0, 0, 768), (0, 1, 1536), (1, 1, None)):
            a, b = mine[line].astype(f32), other[line].astype(f32)
            value = jnp.where(x == half, a, b)
            if column is None:
                proj[:, 384 * group : 384 * group + 384] = value
            else:
                qkv[:, column + 384 * group : column + 384 * group + 384] = value

    def cut(rows, start, width):
        feature = lax.broadcasted_iota(jnp.int32, (WIDE, width), 0)
        lane = lax.broadcasted_iota(jnp.int32, (WIDE, width), 1)
        chosen = (feature == lane + start).astype(f32)
        return lax.dot_general(
            rows, chosen, (NN, ((), ())), precision=lax.Precision.HIGHEST, preferred_element_type=f32
        )

    narrow = cut(bias[...], i * 48, 128)
    for k in range(8):
        vectors[k][...] = narrow[k, 0:48]
    broad = jnp.concatenate([narrow[8 + k : 9 + k, 0:48] for k in range(4)], axis=1)
    vectors[8][...] = broad[0]


def units_results_kernel(info, mine0, other0, mine1, other1, fc1, fc2):
    x = info[1]
    blocks = []
    for half in range(2):
        for mine, other in ((mine0, other0), (mine1, other1)):
            pieces = [
                jnp.concatenate(
                    [jnp.where(x == half, mine[k, p].astype(f32), other[k, p].astype(f32)) for p in range(2)],
                    axis=1,
                )
                for k in range(2)
            ]
            fc2[48 * len(blocks) : 48 * len(blocks) + 48, :] = pieces[1]
            blocks.append(pieces[0])
    for j in range(0, 16, 2):
        cuts = [b[:, 48 * k : 48 * k + 48] for k in (j, j + 1) for b in blocks]
        fc1[:, 192 * j : 192 * j + 384] = jnp.concatenate(cuts, axis=1)


def whole(shape):
    return pl.BlockSpec(shape, lambda *_: (0,) * len(shape))


def once(shape):
    return pl.BlockSpec(shape, lambda *_: (0,) * len(shape), pipeline_mode=pl.Buffered(1))


def rowwise(width):
    return pl.BlockSpec((256, width), lambda r, info: (r, 0))


def run_kernel(kernel, grid, info, operands, outs, scratch, microseconds, vmem, alias=None):
    return pl.pallas_call(
        kernel,
        grid_spec=pltpu.PrefetchScalarGridSpec(
            num_scalar_prefetch=1,
            grid=(grid,),
            in_specs=[spec or once(array.shape) for spec, array in operands],
            out_specs=[spec or whole(shape) for spec, shape, _ in outs],
            scratch_shapes=[pltpu.VMEM(shape, dtype) for shape, dtype in scratch],
        ),
        out_shape=[jax.ShapeDtypeStruct(shape, dtype) for _, shape, dtype in outs],
        input_output_aliases=alias or {},
        compiler_params=pltpu.CompilerParams(
            dimension_semantics=("arbitrary",), vmem_limit_bytes=vmem * MIB
        ),
        cost_estimate=pl.CostEstimate(
            flops=int(microseconds * 1.15e9), bytes_accessed=1 << 20, transcendentals=0
        ),
    )(info, *[array for _, array in operands])


def fast_device(
    tokens,
    lengths,
    keep_mask,
    cotangent,
    ln1_gain,
    ln1_bias,
    qkv_weight,
    q_bias,
    v_bias,
    proj_weight,
    proj_bias,
    ln2_gain,
    ln2_bias,
    fc1_weight,
    fc1_bias,
    fc2_weight,
    fc2_bias,
):
    count = tokens.shape[0] * tokens.shape[1]
    i = lax.axis_index("fsdp")
    x = lax.axis_index("dp")
    info = jnp.concatenate(
        [jnp.stack([i, x]).astype(jnp.int32), lengths.reshape(-1), keep_mask.reshape(-1)]
    )
    tok = tokens.reshape(count, WIDE)
    cot = cotangent.reshape(count, WIDE)

    def full(*arrays):
        return [(None, array) for array in arrays]

    vectors = (ln1_gain, ln1_bias, q_bias, v_bias, proj_bias, ln2_gain, ln2_bias, fc2_bias, fc1_bias)
    lead, units0, units1 = run_kernel(
        prepare_kernel,
        1,
        jnp.stack([i, x]),
        full(qkv_weight, fc1_weight, fc2_weight, *vectors),
        [(None, (1, 160, 384), bf16), (None, (2, PIECE, WIDE), bf16), (None, (2, PIECE, WIDE), bf16)],
        [],
        2,
        60,
    )

    proj = tie(proj_weight[None], lead)
    proj = join(proj, hop(proj, BIT_Y))

    pair = join(lead, hop(lead, BIT_Z1))
    far = hop(pair, BIT_Z0)
    line_b, line_q, line_a = (join(pair[:, k], far[:, k]) for k in (slice(0, 48), slice(48, 96), slice(96, 160)))
    line_a, line_b, line_q, units0 = lax.optimization_barrier((line_a, line_b, line_q, units0))
    got_a, got_b, got_q = hop(line_a, BIT_Y), swap(line_b), hop(line_q, BIT_Y)
    units_far = hop(units0, BIT_Z1)
    got_a, got_b = lax.optimization_barrier((got_a, got_b))
    wide_a, wide_b = join(line_a, got_a), join(line_b, got_b)
    got_a, got_b = swap(wide_a[:, :PIECE]), hop(wide_b, BIT_Y)
    wide_q = join(line_q, got_q)
    got_q = swap(wide_q)
    units_far = tie(units_far, wide_a, wide_b)
    units0 = jnp.stack([units0, units_far], axis=1)
    units_far = hop(units0, BIT_Z0)
    proj = tie(proj, wide_a, wide_b, units0)
    proj_far = hop(proj, BIT_Z1)
    got_a, got_b, got_q, units_far, units1, proj_far = lax.optimization_barrier(
        (got_a, got_b, got_q, units_far, units1, proj_far)
    )
    first = to_other_core((wide_a, got_a, wide_b, got_b, wide_q, got_q))

    units_line = join(units0[0], units_far[0]), join(units0[1], units_far[1])
    units_got = hop(units_line[0], BIT_Y), swap(units_line[1])
    next_far = hop(units1, BIT_Z1)
    proj = join(proj, proj_far)
    proj_far = hop(proj, BIT_Z0)

    vectors = jnp.concatenate([first[k][:, PIECE : PIECE + 12, :PIECE] for k in (0, 6)])
    origin = jnp.array([(p & 1) * 8 + (p >> 1 & 1) * 4 + (p >> 2 & 1) * 2 + (p >> 3) for p in range(16)])
    turned = jnp.arange(16)[:, None] == (origin ^ i)[None, :]
    vectors = jnp.einsum("mp,pkl->kml", turned.astype(bf16), vectors, preferred_element_type=f32)
    small = jnp.concatenate([vectors.reshape(12, WIDE), jnp.zeros((4, WIDE), f32)])

    packed, normed_one = run_kernel(
        qkv_kernel,
        1,
        info,
        full(tok, small, *first),
        [(None, (count, 3 * WIDE), bf16), (None, (count, WIDE), bf16)],
        [((3, WIDE, WIDE), bf16)],
        5,
        40,
    )

    units_got, next_far, proj_far, _ = lax.optimization_barrier((units_got, next_far, proj_far, packed))
    units_wide = tuple(join(line, got) for line, got in zip(units_line, units_got))
    units_got = swap(units_wide[0]), hop(units_wide[1], BIT_Y)
    units1 = jnp.stack([units1, next_far], axis=1)
    next_far = hop(units1, BIT_Z0)
    proj = join(proj, proj_far)
    proj_other = hop(proj, BIT_C)

    attended, grad_two, lse = run_kernel(
        attend_kernel,
        2,
        tie(info, *units_wide, units1, proj),
        [(rowwise(3 * WIDE), packed), (rowwise(WIDE), cot)],
        [
            (rowwise(WIDE), (count, WIDE), bf16),
            (rowwise(WIDE), (count, WIDE), bf16),
            (rowwise(128), (count, 128), f32),
        ],
        [((HEADS, 256, 256), f32), ((HEADS, 256, 256), bf16)],
        6,
        40,
    )

    units_got, next_far, proj_other, _ = lax.optimization_barrier((units_got, next_far, proj_other, lse))
    units = to_other_core((units_wide[0], units_got[0], units_wide[1], units_got[1]))
    next_line = tuple(join(units1[k], next_far[k]) for k in range(2))
    next_got = hop(next_line[0], BIT_Y), swap(next_line[1])

    wide_f32 = (None, (count, WIDE), f32)
    wide_bf16 = (None, (count, WIDE), bf16)
    vectors_f32 = (None, (16, WIDE), f32)
    parts = (None, (4, 8, 2, PIECE, 384), bf16)
    half = (None, (2, 8, 2, PIECE, 384), bf16)
    unit_scratch = [((count, WIDE), bf16)] * 2 + [((WIDE, WIDE), bf16)] * 4

    def first_units(xr, info, left, more, outs, scratch):
        part = pl.BlockSpec((4, PIECE, WIDE), lambda _, __: (xr, 0, 0))
        return run_kernel(
            functools.partial(first_units_kernel, xr),
            1,
            info,
            full(left, grad_two, small, units[xr], units[4 + xr])
            + [(part, units[k]) for k in (2, 3, 6, 7)]
            + full(*more),
            outs + [wide_f32, wide_f32, vectors_f32, half, half],
            scratch + unit_scratch,
            7,
            28,
        )

    middle, normed_two, turned_two, branch, grad_normed, bias, own0, away0 = first_units(
        0,
        tie(info, *next_line),
        attended,
        (tok, proj, proj_other),
        [wide_f32, wide_bf16, (None, (WIDE, count), bf16)],
        [((WIDE, WIDE), bf16)],
    )
    next_got, bias, away0 = lax.optimization_barrier((next_got, bias, away0))
    next_wide = tuple(join(line, got) for line, got in zip(next_line, next_got))
    next_got = swap(next_wide[0]), hop(next_wide[1], BIT_Y)
    came0 = hop(away0, BIT_C)
    branch, grad_normed, bias, own1, away1 = first_units(
        1, tie(info, *next_wide), normed_two, (turned_two, branch, grad_normed, bias), [], []
    )
    next_got, came0, bias, away1 = lax.optimization_barrier((next_got, came0, bias, away1))
    units = to_other_core((next_wide[0], next_got[0], next_wide[1], next_got[1]))
    came1 = hop(away1, BIT_C)
    two = (
        plus(own0[0], came0[0]),
        plus(own1[0], came1[0]),
        join(plus(own0[1, :4], came0[1, :4]), plus(own1[1, :4], came1[1, :4])),
        join(plus(own0[1, 4:], came0[1, 4:]), plus(own1[1, 4:], came1[1, 4:])),
    )
    two_got = first_hops(two)
    output, grad_middle, grad_one, bias, units_own, units_away = run_kernel(
        second_units_kernel,
        2,
        tie(info, *two),
        full(normed_two, turned_two, grad_two, small, branch, grad_normed, bias, middle, cot, *units),
        [wide_bf16, wide_f32, wide_bf16, vectors_f32, parts, parts],
        [((count, WIDE), f32)] * 2 + unit_scratch,
        15,
        40,
    )

    def attend_back(group, info, more, outs, scratch):
        def columns(k):
            return pl.BlockSpec((256, 384), lambda r, _, at=2 * k + group: (r, at))

        narrow = (4, 8, PIECE, 384)
        return run_kernel(
            functools.partial(attend_back_kernel, group),
            2,
            info,
            [(columns(k), packed) for k in range(3)]
            + [(rowwise(128), lse), (rowwise(WIDE), attended), (rowwise(WIDE), grad_one)]
            + full(normed_one, *more),
            [(None, (count, 1152), bf16), (None, narrow, bf16), (None, narrow, bf16)] + outs,
            [((2, 2, WIDE, 384), bf16)]
            + [((6, 256, 256), f32)] * 2
            + [((6, 256, 256), bf16)] * 2
            + scratch,
            8,
            40,
        )

    two_got, bias, units_away = lax.optimization_barrier((two_got, bias, units_away))
    two = first_sums(two, two_got)
    two_got, one_came = second_hops(two), hop(units_away, BIT_C)
    back0, head_own0, head_away0, proj_full, proj_rest = attend_back(
        0,
        tie(info, *two),
        (proj, proj_other),
        [(None, (WIDE, WIDE), bf16), (None, (WIDE, 384), bf16)],
        [((WIDE, WIDE), f32)],
    )

    two_got, one_came, proj_rest, head_away0 = lax.optimization_barrier(
        (two_got, one_came, proj_rest, head_away0)
    )
    two = second_sums(two, two_got)
    one = core_sums(units_own, one_came)
    one_got, two_got, zero_came = first_hops(one), third_hops(two), hop(head_away0, BIT_C)
    back1, head_own1, head_away1 = attend_back(1, tie(info, *two, *one), (proj_full, proj_rest), [], [])

    two_got, one_got, zero_came, head_away1 = lax.optimization_barrier(
        (two_got, one_got, zero_came, head_away1)
    )
    two, one, zero = third_sums(two, two_got), first_sums(one, one_got), core_sums(head_own0, zero_came)
    last_came = hop(head_away1, BIT_C)
    zero_got, one_got = first_hops(zero), second_hops(one)

    def tokens_back(r, info, more, alias):
        def row(width):
            return pl.BlockSpec((256, width), lambda _, __: (r, 0))

        return run_kernel(
            functools.partial(tokens_back_kernel, r),
            1,
            info,
            [(row(WIDE), tok), (row(1152), back0), (row(1152), back1), (row(WIDE), grad_middle)]
            + full(bias, small, *first)
            + more,
            [(row(WIDE), (count, WIDE), f32), (None, (16, WIDE), f32)],
            [((3, WIDE, WIDE), bf16)],
            5,
            40,
            alias,
        )

    tokens_grad, bias = tokens_back(0, tie(info, *two, *one, *zero), [], {})

    zero_got, one_got, last_came, bias = lax.optimization_barrier((zero_got, one_got, last_came, bias))
    last, zero, one = core_sums(head_own1, last_came), first_sums(zero, zero_got), second_sums(one, one_got)
    two_got, one_got = fourth_hops(two), third_hops(one)
    got_x, got_y = together(swap, last[1], zero[3]), together(hop_y, last[3], zero[1])
    last_got, zero_got = (got_x[0], got_y[0]), (got_y[1], got_x[1])
    tokens_grad, bias = tokens_back(
        1, tie(info, *last, *zero, *one), [(pl.BlockSpec(memory_space=pl.ANY), tokens_grad)], {19: 0}
    )

    last_got, zero_got, two_got, one_got, bias = lax.optimization_barrier(
        (last_got, zero_got, two_got, one_got, bias)
    )
    last, zero, two, one = (
        first_sums(last, last_got),
        second_sums(zero, zero_got),
        fourth_sums(two, two_got),
        third_sums(one, one_got),
    )
    last_got, zero_got, one_got, bias_got = lax.optimization_barrier(
        (second_hops(last), third_hops(zero), fourth_hops(one), hop(bias, BIT_Y))
    )
    last, one, zero = second_sums(last, last_got), fourth_sums(one, one_got), third_sums(zero, zero_got)
    bias = bias + bias_got
    last_got, zero_got, got, bias_got = lax.optimization_barrier(
        (third_hops(last), fourth_hops(zero), together(swap, one, two), hop(bias, BIT_Z0))
    )
    one_other, two_other = got
    last, zero, bias = third_sums(last, last_got), fourth_sums(zero, zero_got), bias + bias_got
    last_got, zero_other, bias_got = lax.optimization_barrier(
        (fourth_hops(last), swap(zero), hop(bias, BIT_Z1))
    )
    last, bias = fourth_sums(last, last_got), bias + bias_got
    last_other, bias_got = swap(last), (swap(bias), hop(bias, BIT_C), cross(bias))
    fc1_grad, fc2_grad = run_kernel(
        units_results_kernel,
        1,
        info,
        full(two, two_other, one, one_other),
        [(None, (PIECE, 4 * WIDE), f32), (None, (4 * PIECE, WIDE), f32)],
        [],
        3,
        40,
    )
    bias = (bias + bias_got[0]) + (bias_got[1] + bias_got[2])
    qkv_grad, proj_grad, *narrow = run_kernel(
        results_kernel,
        1,
        info,
        full(zero, zero_other, last, last_other, bias),
        [(None, (PIECE, 3 * WIDE), f32), (None, (PIECE, WIDE), f32)]
        + [(None, (48,), f32)] * 8
        + [(None, (192,), f32)],
        [],
        3,
        40,
    )
    return (
        output.reshape(tokens.shape),
        tokens_grad.reshape(tokens.shape),
        narrow[0],
        narrow[1],
        qkv_grad,
        narrow[2],
        narrow[3],
        proj_grad,
        narrow[4],
        narrow[5],
        narrow[6],
        fc1_grad,
        narrow[8],
        fc2_grad,
        narrow[7],
    )


def solution(mesh):
    in_specs = (
        P(("dp", "fsdp"), None, None),
        P(("dp", "fsdp"), None),
        P(("dp", "fsdp"), None, None),
        P(("dp", "fsdp"), None, None),
        P("fsdp"),
        P("fsdp"),
        P("fsdp", None),
        P("fsdp"),
        P("fsdp"),
        P("fsdp", None),
        P("fsdp"),
        P("fsdp"),
        P("fsdp"),
        P("fsdp", None),
        P("fsdp"),
        P("fsdp", None),
        P("fsdp"),
    )
    out_specs = (
        P(("dp", "fsdp"), None, None),
        P(("dp", "fsdp"), None, None),
        P("fsdp"),
        P("fsdp"),
        P("fsdp", None),
        P("fsdp"),
        P("fsdp"),
        P("fsdp", None),
        P("fsdp"),
        P("fsdp"),
        P("fsdp"),
        P("fsdp", None),
        P("fsdp"),
        P("fsdp", None),
        P("fsdp"),
    )
    fits = mesh.shape["dp"] == 2 and mesh.shape["fsdp"] == 16
    return jax.shard_map(
        fast_device if fits else per_device, mesh=mesh, in_specs=in_specs, out_specs=out_specs, check_vma=False
    )
```

```python
import functools

import jax
import jax.numpy as jnp
from jax import lax
from jax.experimental import pallas as pl
from jax.experimental.pallas import tpu as pltpu
from jax.sharding import PartitionSpec as P

HEADS = 12


EPSILON = 1e-06
KEEP_RATE = 0.9
NEGATIVE = -1e30


def normalize(values, gain, shift):
    center = values - jnp.mean(values, axis=-1, keepdims=True)
    spread = jnp.mean(center * center, axis=-1, keepdims=True)
    return center * lax.rsqrt(spread + EPSILON) * gain + shift


def standardize(values):
    center = values - jnp.mean(values, axis=-1, keepdims=True)
    spread = jnp.mean(center * center, axis=-1, keepdims=True)
    return center * lax.rsqrt(spread + EPSILON)


def affine_low(unit_values, gain, shift):
    return (unit_values * gain.astype(jnp.float32) + shift.astype(jnp.float32)).astype(jnp.bfloat16)


def exact_gelu(values):
    return jax.nn.gelu(values, approximate=False)


def norm_back(values, gain, shift, incoming):
    _, pullback = jax.vjp(normalize, values, gain, shift)
    return pullback(incoming)


def inner_rows(left, right):
    return lax.dot_general(
        left, right, (((0,), (0,)), ((), ())), preferred_element_type=jnp.float32
    )


def times_transpose(left, right):
    return lax.dot_general(
        left, right, (((1,), (1,)), ((), ())), preferred_element_type=jnp.float32
    )


def layout(lengths, keep_mask, length):
    image_ends = jnp.cumsum(lengths, axis=-1, dtype=jnp.int32)
    position = jnp.arange(length, dtype=jnp.int32)
    segment = jnp.sum(
        (position[None, :, None] >= image_ends[:, None, :]).astype(jnp.int32),
        axis=-1,
        dtype=jnp.int32,
    )
    images = jnp.arange(lengths.shape[1], dtype=jnp.int32)
    member = (segment[:, :, None] == images[None, None, :]).astype(jnp.float32)
    keeping = keep_mask.astype(jnp.float32)
    scales = jnp.sum(member[:, :, :, None] * keeping[:, None, :, :], axis=2) / KEEP_RATE
    inside = jnp.sum(member, axis=-1)
    return (segment, scales, inside)


def attention_forward(packed, segment, rowset, length, head_size):
    split_view = packed.reshape(rowset, length, 3, HEADS, head_size)
    queries = split_view[:, :, 0]
    keys_all = split_view[:, :, 1]
    values_all = split_view[:, :, 2]
    scores = jnp.einsum(
        "rqhd,rkhd->rhqk", queries, keys_all, preferred_element_type=jnp.float32
    ) * head_size ** (-0.5)
    matching = segment[:, :, None] == segment[:, None, :]
    scores = jnp.where(matching[:, None], scores, NEGATIVE)
    raised = jnp.exp(scores - jnp.max(scores, axis=-1, keepdims=True))
    weighting = raised / jnp.sum(raised, axis=-1, keepdims=True)
    weighting_low = weighting.astype(jnp.bfloat16)
    attended = jnp.einsum(
        "rhqk,rkhd->rqhd", weighting_low, values_all, preferred_element_type=jnp.float32
    )
    attended = attended.reshape(rowset * length, HEADS * head_size).astype(jnp.bfloat16)
    return (queries, keys_all, values_all, weighting, weighting_low, attended)


def per_device(
    tokens,
    lengths,
    keep_mask,
    cotangent,
    ln1_gain,
    ln1_bias,
    qkv_weight,
    q_bias,
    v_bias,
    proj_weight,
    proj_bias,
    ln2_gain,
    ln2_bias,
    fc1_weight,
    fc1_bias,
    fc2_weight,
    fc2_bias,
):
    rowset, length, features = tokens.shape
    head_size = features // HEADS
    token_count = rowset * length
    segment, scales, inside = layout(lengths, keep_mask, length)
    scale_one = scales[:, :, 0].reshape(token_count, 1)
    scale_two = scales[:, :, 1].reshape(token_count, 1)
    inside_column = inside.reshape(token_count, 1)
    flattened = tokens.reshape(token_count, features).astype(jnp.float32)
    unit_one = standardize(flattened)
    qkv_full, proj_full, gain_one, shift_one, query_bias, value_bias, out_bias = (
        lax.all_gather(qkv_weight, "fsdp", axis=0, tiled=True),
        lax.all_gather(proj_weight, "fsdp", axis=0, tiled=True),
        lax.all_gather(ln1_gain, "fsdp", axis=0, tiled=True),
        lax.all_gather(ln1_bias, "fsdp", axis=0, tiled=True),
        lax.all_gather(q_bias, "fsdp", axis=0, tiled=True),
        lax.all_gather(v_bias, "fsdp", axis=0, tiled=True),
        lax.all_gather(proj_bias, "fsdp", axis=0, tiled=True),
    )
    normed_one = affine_low(unit_one, gain_one, shift_one)
    bias_all = jnp.concatenate(
        [
            query_bias.astype(jnp.float32),
            jnp.zeros((features,), jnp.float32),
            value_bias.astype(jnp.float32),
        ]
    )
    packed = (jnp.dot(normed_one, qkv_full, preferred_element_type=jnp.float32) + bias_all).astype(
        jnp.bfloat16
    )
    _, _, _, _, _, attended = attention_forward(packed, segment, rowset, length, head_size)
    branch_one = jnp.dot(attended, proj_full, preferred_element_type=jnp.float32) + out_bias.astype(
        jnp.float32
    )
    middle = flattened + scale_one * branch_one
    unit_two = standardize(middle)
    up_full, down_full, gain_two, shift_two, up_bias, down_bias = (
        lax.all_gather(fc1_weight, "fsdp", axis=0, tiled=True),
        lax.all_gather(fc2_weight, "fsdp", axis=0, tiled=True),
        lax.all_gather(ln2_gain, "fsdp", axis=0, tiled=True),
        lax.all_gather(ln2_bias, "fsdp", axis=0, tiled=True),
        lax.all_gather(fc1_bias, "fsdp", axis=0, tiled=True),
        lax.all_gather(fc2_bias, "fsdp", axis=0, tiled=True),
    )
    normed_two = affine_low(unit_two, gain_two, shift_two)
    hidden = jnp.dot(normed_two, up_full, preferred_element_type=jnp.float32) + up_bias.astype(
        jnp.float32
    )
    active = exact_gelu(hidden).astype(jnp.bfloat16)
    branch_two = jnp.dot(active, down_full, preferred_element_type=jnp.float32) + down_bias.astype(
        jnp.float32
    )
    output = (
        ((middle + scale_two * branch_two) * inside_column)
        .astype(jnp.bfloat16)
        .reshape(rowset, length, features)
    )
    up_full, down_full = (
        lax.all_gather(fc1_weight, "fsdp", axis=0, tiled=True),
        lax.all_gather(fc2_weight, "fsdp", axis=0, tiled=True),
    )
    gain_two_f = gain_two.astype(jnp.float32)
    shift_two_f = shift_two.astype(jnp.float32)
    grad_out = cotangent.reshape(token_count, features).astype(jnp.float32) * inside_column
    grad_two_low = (grad_out * scale_two).astype(jnp.bfloat16)
    fc2_grad = inner_rows(active, grad_two_low)
    fc2_bias_part = jnp.sum(grad_two_low.astype(jnp.float32), axis=0)
    grad_active = times_transpose(grad_two_low, down_full)
    _, gelu_pull = jax.vjp(exact_gelu, hidden)
    grad_hidden_low = gelu_pull(grad_active)[0].astype(jnp.bfloat16)
    fc1_grad = inner_rows(normed_two, grad_hidden_low)
    fc1_bias_part = jnp.sum(grad_hidden_low.astype(jnp.float32), axis=0)
    grad_normed_two = times_transpose(grad_hidden_low, up_full)
    grad_middle_norm, gain_two_part, shift_two_part = norm_back(
        middle, gain_two_f, shift_two_f, grad_normed_two
    )
    grad_middle = grad_out + grad_middle_norm
    qkv_full, proj_full = (
        lax.all_gather(qkv_weight, "fsdp", axis=0, tiled=True),
        lax.all_gather(proj_weight, "fsdp", axis=0, tiled=True),
    )
    gain_one_f = gain_one.astype(jnp.float32)
    shift_one_f = shift_one.astype(jnp.float32)
    queries, keys_all, values_all, weighting, weighting_low, attended = attention_forward(
        packed, segment, rowset, length, head_size
    )
    grad_one_low = (grad_middle * scale_one).astype(jnp.bfloat16)
    proj_grad = inner_rows(attended, grad_one_low)
    proj_bias_part = jnp.sum(grad_one_low.astype(jnp.float32), axis=0)
    grad_attended_low = times_transpose(grad_one_low, proj_full).astype(jnp.bfloat16)
    grad_attended_low = grad_attended_low.reshape(rowset, length, HEADS, head_size)
    grad_weighting = jnp.einsum(
        "rqhd,rkhd->rhqk", grad_attended_low, values_all, preferred_element_type=jnp.float32
    )
    value_grad = jnp.einsum(
        "rhqk,rqhd->rkhd", weighting_low, grad_attended_low, preferred_element_type=jnp.float32
    )
    row_inner = jnp.sum(grad_weighting * weighting, axis=-1, keepdims=True)
    grad_scores_low = (weighting * (grad_weighting - row_inner)).astype(jnp.bfloat16)
    key_scale = head_size ** (-0.5)
    query_grad = (
        jnp.einsum("rhqk,rkhd->rqhd", grad_scores_low, keys_all, preferred_element_type=jnp.float32)
        * key_scale
    )
    key_grad = (
        jnp.einsum("rhqk,rqhd->rkhd", grad_scores_low, queries, preferred_element_type=jnp.float32)
        * key_scale
    )
    grad_packed_low = (
        jnp.stack([query_grad, key_grad, value_grad], axis=2)
        .reshape(token_count, 3 * features)
        .astype(jnp.bfloat16)
    )
    qkv_grad = inner_rows(normed_one, grad_packed_low)
    column_sums = jnp.sum(grad_packed_low.astype(jnp.float32), axis=0)
    query_bias_part = column_sums[:features]
    value_bias_part = column_sums[2 * features :]
    grad_normed_one = times_transpose(grad_packed_low, qkv_full)
    grad_input_norm, gain_one_part, shift_one_part = norm_back(
        flattened, gain_one_f, shift_one_f, grad_normed_one
    )
    tokens_grad = (grad_middle + grad_input_norm).reshape(rowset, length, features)
    (
        gain_two_grad,
        shift_two_grad,
        fc1_weight_part,
        fc1_bias_shard,
        fc2_weight_part,
        fc2_bias_shard,
    ) = (
        lax.psum_scatter(gain_two_part, "fsdp", scatter_dimension=0, tiled=True),
        lax.psum_scatter(shift_two_part, "fsdp", scatter_dimension=0, tiled=True),
        lax.psum_scatter(fc1_grad, "fsdp", scatter_dimension=0, tiled=True),
        lax.psum_scatter(fc1_bias_part, "fsdp", scatter_dimension=0, tiled=True),
        lax.psum_scatter(fc2_grad, "fsdp", scatter_dimension=0, tiled=True),
        lax.psum_scatter(fc2_bias_part, "fsdp", scatter_dimension=0, tiled=True),
    )
    (
        gain_one_grad,
        shift_one_grad,
        qkv_weight_part,
        query_bias_shard,
        value_bias_shard,
        proj_weight_part,
        proj_bias_shard,
    ) = (
        lax.psum_scatter(gain_one_part, "fsdp", scatter_dimension=0, tiled=True),
        lax.psum_scatter(shift_one_part, "fsdp", scatter_dimension=0, tiled=True),
        lax.psum_scatter(qkv_grad, "fsdp", scatter_dimension=0, tiled=True),
        lax.psum_scatter(query_bias_part, "fsdp", scatter_dimension=0, tiled=True),
        lax.psum_scatter(value_bias_part, "fsdp", scatter_dimension=0, tiled=True),
        lax.psum_scatter(proj_grad, "fsdp", scatter_dimension=0, tiled=True),
        lax.psum_scatter(proj_bias_part, "fsdp", scatter_dimension=0, tiled=True),
    )
    summed = (
        lax.psum(gain_one_grad.astype(jnp.bfloat16), "dp").astype(jnp.float32),
        lax.psum(shift_one_grad.astype(jnp.bfloat16), "dp").astype(jnp.float32),
        lax.psum(qkv_weight_part.astype(jnp.bfloat16), "dp").astype(jnp.float32),
        lax.psum(query_bias_shard.astype(jnp.bfloat16), "dp").astype(jnp.float32),
        lax.psum(value_bias_shard.astype(jnp.bfloat16), "dp").astype(jnp.float32),
        lax.psum(proj_weight_part.astype(jnp.bfloat16), "dp").astype(jnp.float32),
        lax.psum(proj_bias_shard.astype(jnp.bfloat16), "dp").astype(jnp.float32),
        lax.psum(gain_two_grad.astype(jnp.bfloat16), "dp").astype(jnp.float32),
        lax.psum(shift_two_grad.astype(jnp.bfloat16), "dp").astype(jnp.float32),
        lax.psum(fc1_weight_part.astype(jnp.bfloat16), "dp").astype(jnp.float32),
        lax.psum(fc1_bias_shard.astype(jnp.bfloat16), "dp").astype(jnp.float32),
        lax.psum(fc2_weight_part.astype(jnp.bfloat16), "dp").astype(jnp.float32),
        lax.psum(fc2_bias_shard.astype(jnp.bfloat16), "dp").astype(jnp.float32),
    )
    return (
        output,
        tokens_grad,
        summed[0],
        summed[1],
        summed[2],
        summed[3],
        summed[4],
        summed[5],
        summed[6],
        summed[7],
        summed[8],
        summed[9],
        summed[10],
        summed[11],
        summed[12],
    )


BIT_Z1, BIT_Z0, BIT_Y, BIT_C = 8, 4, 2, 1
PIECE = 48
WIDE = 768
SCALE_ON = 1.0 / 0.9
MIB = 1024 * 1024
f32 = jnp.float32
bf16 = jnp.bfloat16


def hop(array, bit):
    return lax.ppermute(array, "fsdp", [(i, i ^ bit) for i in range(16)])


def swap(array):
    return lax.ppermute(array, "dp", [(0, 1), (1, 0)])


def cross(array):
    axes = ("dp", "fsdp")
    return lax.ppermute(array, axes, [(i, i ^ 16 ^ BIT_C) for i in range(32)])


def join(*arrays):
    return jnp.concatenate(arrays, axis=0)


def tie(array, *before):
    return lax.optimization_barrier((array,) + before)[0]


def to_other_core(own):
    return own + tuple(hop(part, BIT_C) for part in own)


def plus(left, right):
    return (left.astype(f32) + right.astype(f32)).astype(bf16)


def core_sums(own, came):
    return tuple(plus(own[a], came[a]) for a in range(4))


def first_hops(parts):
    return swap(parts[1]), hop(parts[3], BIT_Y)


def together(move, *arrays):
    flat = [array.reshape(-1, PIECE, 384) for array in arrays]
    came, at, out = move(join(*flat)), 0, []
    for array, part in zip(arrays, flat):
        out.append(came[at : at + part.shape[0]].reshape(array.shape))
        at += part.shape[0]
    return out


def hop_y(array):
    return hop(array, BIT_Y)


def first_sums(parts, got):
    return (
        plus(parts[0][:4], got[0][:4]),
        plus(parts[0][4:], got[0][4:]),
        plus(parts[2][:4], got[1][:4]),
        plus(parts[2][4:], got[1][4:]),
    )


def second_hops(parts):
    return hop(parts[1], BIT_Y), swap(parts[3])


def second_sums(parts, got):
    return tuple(
        jnp.stack([plus(parts[0][half], got[0][half]), plus(parts[2][half], got[1][half])])
        for half in (slice(0, 2), slice(2, 4))
    )


def third_hops(parts):
    return (hop(parts[1], BIT_Z0),)


def third_sums(parts, got):
    return plus(parts[0][:, 0], got[0][:, 0]), plus(parts[0][:, 1], got[0][:, 1])


def fourth_hops(parts):
    return (hop(parts[1], BIT_Z1),)


def fourth_sums(parts, got):
    return plus(parts[0], got[0])


def product(left, right, dims):
    return lax.dot_general(left, right, (dims, ((), ())), preferred_element_type=f32)


NN = ((1,), (0,))
NT = ((1,), (1,))
TN = ((0,), (0,))


def slot(line, xr, yr):
    return (xr, yr) if line == 0 else (2 + yr, xr)


def rel_places():
    return [(m, m & 1, (m >> 1) & 1, ((m >> 2) & 1) * 2 + (m >> 3)) for m in range(16)]


def rows_of(i, m):
    return pl.ds(pl.multiple_of((i ^ m) * PIECE, 16), PIECE)


def load_line(store, halves, i, columns=slice(None)):
    for m, c, yr, z in rel_places():
        ref, first = halves[c][yr]
        store[rows_of(i, m), columns] = ref[first + z, 0:PIECE, :]


def save_chunk(value, outs, i, line, xr):
    for m in range(16):
        c, yr, z0r, z1r = m & 1, (m >> 1) & 1, (m >> 2) & 1, (m >> 3) & 1
        array, part = slot(line, xr, yr) if isinstance(xr, int) else (2 + yr, xr)
        row = pl.multiple_of((i ^ m) * PIECE, 16)
        outs[c][array, part * 4 + z0r * 2 + z1r] = value[pl.ds(row, PIECE), :]


def row_facts(info, r):
    first = info[2 + 3 * r]
    second = first + info[3 + 3 * r]
    third = second + info[4 + 3 * r]

    def segment(shape, axis):
        t = lax.broadcasted_iota(jnp.int32, shape, axis)
        return (t >= first).astype(jnp.int32) + (t >= second).astype(jnp.int32) + (t >= third).astype(jnp.int32)

    column = segment((256, 1), 0)

    def scale(branch):
        keeps = [info[8 + 6 * r + 2 * j + branch].astype(f32) * SCALE_ON for j in range(3)]
        return jnp.where(
            column == 0, keeps[0], jnp.where(column == 1, keeps[1], jnp.where(column == 2, keeps[2], 0.0))
        )

    inside = jnp.where(column < 3, 1.0, 0.0).astype(f32)
    return column, segment((1, 256), 1), scale, inside


def unit_of(values):
    center = values - jnp.mean(values, axis=-1, keepdims=True)
    spread = jnp.mean(center * center, axis=-1, keepdims=True)
    root = lax.rsqrt(spread + EPSILON)
    return center * root, root


def unit_back(unit, root, gain, incoming):
    eg = incoming * gain
    return root * (
        eg - jnp.mean(eg, axis=-1, keepdims=True) - unit * jnp.mean(eg * unit, axis=-1, keepdims=True)
    )


def sums(values):
    return jnp.sum(values, axis=0, keepdims=True)


def load_direct(store, own, other, i, spots):
    for m in range(16):
        spot = spots[0] * (m >> 3) + spots[1] * (m >> 2 & 1) + spots[2] * (m >> 1 & 1)
        row = pl.multiple_of((i ^ m) * PIECE, 16)
        store[pl.ds(row, PIECE), :] = (other if m & 1 else own)[spot, 0:PIECE, :]


def prepare_kernel(info, qkv, fc1, fc2, *rest):
    vectors, (lead, *groups) = rest[:9], rest[9:]
    x = info[1]
    at = pl.multiple_of(WIDE + WIDE * x, 128)
    lead[0, 0:48, :] = qkv[:, pl.ds(at + 384, 384)]
    lead[0, 48:96, :] = qkv[:, pl.ds(pl.multiple_of(384 * x, 128), 384)]
    lead[0, 96:144, :] = qkv[:, pl.ds(at, 384)]
    rows = [v[...].astype(f32).reshape(1, -1) for v in vectors]
    rows = rows[:8] + [rows[8][:, 48 * k : 48 * k + 48] for k in range(4)]
    rows = [jnp.pad(row, ((0, 0), (0, 336))) for row in rows]
    lead[0, 144:160, :] = jnp.concatenate(rows + [jnp.zeros((4, 384), f32)]).astype(bf16)
    for half in range(2):

        @pl.when(x == half)
        def _():
            for s in range(2):
                first = 48 * (2 * half + s)
                cuts = [fc1[:, 192 * j + first : 192 * j + first + 48] for j in range(16)]
                groups[s][0] = jnp.concatenate(cuts, axis=1)
                groups[s][1] = fc2[first : first + 48, :]


def load_qkv(weight, refs, i, x):
    for xr in range(2):
        h = x ^ xr
        a = [[(refs[6 * c + xr], 4 * yr) for yr in range(2)] for c in range(2)]
        b = [[(refs[6 * c + 2 + yr], 4 * xr) for yr in range(2)] for c in range(2)]
        q = [[(refs[6 * c + 4 + xr], 4 * yr) for yr in range(2)] for c in range(2)]
        load_line(weight.at[1 + h], a, i, slice(0, 384))
        load_line(weight.at[1 + h], b, i, slice(384, 768))
        load_line(weight.at[0], q, i, pl.ds(pl.multiple_of(384 * h, 128), 384))


def qkv_kernel(info, tok, small, *rest):
    refs, (packed, normed, weight) = rest[:12], rest[12:]
    i, x = info[0], info[1]
    load_qkv(weight, refs, i, x)
    for r in range(2):
        rows = slice(256 * r, 256 * r + 256)
        unit, _ = unit_of(tok[rows, :].astype(f32))
        normed[rows, :] = (unit * small[0:1, :] + small[1:2, :]).astype(bf16)
    for r in range(2):
        rows = slice(256 * r, 256 * r + 256)
        low = normed[rows, :]
        packed[rows, 0:768] = (product(low, weight[0], NN) + small[2:3, :]).astype(bf16)
        packed[rows, 768:1536] = product(low, weight[1], NN).astype(bf16)
        packed[rows, 1536:2304] = (product(low, weight[2], NN) + small[3:4, :]).astype(bf16)


def attend_kernel(info, packed, cot, attended, grad_two, lse, scores, weighting):
    r = pl.program_id(0)
    column, across, scale, inside = row_facts(info, r)
    same = column == across
    lane = lax.broadcasted_iota(jnp.int32, (256, 128), 1)
    kept = jnp.zeros((256, 128), f32)
    for g in range(HEADS):
        query = packed[:, 64 * g : 64 * g + 64] * 0.125
        scores[g] = product(query, packed[:, 768 + 64 * g : 832 + 64 * g], NT)
    for g in range(HEADS):
        masked = jnp.where(same, scores[g], NEGATIVE)
        top = jnp.max(masked, axis=-1, keepdims=True)
        raised = jnp.exp(masked - top)
        total = jnp.sum(raised, axis=-1, keepdims=True)
        weighting[g] = (raised * (1.0 / total)).astype(bf16)
        kept = jnp.where(lane == g, top + jnp.log(total), kept)
    lse[...] = kept
    for h in range(0, HEADS, 2):
        pair = [
            product(weighting[g], packed[:, 1536 + 64 * g : 1600 + 64 * g], NN).astype(bf16)
            for g in (h, h + 1)
        ]
        attended[:, 64 * h : 64 * h + 128] = jnp.concatenate(pair, axis=1)
    grad_two[...] = (cot[...].astype(f32) * inside * scale(1)).astype(bf16)


def hidden_units(block, normed, turned, grad_two, small, branch, grad_normed, bias, weights, scratch):
    active, low = scratch[:2]
    for r in range(2):
        rows = slice(256 * r, 256 * r + 256)
        value = product(normed[rows, :], weights[0], NN) + small[pl.ds(8 + block, 1), :]
        share = 0.5 * (1.0 + lax.erf(value * (0.5**0.5)))
        active[rows, :] = (value * share).astype(bf16)
        slope = share + value * (jnp.exp(-0.5 * value * value) * 0.3989422804014327)
        low[rows, :] = (product(grad_two[rows, :], weights[1], NT) * slope).astype(bf16)
    bias[pl.ds(8 + block, 1), :] = sums(low[...].astype(f32))
    for r in range(2):
        rows = slice(256 * r, 256 * r + 256)
        branch[rows, :] += product(active[rows, :], weights[1], NN)
        grad_normed[rows, :] += product(low[rows, :], weights[0], NT)
    scratch[2][...] = product(turned[...], low[...], NN).astype(bf16)
    scratch[3][...] = product(active[...], grad_two[...], TN).astype(bf16)


def load_units(scratch, refs, i, t):
    for step in range(2):

        @pl.when(t == step)
        def _():
            up = [[(refs[4 * c + step], 4 * yr) for yr in range(2)] for c in range(2)]
            down = [[(refs[4 * c + 2 + yr], 4 * step) for yr in range(2)] for c in range(2)]
            load_line(scratch[4], up, i)
            load_line(scratch[5], down, i)

    return scratch[4][...], scratch[5][...]


def save_units(scratch, own, away, i, t):
    for m, c, yr, z in rel_places():
        for part in range(2):
            here = slice(384 * part, 384 * part + 384)
            (own, away)[c][t, 4 * yr + z, part] = scratch[2][rows_of(i, m), here]
            (own, away)[c][2 + yr, 4 * t + z, part] = scratch[3][rows_of(i, m), here]


def first_units_kernel(xr, info, left, grad_two, small, *rest):
    refs, rest = rest[:6], rest[6:]
    i, x = info[0], info[1]
    if xr == 0:
        tok, proj_own, proj_other, middle, normed, turned, branch, grad_normed, bias, own, away, proj = rest[:12]
        scratch = rest[12:]
        load_direct(proj, proj_own, proj_other, i, (2, 4, 1))
        for r in range(2):
            rows = slice(256 * r, 256 * r + 256)
            _, _, scale, _ = row_facts(info, r)
            after = tok[rows, :].astype(f32) + scale(0) * (
                product(left[rows, :], proj[...], NN) + small[4:5, :]
            )
            middle[rows, :] = after
            unit, _ = unit_of(after)
            normed[rows, :] = (unit * small[5:6, :] + small[6:7, :]).astype(bf16)
        turned[...] = normed[...].T
        branch[...] = jnp.zeros_like(branch)
        grad_normed[...] = jnp.zeros_like(grad_normed)
        bias[...] = jnp.zeros_like(bias)
        bias[7:8, :] = sums(grad_two[...].astype(f32))
    else:
        turned, branch_in, grad_normed_in, bias_in, branch, grad_normed, bias, own, away, *scratch = rest
        normed = left
        branch[...] = branch_in[...]
        grad_normed[...] = grad_normed_in[...]
        bias[...] = bias_in[...]
    load_line(scratch[4], [[(refs[c], 4 * yr) for yr in range(2)] for c in range(2)], i)
    load_line(scratch[5], [[(refs[2 + 2 * c + yr], 0) for yr in range(2)] for c in range(2)], i)
    weights = (scratch[4][...], scratch[5][...])
    hidden_units(2 * (x ^ xr), normed, turned, grad_two, small, branch, grad_normed, bias, weights, scratch)
    for m, c, yr, z in rel_places():
        for part in range(2):
            here = slice(384 * part, 384 * part + 384)
            for k in range(2):
                (own, away)[c][k, 4 * yr + z, part] = scratch[2 + k][rows_of(i, m), here]


def second_units_kernel(
    info, normed, turned, grad_two, small, branch_in, grad_normed_in, bias_in, middle, cot, *rest
):
    refs, (result, grad_middle, grad_one, bias, own, away, branch, grad_normed, *scratch) = rest[:8], rest[8:]
    i, x, t = info[0], info[1], pl.program_id(0)

    @pl.when(t == 0)
    def _():
        branch[...] = branch_in[...]
        grad_normed[...] = grad_normed_in[...]
        bias[...] = bias_in[...]

    weights = load_units(scratch, refs, i, t)
    hidden_units(2 * (t ^ x) + 1, normed, turned, grad_two, small, branch, grad_normed, bias, weights, scratch)
    save_units(scratch, own, away, i, t)

    @pl.when(t == 1)
    def _():
        for r in range(2):
            rows = slice(256 * r, 256 * r + 256)
            _, _, scale, inside = row_facts(info, r)
            after = middle[rows, :]
            result[rows, :] = (
                (after + scale(1) * (branch[rows, :] + small[7:8, :])) * inside
            ).astype(bf16)
            unit, root = unit_of(after)
            incoming = grad_normed[rows, :]
            bias[5:6, :] += sums(incoming * unit)
            bias[6:7, :] += sums(incoming)
            total = cot[rows, :].astype(f32) * inside + unit_back(unit, root, small[5:6, :], incoming)
            grad_middle[rows, :] = total
            low_one = (total * scale(0)).astype(bf16)
            grad_one[rows, :] = low_one
            bias[4:5, :] += sums(low_one.astype(f32))


def attend_back_kernel(group, info, queries, keys, values, lse, attended, grad_one, normed, *rest):
    if group == 0:
        proj_own, proj_other, grad_packed, own, away, weight, proj_rest, grad, *heads, total = rest
    else:
        weight, proj_rest, grad_packed, own, away, grad, *heads = rest
    i, x, r = info[0], info[1], pl.program_id(0)
    if group == 0:

        @pl.when(r == 0)
        def _():
            load_direct(weight, proj_own, proj_other, i, (2, 4, 1))
            total[...] = jnp.zeros_like(total)

        total[...] += product(attended[...], grad_one[...], TN)

    column, across, _, _ = row_facts(info, r)
    same = column == across
    grad_attended = product(grad_one[...], weight[384 * group : 384 * group + 384, :], NT).astype(bf16)
    rows = pl.ds(pl.multiple_of(r * 256, 256), 256)
    scores, backs, lows, highs = heads
    queried = [queries[:, 64 * g : 64 * g + 64] * 0.125 for g in range(6)]
    returned = [grad_attended[:, 64 * g : 64 * g + 64] for g in range(6)]
    for g in range(6):
        here = slice(64 * g, 64 * g + 64)
        scores[g] = product(queried[g], keys[:, here], NT)
        backs[g] = product(returned[g], values[:, here], NT)
    for g in range(6):
        head = 6 * group + g
        weighting = jnp.where(same, jnp.exp(scores[g] - lse[:, head : head + 1]), 0.0)
        highs[g] = weighting.astype(bf16)
        share = backs[g] * weighting
        inner = jnp.sum(share, axis=-1, keepdims=True)
        lows[g] = (share - weighting * inner).astype(bf16)
    for h in range(0, 6, 2):
        pairs = ([], [], [])
        for g in (h, h + 1):
            pairs[0].append(product(lows[g], keys[:, 64 * g : 64 * g + 64], NN) * 0.125)
            pairs[1].append(product(lows[g], queried[g], TN))
            pairs[2].append(product(highs[g], returned[g], TN))
        for k in range(3):
            grad_packed[rows, 384 * k + 64 * h : 384 * k + 64 * h + 128] = jnp.concatenate(
                pairs[k], axis=1
            ).astype(bf16)

    @pl.when(r == 1)
    def _():
        turned = normed[...].T
        grad[1, 0] = product(turned, grad_packed[:, 0:384], NN).astype(bf16)
        grad[0, 0] = product(turned, grad_packed[:, 384:768], NN).astype(bf16)
        grad[0, 1] = product(turned, grad_packed[:, 768:1152], NN).astype(bf16)
        if group == 0:
            grad[1, 1] = total[:, 0:384].astype(bf16)
            proj_rest[...] = total[:, 384:768].astype(bf16)
        else:
            grad[1, 1] = proj_rest[...]
        for line in range(2):
            for xr in range(2):
                save_chunk(grad.at[line, x ^ xr], (own, away), i, line, xr)


def tokens_back_kernel(r, info, tok, back0, back1, grad_middle, bias_in, small, *rest):
    refs, (tokens_grad, bias, weight) = rest[:12], rest[-3:]
    i, x = info[0], info[1]
    load_qkv(weight, refs, i, x)
    bias[...] = bias_in[...]
    for part, back in ((0, back0), (1, back1)):
        columns = slice(384 * part, 384 * part + 384)
        bias[2:3, columns] += sums(back[:, 0:384].astype(f32))
        bias[3:4, columns] += sums(back[:, 768:1152].astype(f32))
    incoming = jnp.zeros((256, WIDE), f32)
    for k in range(3):
        here = slice(384 * k, 384 * k + 384)
        joined = jnp.concatenate([back0[:, here], back1[:, here]], axis=1)
        incoming += product(joined, weight[k], NT)
    unit, root = unit_of(tok[...].astype(f32))
    bias[0:1, :] += sums(incoming * unit)
    bias[1:2, :] += sums(incoming)
    tokens_grad[...] = grad_middle[...] + unit_back(unit, root, small[0:1, :], incoming)


def results_kernel(info, mine0, other0, mine1, other1, bias, qkv, proj, *vectors):
    i, x = info[0], info[1]
    for group, mine, other in ((0, mine0, other0), (1, mine1, other1)):
        for line, half, column in ((1, 0, 0), (0, 0, 768), (0, 1, 1536), (1, 1, None)):
            a, b = mine[line].astype(f32), other[line].astype(f32)
            value = jnp.where(x == half, a, b)
            if column is None:
                proj[:, 384 * group : 384 * group + 384] = value
            else:
                qkv[:, column + 384 * group : column + 384 * group + 384] = value

    def cut(rows, start, width):
        feature = lax.broadcasted_iota(jnp.int32, (WIDE, width), 0)
        lane = lax.broadcasted_iota(jnp.int32, (WIDE, width), 1)
        chosen = (feature == lane + start).astype(f32)
        return lax.dot_general(
            rows, chosen, (NN, ((), ())), precision=lax.Precision.HIGHEST, preferred_element_type=f32
        )

    narrow = cut(bias[...], i * 48, 128)
    for k in range(8):
        vectors[k][...] = narrow[k, 0:48]
    broad = jnp.concatenate([narrow[8 + k : 9 + k, 0:48] for k in range(4)], axis=1)
    vectors[8][...] = broad[0]


def units_results_kernel(info, mine0, other0, mine1, other1, fc1, fc2):
    x = info[1]
    blocks = []
    for half in range(2):
        for mine, other in ((mine0, other0), (mine1, other1)):
            pieces = [
                jnp.concatenate(
                    [jnp.where(x == half, mine[k, p].astype(f32), other[k, p].astype(f32)) for p in range(2)],
                    axis=1,
                )
                for k in range(2)
            ]
            fc2[48 * len(blocks) : 48 * len(blocks) + 48, :] = pieces[1]
            blocks.append(pieces[0])
    for j in range(0, 16, 2):
        cuts = [b[:, 48 * k : 48 * k + 48] for k in (j, j + 1) for b in blocks]
        fc1[:, 192 * j : 192 * j + 384] = jnp.concatenate(cuts, axis=1)


def whole(shape):
    return pl.BlockSpec(shape, lambda *_: (0,) * len(shape))


def once(shape):
    return pl.BlockSpec(shape, lambda *_: (0,) * len(shape), pipeline_mode=pl.Buffered(1))


def rowwise(width):
    return pl.BlockSpec((256, width), lambda r, info: (r, 0))


def run_kernel(kernel, grid, info, operands, outs, scratch, microseconds, vmem, alias=None):
    return pl.pallas_call(
        kernel,
        grid_spec=pltpu.PrefetchScalarGridSpec(
            num_scalar_prefetch=1,
            grid=(grid,),
            in_specs=[spec or once(array.shape) for spec, array in operands],
            out_specs=[spec or whole(shape) for spec, shape, _ in outs],
            scratch_shapes=[pltpu.VMEM(shape, dtype) for shape, dtype in scratch],
        ),
        out_shape=[jax.ShapeDtypeStruct(shape, dtype) for _, shape, dtype in outs],
        input_output_aliases=alias or {},
        compiler_params=pltpu.CompilerParams(
            dimension_semantics=("arbitrary",), vmem_limit_bytes=vmem * MIB
        ),
        cost_estimate=pl.CostEstimate(
            flops=int(microseconds * 1.15e9), bytes_accessed=1 << 20, transcendentals=0
        ),
    )(info, *[array for _, array in operands])


def fast_device(
    tokens,
    lengths,
    keep_mask,
    cotangent,
    ln1_gain,
    ln1_bias,
    qkv_weight,
    q_bias,
    v_bias,
    proj_weight,
    proj_bias,
    ln2_gain,
    ln2_bias,
    fc1_weight,
    fc1_bias,
    fc2_weight,
    fc2_bias,
):
    count = tokens.shape[0] * tokens.shape[1]
    i = lax.axis_index("fsdp")
    x = lax.axis_index("dp")
    info = jnp.concatenate(
        [jnp.stack([i, x]).astype(jnp.int32), lengths.reshape(-1), keep_mask.reshape(-1)]
    )
    tok = tokens.reshape(count, WIDE)
    cot = cotangent.reshape(count, WIDE)

    def full(*arrays):
        return [(None, array) for array in arrays]

    vectors = (ln1_gain, ln1_bias, q_bias, v_bias, proj_bias, ln2_gain, ln2_bias, fc2_bias, fc1_bias)
    lead, units0, units1 = run_kernel(
        prepare_kernel,
        1,
        jnp.stack([i, x]),
        full(qkv_weight, fc1_weight, fc2_weight, *vectors),
        [(None, (1, 160, 384), bf16), (None, (2, PIECE, WIDE), bf16), (None, (2, PIECE, WIDE), bf16)],
        [],
        2,
        60,
    )

    proj = tie(proj_weight[None], lead)
    proj = join(proj, hop(proj, BIT_Y))

    pair = join(lead, hop(lead, BIT_Z1))
    far = hop(pair, BIT_Z0)
    line_b, line_q, line_a = (join(pair[:, k], far[:, k]) for k in (slice(0, 48), slice(48, 96), slice(96, 160)))
    line_a, line_b, line_q, units0 = lax.optimization_barrier((line_a, line_b, line_q, units0))
    got_a, got_b, got_q = hop(line_a, BIT_Y), swap(line_b), hop(line_q, BIT_Y)
    units_far = hop(units0, BIT_Z1)
    got_a, got_b = lax.optimization_barrier((got_a, got_b))
    wide_a, wide_b = join(line_a, got_a), join(line_b, got_b)
    got_a, got_b = swap(wide_a[:, :PIECE]), hop(wide_b, BIT_Y)
    wide_q = join(line_q, got_q)
    got_q = swap(wide_q)
    units_far = tie(units_far, wide_a, wide_b)
    units0 = jnp.stack([units0, units_far], axis=1)
    units_far = hop(units0, BIT_Z0)
    proj = tie(proj, wide_a, wide_b, units0)
    proj_far = hop(proj, BIT_Z1)
    got_a, got_b, got_q, units_far, units1, proj_far = lax.optimization_barrier(
        (got_a, got_b, got_q, units_far, units1, proj_far)
    )
    first = to_other_core((wide_a, got_a, wide_b, got_b, wide_q, got_q))

    units_line = join(units0[0], units_far[0]), join(units0[1], units_far[1])
    units_got = hop(units_line[0], BIT_Y), swap(units_line[1])
    next_far = hop(units1, BIT_Z1)
    proj = join(proj, proj_far)
    proj_far = hop(proj, BIT_Z0)

    vectors = jnp.concatenate([first[k][:, PIECE : PIECE + 12, :PIECE] for k in (0, 6)])
    origin = jnp.array([(p & 1) * 8 + (p >> 1 & 1) * 4 + (p >> 2 & 1) * 2 + (p >> 3) for p in range(16)])
    turned = jnp.arange(16)[:, None] == (origin ^ i)[None, :]
    vectors = jnp.einsum("mp,pkl->kml", turned.astype(bf16), vectors, preferred_element_type=f32)
    small = jnp.concatenate([vectors.reshape(12, WIDE), jnp.zeros((4, WIDE), f32)])

    packed, normed_one = run_kernel(
        qkv_kernel,
        1,
        info,
        full(tok, small, *first),
        [(None, (count, 3 * WIDE), bf16), (None, (count, WIDE), bf16)],
        [((3, WIDE, WIDE), bf16)],
        5,
        40,
    )

    units_got, next_far, proj_far, _ = lax.optimization_barrier((units_got, next_far, proj_far, packed))
    units_wide = tuple(join(line, got) for line, got in zip(units_line, units_got))
    units_got = swap(units_wide[0]), hop(units_wide[1], BIT_Y)
    units1 = jnp.stack([units1, next_far], axis=1)
    next_far = hop(units1, BIT_Z0)
    proj = join(proj, proj_far)
    proj_other = hop(proj, BIT_C)

    attended, grad_two, lse = run_kernel(
        attend_kernel,
        2,
        tie(info, *units_wide, units1, proj),
        [(rowwise(3 * WIDE), packed), (rowwise(WIDE), cot)],
        [
            (rowwise(WIDE), (count, WIDE), bf16),
            (rowwise(WIDE), (count, WIDE), bf16),
            (rowwise(128), (count, 128), f32),
        ],
        [((HEADS, 256, 256), f32), ((HEADS, 256, 256), bf16)],
        6,
        40,
    )

    units_got, next_far, proj_other, _ = lax.optimization_barrier((units_got, next_far, proj_other, lse))
    units = to_other_core((units_wide[0], units_got[0], units_wide[1], units_got[1]))
    next_line = tuple(join(units1[k], next_far[k]) for k in range(2))
    next_got = hop(next_line[0], BIT_Y), swap(next_line[1])

    wide_f32 = (None, (count, WIDE), f32)
    wide_bf16 = (None, (count, WIDE), bf16)
    vectors_f32 = (None, (16, WIDE), f32)
    parts = (None, (4, 8, 2, PIECE, 384), bf16)
    half = (None, (2, 8, 2, PIECE, 384), bf16)
    unit_scratch = [((count, WIDE), bf16)] * 2 + [((WIDE, WIDE), bf16)] * 4

    def first_units(xr, info, left, more, outs, scratch):
        part = pl.BlockSpec((4, PIECE, WIDE), lambda _, __: (xr, 0, 0))
        return run_kernel(
            functools.partial(first_units_kernel, xr),
            1,
            info,
            full(left, grad_two, small, units[xr], units[4 + xr])
            + [(part, units[k]) for k in (2, 3, 6, 7)]
            + full(*more),
            outs + [wide_f32, wide_f32, vectors_f32, half, half],
            scratch + unit_scratch,
            7,
            28,
        )

    middle, normed_two, turned_two, branch, grad_normed, bias, own0, away0 = first_units(
        0,
        tie(info, *next_line),
        attended,
        (tok, proj, proj_other),
        [wide_f32, wide_bf16, (None, (WIDE, count), bf16)],
        [((WIDE, WIDE), bf16)],
    )
    next_got, bias, away0 = lax.optimization_barrier((next_got, bias, away0))
    next_wide = tuple(join(line, got) for line, got in zip(next_line, next_got))
    next_got = swap(next_wide[0]), hop(next_wide[1], BIT_Y)
    came0 = hop(away0, BIT_C)
    branch, grad_normed, bias, own1, away1 = first_units(
        1, tie(info, *next_wide), normed_two, (turned_two, branch, grad_normed, bias), [], []
    )
    next_got, came0, bias, away1 = lax.optimization_barrier((next_got, came0, bias, away1))
    units = to_other_core((next_wide[0], next_got[0], next_wide[1], next_got[1]))
    came1 = hop(away1, BIT_C)
    two = (
        plus(own0[0], came0[0]),
        plus(own1[0], came1[0]),
        join(plus(own0[1, :4], came0[1, :4]), plus(own1[1, :4], came1[1, :4])),
        join(plus(own0[1, 4:], came0[1, 4:]), plus(own1[1, 4:], came1[1, 4:])),
    )
    two_got = first_hops(two)
    output, grad_middle, grad_one, bias, units_own, units_away = run_kernel(
        second_units_kernel,
        2,
        tie(info, *two),
        full(normed_two, turned_two, grad_two, small, branch, grad_normed, bias, middle, cot, *units),
        [wide_bf16, wide_f32, wide_bf16, vectors_f32, parts, parts],
        [((count, WIDE), f32)] * 2 + unit_scratch,
        15,
        40,
    )

    def attend_back(group, info, more, outs, scratch):
        def columns(k):
            return pl.BlockSpec((256, 384), lambda r, _, at=2 * k + group: (r, at))

        narrow = (4, 8, PIECE, 384)
        return run_kernel(
            functools.partial(attend_back_kernel, group),
            2,
            info,
            [(columns(k), packed) for k in range(3)]
            + [(rowwise(128), lse), (rowwise(WIDE), attended), (rowwise(WIDE), grad_one)]
            + full(normed_one, *more),
            [(None, (count, 1152), bf16), (None, narrow, bf16), (None, narrow, bf16)] + outs,
            [((2, 2, WIDE, 384), bf16)]
            + [((6, 256, 256), f32)] * 2
            + [((6, 256, 256), bf16)] * 2
            + scratch,
            8,
            30,
        )

    two_got, bias, units_away = lax.optimization_barrier((two_got, bias, units_away))
    two = first_sums(two, two_got)
    two_got, one_came = second_hops(two), hop(units_away, BIT_C)
    back0, head_own0, head_away0, proj_full, proj_rest = attend_back(
        0,
        tie(info, *two),
        (proj, proj_other),
        [(None, (WIDE, WIDE), bf16), (None, (WIDE, 384), bf16)],
        [((WIDE, WIDE), f32)],
    )

    two_got, one_came, proj_rest, head_away0 = lax.optimization_barrier(
        (two_got, one_came, proj_rest, head_away0)
    )
    two = second_sums(two, two_got)
    one = core_sums(units_own, one_came)
    one_got, two_got, zero_came = first_hops(one), third_hops(two), hop(head_away0, BIT_C)
    back1, head_own1, head_away1 = attend_back(1, tie(info, *two, *one), (proj_full, proj_rest), [], [])

    two_got, one_got, zero_came, head_away1 = lax.optimization_barrier(
        (two_got, one_got, zero_came, head_away1)
    )
    two, one, zero = third_sums(two, two_got), first_sums(one, one_got), core_sums(head_own0, zero_came)
    last_came = hop(head_away1, BIT_C)
    zero_got, one_got = first_hops(zero), second_hops(one)

    def tokens_back(r, info, more, alias):
        def row(width):
            return pl.BlockSpec((256, width), lambda _, __: (r, 0))

        return run_kernel(
            functools.partial(tokens_back_kernel, r),
            1,
            info,
            [(row(WIDE), tok), (row(1152), back0), (row(1152), back1), (row(WIDE), grad_middle)]
            + full(bias, small, *first)
            + more,
            [(row(WIDE), (count, WIDE), f32), (None, (16, WIDE), f32)],
            [((3, WIDE, WIDE), bf16)],
            5,
            40,
            alias,
        )

    tokens_grad, bias = tokens_back(0, tie(info, *two, *one, *zero), [], {})

    zero_got, one_got, last_came, bias = lax.optimization_barrier((zero_got, one_got, last_came, bias))
    last, zero, one = core_sums(head_own1, last_came), first_sums(zero, zero_got), second_sums(one, one_got)
    two_got, one_got = fourth_hops(two), third_hops(one)
    got_x, got_y = together(swap, last[1], zero[3]), together(hop_y, last[3], zero[1])
    last_got, zero_got = (got_x[0], got_y[0]), (got_y[1], got_x[1])
    tokens_grad, bias = tokens_back(
        1, tie(info, *last, *zero, *one), [(pl.BlockSpec(memory_space=pl.ANY), tokens_grad)], {19: 0}
    )

    last_got, zero_got, two_got, one_got, bias = lax.optimization_barrier(
        (last_got, zero_got, two_got, one_got, bias)
    )
    last, zero, two, one = (
        first_sums(last, last_got),
        second_sums(zero, zero_got),
        fourth_sums(two, two_got),
        third_sums(one, one_got),
    )
    last_got, zero_got, one_got, bias_got = lax.optimization_barrier(
        (second_hops(last), third_hops(zero), fourth_hops(one), hop(bias, BIT_Y))
    )
    last, one, zero = second_sums(last, last_got), fourth_sums(one, one_got), third_sums(zero, zero_got)
    bias = bias + bias_got
    last_got, zero_got, got, bias_got = lax.optimization_barrier(
        (third_hops(last), fourth_hops(zero), together(swap, one, two), hop(bias, BIT_Z0))
    )
    one_other, two_other = got
    last, zero, bias = third_sums(last, last_got), fourth_sums(zero, zero_got), bias + bias_got
    last_got, zero_other, bias_got = lax.optimization_barrier(
        (fourth_hops(last), swap(zero), hop(bias, BIT_Z1))
    )
    last, bias = fourth_sums(last, last_got), bias + bias_got
    last_other, bias_got = swap(last), (swap(bias), hop(bias, BIT_C), cross(bias))
    fc1_grad, fc2_grad = run_kernel(
        units_results_kernel,
        1,
        info,
        full(two, two_other, one, one_other),
        [(None, (PIECE, 4 * WIDE), f32), (None, (4 * PIECE, WIDE), f32)],
        [],
        3,
        40,
    )
    bias = (bias + bias_got[0]) + (bias_got[1] + bias_got[2])
    qkv_grad, proj_grad, *narrow = run_kernel(
        results_kernel,
        1,
        info,
        full(zero, zero_other, last, last_other, bias),
        [(None, (PIECE, 3 * WIDE), f32), (None, (PIECE, WIDE), f32)]
        + [(None, (48,), f32)] * 8
        + [(None, (192,), f32)],
        [],
        3,
        40,
    )
    return (
        output.reshape(tokens.shape),
        tokens_grad.reshape(tokens.shape),
        narrow[0],
        narrow[1],
        qkv_grad,
        narrow[2],
        narrow[3],
        proj_grad,
        narrow[4],
        narrow[5],
        narrow[6],
        fc1_grad,
        narrow[8],
        fc2_grad,
        narrow[7],
    )


def solution(mesh):
    in_specs = (
        P(("dp", "fsdp"), None, None),
        P(("dp", "fsdp"), None),
        P(("dp", "fsdp"), None, None),
        P(("dp", "fsdp"), None, None),
        P("fsdp"),
        P("fsdp"),
        P("fsdp", None),
        P("fsdp"),
        P("fsdp"),
        P("fsdp", None),
        P("fsdp"),
        P("fsdp"),
        P("fsdp"),
        P("fsdp", None),
        P("fsdp"),
        P("fsdp", None),
        P("fsdp"),
    )
    out_specs = (
        P(("dp", "fsdp"), None, None),
        P(("dp", "fsdp"), None, None),
        P("fsdp"),
        P("fsdp"),
        P("fsdp", None),
        P("fsdp"),
        P("fsdp"),
        P("fsdp", None),
        P("fsdp"),
        P("fsdp"),
        P("fsdp"),
        P("fsdp", None),
        P("fsdp"),
        P("fsdp", None),
        P("fsdp"),
    )
    fits = mesh.shape["dp"] == 2 and mesh.shape["fsdp"] == 16
    return jax.shard_map(
        fast_device if fits else per_device, mesh=mesh, in_specs=in_specs, out_specs=out_specs, check_vma=False
    )
```
